256 devices in a mesh: blk: 64 (over z, y, core), vec: 4 (over x).
Axes of the slice: x: 4, y: 4, z: 8, core: 2. Of those that a mesh axis runs over, the one named last changes fastest.
Arguments:
- vectors: float32 [8, 128, 5, 2, 64, 128], P('vec', 'blk'), may hold values from -15 to 15
- metric: float32 [128, 2, 64, 128], P('blk'), may hold values from 0.5 to 2
- jacobians: float32 [3, 5, 5], replicated, may hold values from -2 to 2
- block_rows: int32 [128], P('blk'), may hold values from 32 to 64, as said below
- neighbours: int32 [128, 2], P('blk'), may hold values from 0 to 127, as said below
- flipped: int32 [128, 2], P('blk'), may hold values from 0 to 1, as said below
Outputs:
- basis: float32 [8, 128, 5, 2, 64, 128], P('vec', 'blk')
- factor: float32 [8, 8], replicated
The draws below stay inside these ranges and needn't reach their ends.
Inputs may be any that keep to these rules, and one draw needn't show every extreme that they name: Rows from block_rows[b] on are padding; some block has 64 live rows and some 64 // 2. neighbours[b, 1] is the block whose first row faces the last live row of b, and neighbours[neighbours[b, 1], 0] = b; following neighbours[., 1] from any block visits all 128 blocks in one cycle. flipped[b, 1] = flipped[neighbours[b, 1], 0].
All inputs are finite; a program needn't handle non-finite values.
Results may differ from the reference program's by a relative error of at most 0.0003.
Values sent between devices are 32-bit elements; how exact they have to be, the bound alone decides.
A program may use at most 192 MiB of HBM per device.

```python
import math
import jax
import jax.numpy as jnp
from jax import lax

FIELDS = 5
BI = 128
BJ = 64
BK = 2
NB = 128
NV = 8


def cycle_tables(key):
    cycle_order = jax.random.permutation(jax.random.fold_in(key, 101), NB).astype(jnp.int32)
    successor_ids = jnp.roll(cycle_order, -1)
    after_ids = jnp.zeros((NB,), jnp.int32).at[cycle_order].set(successor_ids)
    before_ids = jnp.zeros((NB,), jnp.int32).at[successor_ids].set(cycle_order)
    turn_bits = jax.random.randint(jax.random.fold_in(key, 102), (NB,), 0, 2, dtype=jnp.int32)
    flip_high = jnp.zeros((NB,), jnp.int32).at[cycle_order].set(turn_bits)
    flip_low = jnp.zeros((NB,), jnp.int32).at[successor_ids].set(turn_bits)
    return (jnp.stack([before_ids, after_ids], axis=1), jnp.stack([flip_low, flip_high], axis=1))


def draw_neighbours(key, part):
    tables = cycle_tables(key)
    return tables[0]


def draw_flipped(key, part):
    tables = cycle_tables(key)
    return tables[1]


def draw_block_rows(key, part):
    key = jax.random.fold_in(key, 7)
    counts = jax.random.randint(jax.random.fold_in(key, 1), (NB,), BJ // 2, BJ + 1, dtype=jnp.int32)
    chosen = jax.random.randint(jax.random.fold_in(key, 2), (), 0, NB, dtype=jnp.int32)
    other = (chosen + 1 + jax.random.randint(jax.random.fold_in(key, 3), (), 0, NB - 1, dtype=jnp.int32)) % NB
    block_index = jnp.arange(NB, dtype=jnp.int32)
    counts = jnp.where(block_index == chosen, BJ, counts)
    counts = jnp.where(block_index == other, BJ // 2, counts)
    return counts


def draw_vectors(key, part):
    key = jax.random.fold_in(key, 11)
    full_shape = (NV, NB, FIELDS, BK, BJ, BI)
    block_ramp = 1.0 + 2.0 * jnp.arange(NB, dtype=jnp.float32) / max(NB - 1, 1)
    block_ramp = block_ramp[None, :, None, None, None, None]
    drawn = jax.random.normal(jax.random.fold_in(key, 1), full_shape, jnp.float32)
    drawn = jnp.clip(drawn, -5.0, 5.0) * block_ramp
    return drawn.astype(jnp.float32)


def block_levels(rng, dims, shards, smallest, high):
    gain = 1.0
    for position, parts in shards:
        steps = jax.random.uniform(jax.random.fold_in(jax.random.fold_in(rng, 6), position), (parts,), jnp.float32, smallest / len(shards), high / len(shards))
        gain = gain * jnp.repeat(jnp.exp(steps), dims[position] // parts).reshape((-1,) + (1,) * (len(dims) - 1 - position))
    return gain


def bell_draw(rng, dims, scale, limit, kind=jnp.bfloat16):
    values = scale * jax.random.normal(rng, dims, jnp.float32)
    return jnp.clip(values, min=-limit, max=limit).astype(kind)


def setup_inputs(seed: int = 0) -> dict:
    splits = jax.random.split(jax.random.key(seed), 7)
    return {
        "vectors": draw_vectors(jax.random.fold_in(splits[6], 71), 0),
        "metric": jnp.clip(jnp.exp(math.log(2.0) - 1.3862944 * jax.random.uniform(splits[1], (NB, BK, BJ, BI), jnp.float32) ** block_levels(splits[1], (NB, BK, BJ, BI), ((0, 64),), -0.2, 0.2)), 0.5, 2.0),
        "jacobians": bell_draw(splits[2], (3, FIELDS, FIELDS), 10 ** -0.5, 2.0, jnp.float32),
        "block_rows": draw_block_rows(jax.random.fold_in(splits[6], 71), 0),
        "neighbours": draw_neighbours(jax.random.fold_in(splits[6], 71), 0),
        "flipped": draw_flipped(jax.random.fold_in(splits[6], 71), 0),
    }


viscous = 0.1
epsilon = 1e-06
hardest = lax.Precision.HIGHEST

def turn_sign():
    return jnp.array([1.0, -1.0, 1.0, 1.0, 1.0], jnp.float32)

def block_faces(field_state, row_counts):
    low_face = field_state[:, :, :, :, 0, :]
    last_index = (row_counts - 1).astype(jnp.int32)[None, :, None, None, None, None]
    full_shape = field_state.shape[:4] + (1,) + field_state.shape[5:]
    high_face = jnp.take_along_axis(field_state, jnp.broadcast_to(last_index, full_shape), axis=4)[:, :, :, :, 0, :]
    return jnp.stack([low_face, high_face], axis=2)

def orient(face_cells, face_flags):
    turned = jnp.flip(face_cells, -1) * turn_sign().astype(face_cells.dtype)[None, None, :, None, None]
    return jnp.where(face_flags[None, :, None, None, None] > 0, turned, face_cells)

def local_update(field_state, ghost_low, ghost_high, row_counts, jacobians, metric):
    height = field_state.shape[4]
    row_index = jnp.arange(height, dtype=jnp.int32)
    alive_mask = (row_index[None, :] < row_counts[:, None]).astype(field_state.dtype)[None, :, None, None, :, None]
    top_row = (row_index[None, :] == row_counts[:, None] - 1).astype(field_state.dtype)[None, :, None, None, :, None]
    first_row = (row_index == 0).astype(field_state.dtype)[None, None, None, None, :, None]
    zero_row = jnp.zeros_like(field_state[:, :, :, :, :1, :])
    above_cells = jnp.concatenate([field_state[:, :, :, :, 1:, :], zero_row], axis=4) + top_row * ghost_high[:, :, :, :, None, :]
    below_cells = jnp.concatenate([zero_row, field_state[:, :, :, :, :-1, :]], axis=4) + first_row * ghost_low[:, :, :, :, None, :]
    zero_layer = jnp.zeros_like(field_state[:, :, :, :1])
    deeper = jnp.concatenate([field_state[:, :, :, 1:], zero_layer], axis=3)
    shallower = jnp.concatenate([zero_layer, field_state[:, :, :, :-1]], axis=3)
    right_cells = jnp.roll(field_state, -1, axis=5)
    left_cells = jnp.roll(field_state, 1, axis=5)
    flux_sum = jnp.einsum('fg,vbgkji->vbfkji', jacobians[0], right_cells - left_cells, precision=hardest)
    flux_sum = flux_sum + jnp.einsum('fg,vbgkji->vbfkji', jacobians[1], above_cells - below_cells, precision=hardest)
    flux_sum = flux_sum + jnp.einsum('fg,vbgkji->vbfkji', jacobians[2], deeper - shallower, precision=hardest)
    spread = right_cells + left_cells + above_cells + below_cells + deeper + shallower - 6.0 * field_state
    return alive_mask * (field_state - metric[None, :, None] * flux_sum + viscous * spread)

def advance(field_state, row_counts, neighbours, flipped, jacobians, metric):
    faces = block_faces(field_state, row_counts)
    ghost_low = orient(jnp.take(faces, neighbours[:, 0], axis=1)[:, :, 1], flipped[:, 0])
    ghost_high = orient(jnp.take(faces, neighbours[:, 1], axis=1)[:, :, 0], flipped[:, 1])
    return local_update(field_state, ghost_low, ghost_high, row_counts, jacobians, metric)

def reference(vectors, metric, jacobians, block_rows, neighbours, flipped):
    vector_count = vectors.shape[0]
    row_index = jnp.arange(vectors.shape[4], dtype=jnp.int32)
    alive_mask = (row_index[None, :] < block_rows[:, None]).astype(vectors.dtype)[None, :, None, None, :, None]
    stepped = []
    for member in range(vector_count):
        field_state = vectors[member:member + 1] * alive_mask
        field_state = advance(field_state, block_rows, neighbours, flipped, jacobians, metric)
        field_state = field_state / jnp.sqrt(jnp.sum(field_state * field_state) + epsilon)
        field_state = advance(field_state, block_rows, neighbours, flipped, jacobians, metric)
        stepped.append(field_state)
    second = jnp.concatenate(stepped, axis=0)
    flat_field = second.reshape(vector_count, -1)
    gram_matrix = jnp.dot(flat_field, flat_field.T, precision=hardest)
    lower_factor = jnp.linalg.cholesky(gram_matrix)
    inverse = jax.scipy.linalg.solve_triangular(lower_factor, jnp.eye(vector_count, dtype=gram_matrix.dtype), lower=True)
    basis = jnp.dot(inverse, flat_field, precision=hardest).reshape(second.shape)
    return (basis, lower_factor.T)
```

```python
import jax
import jax.numpy as jnp
from jax import lax
from jax.experimental import pallas as pl
from jax.experimental.pallas import tpu as pltpu
from jax.sharding import PartitionSpec as P

MESH = pl.DeviceIdType.MESH
F32 = jnp.float32
HI = lax.Precision.HIGHEST
NF = 5
NZ, NY, NC, NX = 8, 4, 2, 4
NR = NY * NC
VISC = 0.1
EPS = 1e-06
SCALE = 1024.0


def pair(v, w):
    return v * (v + 1) // 2 + w


def kernel(vec, met, jac, rows, nbr, flip, out, fac,
           st, fi, se, gath, bas, rel1, rel2, pay, zb, rq, rqs, o2, rb, own, gst, cs, cb, gacc, ar, arx, ary, arz, spl, mix,
           loc_sem, xs, xr, fs, fr, zs, zr, qs, qr, ys, yr, cs_s, cs_r, as_s, as_r, os, orr):
    blk = lax.axis_index("blk")
    x = lax.axis_index("vec")
    z = blk // NR
    rho = lax.rem(blk, NR)
    c = lax.rem(blk, NC)
    col = lax.rem(blk, NR)

    def zdev(dz, core):
        zz = lax.rem(z + dz + NZ, NZ)
        return zz * NR + (rho - c) + core

    bar = pltpu.get_barrier_semaphore()
    n_part = 0
    for d in range(1, NX):
        pl.semaphore_signal(bar, inc=1, device_id={"blk": blk, "vec": lax.rem(x + d, NX)}, device_id_type=MESH)
        n_part += 1
    for d in range(1, NR):
        pl.semaphore_signal(bar, inc=1, device_id={"blk": z * NR + lax.rem(rho + d, NR), "vec": x}, device_id_type=MESH)
        n_part += 1
    for d in range(1, NZ):
        pl.semaphore_signal(bar, inc=1, device_id={"blk": zdev(d, c), "vec": x}, device_id_type=MESH)
        n_part += 1
    for d in (1, NZ - 1):
        pl.semaphore_signal(bar, inc=1, device_id={"blk": zdev(d, 1 - c), "vec": x}, device_id_type=MESH)
        n_part += 1

    def rcopy(src, dst, ssem, rsem, b_, x_):
        return pltpu.make_async_remote_copy(src_ref=src, dst_ref=dst, send_sem=ssem, recv_sem=rsem,
                                            device_id={"blk": b_, "vec": x_}, device_id_type=MESH)

    iota64 = lax.broadcasted_iota(jnp.int32, (64, 128), 0)
    iota8 = lax.broadcasted_iota(jnp.int32, (8, 128), 0)
    lane8 = lax.broadcasted_iota(jnp.int32, (8, 128), 1)
    zero8 = jnp.zeros((8, 128), F32)

    def fill(i, _):
        vb = i // 10
        v, b = vb // 2, lax.rem(vb, 2)
        fk = lax.rem(i, 10)
        f, k = fk // 2, lax.rem(fk, 2)
        q = vec[v, b, f, k]
        st[v, b, f, k, 8:72, :] = jnp.where(iota64 < rows[b], q, 0.0)
        st[v, b, f, k, 0:8, :] = zero8
        st[v, b, f, k, 72:80, :] = zero8
        fi[v, b, f, k, 0:8, :] = zero8
        fi[v, b, f, k, 72:80, :] = zero8
        return 0

    lax.fori_loop(0, 40, fill, 0)

    def advance_tile(src, v, b, t, scale, store):
        r0 = pl.multiple_of(t * 8, 8)
        alive = (iota8 + r0) < rows[b]
        qs_, d0, d1, base = [], [], [], []
        for k in range(2):
            qk = [src[v, b, f, k, pl.ds(r0 + 8, 8), :] for f in range(NF)]
            qs_.append(qk)
        for k in range(2):
            a0, a1, ab = [], [], []
            for f in range(NF):
                q = qs_[k][f]
                e = pltpu.roll(q, 127, 1)
                w = pltpu.roll(q, 1, 1)
                n = src[v, b, f, k, pl.ds(r0 + 9, 8), :]
                s = src[v, b, f, k, pl.ds(r0 + 7, 8), :]
                a0.append(e - w)
                a1.append(n - s)
                ab.append((scale * (1.0 - 6.0 * VISC)) * q + (scale * VISC) * ((e + w) + (n + s) + qs_[1 - k][f]))
            d0.append(a0)
            d1.append(a1)
            base.append(ab)
        mk = [met[b, k, pl.ds(r0, 8), :] * scale for k in range(2)]
        for f in range(NF):
            c0 = [jac[0, f, g] for g in range(NF)]
            c1 = [jac[1, f, g] for g in range(NF)]
            c2 = [jac[2, f, g] for g in range(NF)]
            for k in range(2):
                acc = c0[0] * d0[k][0] + c1[0] * d1[k][0]
                oth = c2[0] * qs_[1 - k][0]
                for g in range(1, NF):
                    acc = acc + c0[g] * d0[k][g] + c1[g] * d1[k][g]
                    oth = oth + c2[g] * qs_[1 - k][g]
                flux = acc + oth if k == 0 else acc - oth
                store(f, k, jnp.where(alive, base[k][f] - mk[k] * flux, 0.0))

    def first_pass(i, sums):
        vb, t = i // 8, lax.rem(i, 8)
        v, b = vb // 2, lax.rem(vb, 2)
        r0 = t * 8
        row = iota8 + r0
        inner = jnp.logical_and(row > 0, row != rows[b] - 1)
        box = [jnp.zeros((8, 128), F32)]

        def store(f, k, val):
            fi[v, b, f, k, pl.ds(pl.multiple_of(r0 + 8, 8), 8), :] = val
            box[0] = box[0] + val * val

        advance_tile(st, v, b, t, 1.0, store)
        sq = jnp.where(inner, box[0], 0.0)
        s0, s1 = sums
        return s0 + jnp.where(v == 0, sq, 0.0), s1 + jnp.where(v == 1, sq, 0.0)

    ssq = lax.fori_loop(0, 32, first_pass, (zero8, zero8))

    def faces(i, _):
        b, side, v = i // 4, lax.rem(i // 2, 2), lax.rem(i, 2)
        last = jnp.maximum(rows[b] - 1, 1)
        r = jnp.where(side == 0, 0, last)
        adj = jnp.where(side == 0, 1, last - 1)
        slot = b * 2 + side
        lane_row = b * 8 + side * 2 + v
        for f in range(NF):
            for k in range(2):
                a = st[v, b, f, k, pl.ds(r + 8, 1), :]
                p = fi[v, b, f, k, pl.ds(r + 8, 1), :]
                pay[v, slot, f * 2 + k:f * 2 + k + 1, :] = a
                pay[v, slot, 10 + f * 2 + k:11 + f * 2 + k, :] = p
                own[f, pl.ds(lane_row + 4 * k, 1), :] = a
                own[NF + f, pl.ds(lane_row + 4 * k, 1), :] = p
        for k in range(2):
            m = met[b, k, pl.ds(r, 1), :]
            pay[v, slot, 20 + k:21 + k, :] = m
            pay[v, slot, 22 + k:23 + k, :] = m
            own[10, pl.ds(lane_row + 4 * k, 1), :] = m
            own[11, pl.ds(lane_row + 4 * k, 1), :] = met[b, k, pl.ds(adj, 1), :]
        return 0

    lax.fori_loop(0, 8, faces, 0)
    req = jnp.where(lane8 == 0, nbr[0, 0], jnp.where(lane8 == 1, nbr[0, 1], jnp.where(lane8 == 2, nbr[1, 0], nbr[1, 1])))
    rq[rho] = req

    pl.semaphore_wait(bar, n_part)

    mine = pltpu.make_async_copy(pay.at[c], zb.at[z, c], loc_sem.at[0])
    mine.start()
    z_copies = []
    for j in range(2):
        core = lax.rem(c + j, NC)
        for side, dz in ((0, 1), (1, -1)):
            n = side * 2 + j
            cp = rcopy(pay.at[core], zb.at[z, c], zs.at[n], zr.at[n], zdev(dz, core), x)
            cp.start()
            z_copies.append(cp)
    other = rcopy(pay.at[1 - c], zb.at[z, c], zs.at[4], zr.at[4], zdev(0, 1 - c), x)
    other.start()
    q_copies = []
    for d in range(1, NR):
        cp = rcopy(rq.at[rho], rq.at[rho], qs.at[d - 1], qr.at[d - 1], z * NR + lax.rem(rho + d, NR), x)
        cp.start()
        q_copies.append(cp)

    def second_pass(v):
        def body(i, _):
            b, t = i // 8, lax.rem(i, 8)

            def store(f, k, val):
                se[b * 2 + k, v, f, pl.ds(pl.multiple_of(t * 8, 8), 8), :] = val

            advance_tile(fi, v, b, t, SCALE, store)
            return 0

        lax.fori_loop(0, 16, body, 0)

    def xdev(d):
        return lax.rem(x + d + NX, NX)

    sends = []

    def send_second(v):
        far = xdev(2)
        for s, d in ((0, 1), (1, -1)):
            half = pl.ds(32 * s, 32)
            cp = rcopy(se.at[far, v, :, half, :], rel1.at[v, s], xs.at[v, s], xr.at[v, s], blk, xdev(d))
            cp.start()
            sends.append(cp)
        for s, d in ((0, 1), (1, -1)):
            cp = rcopy(se.at[xdev(d), v], gath.at[2 * x + v], xs.at[v, 2 + s], xr.at[v, 2 + s], blk, xdev(d))
            cp.start()
            sends.append(cp)

    def relay_second(v):
        cps = []
        for s, d in ((0, 1), (1, -1)):
            half = pl.ds(32 * s, 32)
            sends[v * 4 + s].wait_recv()
            src = xdev(-d)
            cp = rcopy(rel1.at[v, s], gath.at[2 * src + v, :, half, :], fs.at[v, s], fr.at[v, s], blk, xdev(d))
            cp.start()
            cps.append(cp)
        return cps

    second_pass(0)
    send_second(0)

    mine.wait()
    other.wait()
    for cp in z_copies:
        cp.wait()
    ring = []

    def ring_step(s):
        cps = []
        for side, dz in ((0, 1), (1, -1)):
            n = 5 + (s - 1) * 2 + side
            slot = lax.rem(z - dz * s + NZ, NZ)
            if s < 3:
                part = zb.at[slot]
            else:
                part = zb.at[slot, side]
            cp = rcopy(part, part, zs.at[n], zr.at[n], zdev(dz, c), x)
            cp.start()
            cps.append(cp)
        return cps

    ring1 = ring_step(1)
    second_pass(1)
    send_second(1)
    for cp in ring1:
        cp.wait()
    ring2 = ring_step(2)
    relays0 = relay_second(0)
    for cp in ring2:
        cp.wait()
    ring3 = ring_step(3)
    for cp in q_copies:
        cp.wait()
    tosmem = pltpu.make_async_copy(rq, rqs, loc_sem.at[1])
    tosmem.start()
    mygath = pltpu.make_async_copy(se.at[x], gath.at[pl.ds(2 * x, 2)], loc_sem.at[2])
    mygath.start()
    relays1 = relay_second(1)
    tosmem.wait()
    for cp in ring3:
        cp.wait()

    def pick(i, _):
        to, r = i // 4, lax.rem(i, 4)
        bid = rqs[to, 0, r]
        side = lax.rem(r, 2)
        o2[to, r] = zb[bid >> 4, (bid >> 1) & 1, (bid & 1) * 2 + (1 - side)]
        return 0

    lax.fori_loop(0, 4 * NR, pick, 0)
    y_copies = []
    for d in range(1, NR):
        to = lax.rem(rho + d, NR)
        cp = rcopy(o2.at[to], rb.at[rho], ys.at[d - 1], yr.at[d - 1], z * NR + to, x)
        cp.start()
        y_copies.append(cp)
    rb[rho] = o2[rho]
    for cp in y_copies:
        cp.wait()

    rev = 127 - lane8

    def unpack(i, _):
        b, side, v = i // 4, lax.rem(i // 2, 2), lax.rem(i, 2)
        r = b * 2 + side
        bid = nbr[b, side]
        f_ = flip[b, side]
        lane_row = b * 8 + side * 2 + v
        src = ((bid >> 2) & 3) * 2 + v
        for h in range(3):
            q = rb[src, r, 8 * h:8 * h + 8, :]
            turned = jnp.take_along_axis(q, rev, axis=1)
            rowh = iota8 + 8 * h
            neg = jnp.logical_or(jnp.logical_or(rowh == 2, rowh == 3), jnp.logical_or(rowh == 12, rowh == 13))
            turned = jnp.where(neg, -turned, turned)
            q = jnp.where(f_ > 0, turned, q)
            for j in range(8):
                w = 8 * h + j
                if w >= 22:
                    continue
                item, k = (w // 2, w % 2)
                gst[item, pl.ds(lane_row + 4 * k, 1), :] = q[j:j + 1, :]
        sign = jnp.where(f_ > 0, -1.0, 1.0) + jnp.zeros((1, 128), F32)
        for k in range(2):
            gst[11, pl.ds(lane_row + 4 * k, 1), :] = sign
        return 0

    lax.fori_loop(0, 8, unpack, 0)

    sig = jnp.where((iota8 >> 1) & 1 == 0, -1.0, 1.0)
    sk = jnp.where(iota8 < 4, 1.0, -1.0)
    odd = iota8 & 1

    def jmul(d, g_, f):
        acc = jac[d, f, 0] * g_[0]
        for g in range(1, NF):
            acc = acc + jac[d, f, g] * g_[g]
        return acc

    def fix(b, sums):
        base = pl.ds(pl.multiple_of(b * 8, 8), 8)
        g0 = [gst[f, base, :] for f in range(NF)]
        gf = [gst[NF + f, base, :] for f in range(NF)]
        gm = gst[10, base, :]
        turn = gst[11, base, :]
        o = [own[f, base, :] for f in range(NF)]
        of = [own[NF + f, base, :] for f in range(NF)]
        m0 = own[10, base, :]
        m1 = own[11, base, :]
        od = [o[f] * turn if f == 1 else o[f] for f in range(NF)]
        g1, c1 = [], []
        total = zero8
        for f in range(NF):
            tf = jmul(1, od, f)
            if f == 1:
                tf = tf * turn
            g1.append(gf[f] + VISC * o[f] + sig * gm * tf)
            cf = VISC * g0[f] - sig * m0 * jmul(1, g0, f)
            c1.append(cf)
            ff = of[f] + cf
            total = total + ff * ff
        e = [pltpu.roll(cf, 127, 1) for cf in c1]
        w = [pltpu.roll(cf, 1, 1) for cf in c1]
        ok = [pltpu.roll(cf, 4, 0) for cf in c1]
        ew = [a - b_ for a, b_ in zip(e, w)]
        for f in range(NF):
            flux = jmul(0, ew, f) + sk * jmul(2, ok, f) + sig * jmul(1, g1, f)
            face = (1.0 - 6.0 * VISC) * c1[f] + VISC * (e[f] + w[f] + ok[f] + g1[f]) - m0 * flux
            near = VISC * c1[f] - sig * m1 * jmul(1, c1, f)
            face = face * SCALE
            near = near * SCALE
            cs[b * 2, f, 0:4, :] = face[0:4]
            cs[b * 2, f, 4:8, :] = near[0:4]
            cs[b * 2 + 1, f, 0:4, :] = face[4:8]
            cs[b * 2 + 1, f, 4:8, :] = near[4:8]
        s0, s1 = sums
        return s0 + jnp.where(odd == 0, total, 0.0), s1 + jnp.where(odd == 1, total, 0.0)

    ssq = lax.fori_loop(0, 2, fix, ssq)
    c_copies = []
    for d in (2, 1, 3):
        cp = rcopy(cs.at[xdev(d)], cb.at[x], cs_s.at[d - 1], cs_r.at[d - 1], blk, xdev(d))
        cp.start()
        c_copies.append(cp)
    cb[x] = cs[x]

    mygath.wait()
    for cp in sends[2:4] + sends[6:8]:
        cp.wait()
    for cp in sends[0:2] + sends[4:6]:
        cp.wait_send()
    for cp in relays0 + relays1:
        cp.wait()
    for cp in c_copies:
        cp.wait()

    bq = x // 2
    my_last = jnp.where(bq == 0, rows[0], rows[1]) - 1

    def gram_tile(i, acc):
        f, t = i // 8, lax.rem(i, 8)
        row = iota8 + t * 8
        at = [row == 0, row == my_last, row == 1, row == my_last - 1]
        vals = []
        for v in range(8):
            q = gath[v, f, pl.ds(pl.multiple_of(t * 8, 8), 8), :]
            for n, (typ, side) in enumerate(((0, 0), (0, 1), (1, 0), (1, 1))):
                w = typ * 4 + side * 2 + v % 2
                q = q + jnp.where(at[n], jnp.broadcast_to(cb[v // 2, f, w:w + 1, :], (8, 128)), 0.0)
            gath[v, f, pl.ds(pl.multiple_of(t * 8, 8), 8), :] = q
            vals.append(q)
        res = list(acc)
        for v in range(8):
            for w in range(v + 1):
                res[pair(v, w)] = res[pair(v, w)] + vals[v] * vals[w]
        return tuple(res)

    grams = lax.fori_loop(0, 40, gram_tile, tuple(zero8 for _ in range(36)))
    gacc[...] = jnp.zeros((128, 128), F32)
    for n in range(36):
        gacc[n:n + 1, :] = jnp.sum(grams[n], axis=0, keepdims=True)
    for v in range(2):
        gacc[pl.ds(36 + 2 * x + v, 1), :] = jnp.sum(ssq[v], axis=0, keepdims=True)
    ones8 = jnp.ones((8, 128), F32)
    ar[...] = lax.dot_general(ones8, gacc[...], (((1,), (1,)), ((), ())), precision=HI, preferred_element_type=F32)

    def exchange(buf, me, n, first, dev):
        buf[me] = ar[...]
        cps = []
        for d in range(1, n):
            b_, x_ = dev(d)
            cp = rcopy(ar, buf.at[me], as_s.at[first + d - 1], as_r.at[first + d - 1], b_, x_)
            cp.start()
            cps.append(cp)
        for cp in cps:
            cp.wait()
        tot = buf[0]
        for j in range(1, n):
            tot = tot + buf[j]
        ar[...] = tot

    exchange(arx, x, NX, 0, lambda d: (blk, xdev(d)))
    exchange(ary, rho, NR, 3, lambda d: (z * NR + lax.rem(rho + d, NR), x))
    exchange(arz, z, NZ, 10, lambda d: (zdev(d, c), x))

    r48 = lax.broadcasted_iota(jnp.int32, (48, 128), 0)
    l48 = lax.broadcasted_iota(jnp.int32, (48, 128), 1)
    spread = jnp.where(r48 == l48, jnp.broadcast_to(ar[0:1, :], (48, 128)), 0.0)
    spl[...] = jnp.dot(spread, jnp.ones((128, 128), F32), precision=HI, preferred_element_type=F32)

    def entry(n):
        return spl[n:n + 1, :]

    s = [1.0 / (SCALE * jnp.sqrt(entry(36 + v) + EPS)) for v in range(8)]
    low = {}
    inv = []
    for j in range(8):
        a = entry(pair(j, j)) * s[j] * s[j]
        for k in range(j):
            a = a - low[j, k] * low[j, k]
        low[j, j] = jnp.sqrt(a)
        inv.append(1.0 / low[j, j])
        for i in range(j + 1, 8):
            a = entry(pair(i, j)) * s[i] * s[j]
            for k in range(j):
                a = a - low[i, k] * low[j, k]
            low[i, j] = a * inv[j]
    xx = {}
    for j in range(8):
        xx[j, j] = inv[j]
        for i in range(j + 1, 8):
            a = low[i, j] * xx[j, j]
            for k in range(j + 1, i):
                a = a + low[i, k] * xx[k, j]
            xx[i, j] = -a * inv[i]
    upper = zero8
    for i in range(8):
        for j in range(i + 1):
            mix[pair(i, j)] = jnp.broadcast_to(xx[i, j] * s[j], (8, 128))
            upper = jnp.where(jnp.logical_and(iota8 == j, lane8 == i), jnp.broadcast_to(low[i, j], (8, 128)), upper)
    fac[...] = upper[:, 0:8]

    def combine(i, _):
        f, t = i // 8, lax.rem(i, 8)
        rr = pl.ds(pl.multiple_of(t * 8, 8), 8)
        vals = [gath[v, f, rr, :] for v in range(8)]
        for v in range(8):
            a = mix[pair(v, 0)] * vals[0]
            for w in range(1, v + 1):
                a = a + mix[pair(v, w)] * vals[w]
            bas[v, f, rr, :] = a
        return 0

    lax.fori_loop(0, 40, combine, 0)
    kq = lax.rem(x, 2)
    homes, first_hops, relays = [], [], []
    far = xdev(2)
    for v in range(2):
        for sd, d in ((0, 1), (1, -1)):
            half = pl.ds(32 * sd, 32)
            cp = rcopy(bas.at[2 * far + v, :, half, :], rel2.at[v, sd], os.at[v, sd], orr.at[v, sd], blk, xdev(d))
            cp.start()
            first_hops.append(cp)
    for v in range(2):
        for sd, d in ((0, 1), (1, -1)):
            cp = rcopy(bas.at[2 * xdev(d) + v], out.at[v, bq, :, kq], os.at[v, 2 + sd], orr.at[v, 2 + sd], blk, xdev(d))
            cp.start()
            homes.append(cp)
    keep = []
    for v in range(2):
        cp = pltpu.make_async_copy(bas.at[2 * x + v], out.at[v, bq, :, kq], loc_sem.at[3 + v])
        cp.start()
        keep.append(cp)
    for v in range(2):
        for sd, d in ((0, 1), (1, -1)):
            half = pl.ds(32 * sd, 32)
            first_hops[v * 2 + sd].wait_recv()
            src = xdev(-d)
            cp = rcopy(rel2.at[v, sd], out.at[v, src // 2, :, lax.rem(src, 2), half, :], os.at[v, 4 + sd], orr.at[v, 4 + sd], blk, xdev(d))
            cp.start()
            relays.append(cp)
    for cp in keep:
        cp.wait()
    for cp in first_hops:
        cp.wait_send()
    for cp in homes + relays:
        cp.wait()


def per_device(vectors, metric, jacobians, block_rows, neighbours, flipped):
    vm = pl.BlockSpec(memory_space=pltpu.VMEM)
    sm = pl.BlockSpec(memory_space=pltpu.SMEM)
    dma = pltpu.SemaphoreType.DMA
    return pl.pallas_call(
        kernel,
        out_shape=(jax.ShapeDtypeStruct(vectors.shape, F32), jax.ShapeDtypeStruct((8, 8), F32)),
        in_specs=[vm, vm, sm, sm, sm, sm],
        out_specs=(pl.BlockSpec(memory_space=pl.ANY), vm),
        scratch_shapes=[
            pltpu.VMEM((2, 2, NF, 2, 80, 128), F32),
            pltpu.VMEM((2, 2, NF, 2, 80, 128), F32),
            pltpu.VMEM((4, 2, NF, 64, 128), F32),
            pltpu.VMEM((8, NF, 64, 128), F32),
            pltpu.VMEM((8, NF, 64, 128), F32),
            pltpu.VMEM((2, 2, NF, 32, 128), F32),
            pltpu.VMEM((2, 2, NF, 32, 128), F32),
            pltpu.VMEM((2, 4, 24, 128), F32),
            pltpu.VMEM((NZ, NC, 4, 24, 128), F32),
            pltpu.VMEM((NR, 8, 128), jnp.int32),
            pltpu.SMEM((NR, 8, 128), jnp.int32),
            pltpu.VMEM((NR, 4, 24, 128), F32),
            pltpu.VMEM((NR, 4, 24, 128), F32),
            pltpu.VMEM((12, 16, 128), F32),
            pltpu.VMEM((12, 16, 128), F32),
            pltpu.VMEM((4, NF, 8, 128), F32),
            pltpu.VMEM((4, NF, 8, 128), F32),
            pltpu.VMEM((128, 128), F32),
            pltpu.VMEM((8, 128), F32),
            pltpu.VMEM((NX, 8, 128), F32),
            pltpu.VMEM((NR, 8, 128), F32),
            pltpu.VMEM((NZ, 8, 128), F32),
            pltpu.VMEM((48, 128), F32),
            pltpu.VMEM((36, 8, 128), F32),
            dma((5,)),
            dma((2, 4)), dma((2, 4)),
            dma((2, 2)), dma((2, 2)),
            dma((11,)), dma((11,)),
            dma((7,)), dma((7,)),
            dma((7,)), dma((7,)),
            dma((3,)), dma((3,)),
            dma((17,)), dma((17,)),
            dma((2, 6)), dma((2, 6)),
        ],
        compiler_params=pltpu.CompilerParams(collective_id=0, has_side_effects=True, vmem_limit_bytes=48 * 1024 * 1024),
        cost_estimate=pl.CostEstimate(flops=60_000_000, bytes_accessed=4_000_000, transcendentals=0),
    )(vectors, metric, jacobians, block_rows, neighbours, flipped)


def solution(mesh):
    wide = P("vec", "blk", None, None, None, None)
    in_specs = (wide, P("blk", None, None, None), P(), P("blk"), P("blk", None), P("blk", None))
    return jax.shard_map(per_device, mesh=mesh, in_specs=in_specs, out_specs=(wide, P()), check_vma=False)
```

```python
import jax
import jax.numpy as jnp
from jax import lax
from jax.experimental import pallas as pl
from jax.experimental.pallas import tpu as pltpu
from jax.sharding import PartitionSpec as P

MESH = pl.DeviceIdType.MESH
F32 = jnp.float32
HI = lax.Precision.HIGHEST
NF = 5
NZ, NY, NC, NX = 8, 4, 2, 4
NR = NY * NC
VISC = 0.1
EPS = 1e-06
SCALE = 1024.0


def pair(v, w):
    return v * (v + 1) // 2 + w


def kernel(vec_h, met_h, jac_h, rows_h, nbr_h, flip_h, out, fac,
           vec, met, jac, rows, nbr, flip, st, fi, se, gath, bas, pay, zb, rq, rqs, o2, rb, own, gst, cs, cb, gacc, ar, ar2, arx, ary, spl, mix,
           loc_sem, in_sem, vec_sem, xs, xr, zs, zr, qs, qr, ys, yr, cs_s, cs_r, as_s, as_r, os, orr):
    blk = lax.axis_index("blk")
    x = lax.axis_index("vec")
    z = blk // NR
    rho = lax.rem(blk, NR)
    c = lax.rem(blk, NC)
    col = lax.rem(blk, NR)

    def zdev(dz, core):
        zz = lax.rem(z + dz + NZ, NZ)
        return zz * NR + (rho - c) + core

    small = [pltpu.make_async_copy(h, d, in_sem.at[n]) for n, (h, d) in enumerate(
        ((rows_h, rows), (jac_h, jac), (nbr_h, nbr), (flip_h, flip), (met_h, met)))]
    big = [pltpu.make_async_copy(vec_h.at[n // 2, n % 2], vec.at[n // 2, n % 2], vec_sem.at[n]) for n in range(4)]
    for cp in small[:1] + big + small[1:]:
        cp.start()

    bar = pltpu.get_barrier_semaphore()
    def xdev(d):
        return lax.rem(x + d + NX, NX)

    def zc(d):
        m = lax.rem(z * NC + c + d, NZ * NC)
        return (m // NC) * NR + (rho - c) + lax.rem(m, NC), x

    def yx(d):
        m = lax.rem((rho // NC) * NX + x + d, (NR // NC) * NX)
        return z * NR + (m // NX) * NC + c, lax.rem(m, NX)

    def yc(d):
        return z * NR + lax.rem(rho + d, NR), x

    partners = [zc(d) for d in range(1, 16)] + [yx(d) for d in range(1, 16)]
    partners += [(z * NR + lax.rem(rho - c + NC * d, NR) + 1 - c, x) for d in range(1, NR // NC)]
    for b_, x_ in partners:
        pl.semaphore_signal(bar, inc=1, device_id={"blk": b_, "vec": x_}, device_id_type=MESH)
    n_part = len(partners)

    def rcopy(src, dst, ssem, rsem, b_, x_):
        return pltpu.make_async_remote_copy(src_ref=src, dst_ref=dst, send_sem=ssem, recv_sem=rsem,
                                            device_id={"blk": b_, "vec": x_}, device_id_type=MESH)

    iota64 = lax.broadcasted_iota(jnp.int32, (64, 128), 0)
    iota8 = lax.broadcasted_iota(jnp.int32, (8, 128), 0)
    lane8 = lax.broadcasted_iota(jnp.int32, (8, 128), 1)
    zero8 = jnp.zeros((8, 128), F32)

    def fill(i, _):
        vb = i // 10
        v, b = vb // 2, lax.rem(vb, 2)
        fk = lax.rem(i, 10)
        f, k = fk // 2, lax.rem(fk, 2)
        q = vec[v, b, f, k]
        st[v, b, f, k, 8:72, :] = jnp.where(iota64 < rows[b], q, 0.0)
        st[v, b, f, k, 0:8, :] = zero8
        st[v, b, f, k, 72:80, :] = zero8
        fi[v, b, f, k, 0:8, :] = zero8
        fi[v, b, f, k, 72:80, :] = zero8
        return 0

    small[0].wait()
    for n in range(4):
        big[n].wait()
        lax.fori_loop(10 * n, 10 * n + 10, fill, 0)
    for cp in small[1:]:
        cp.wait()

    def advance_tile(src, v, b, t, scale, store):
        r0 = pl.multiple_of(t * 8, 8)
        alive = (iota8 + r0) < rows[b]
        qs_, d0, d1, base = [], [], [], []
        for k in range(2):
            qk = [src[v, b, f, k, pl.ds(r0 + 8, 8), :] for f in range(NF)]
            qs_.append(qk)
        for k in range(2):
            a0, a1, ab = [], [], []
            for f in range(NF):
                q = qs_[k][f]
                e = pltpu.roll(q, 127, 1)
                w = pltpu.roll(q, 1, 1)
                n = src[v, b, f, k, pl.ds(r0 + 9, 8), :]
                s = src[v, b, f, k, pl.ds(r0 + 7, 8), :]
                a0.append(e - w)
                a1.append(n - s)
                ab.append((scale * (1.0 - 6.0 * VISC)) * q + (scale * VISC) * ((e + w) + (n + s) + qs_[1 - k][f]))
            d0.append(a0)
            d1.append(a1)
            base.append(ab)
        mk = [met[b, k, pl.ds(r0, 8), :] * scale for k in range(2)]
        for f in range(NF):
            c0 = [jac[f, 0, g] for g in range(NF)]
            c1 = [jac[f, 1, g] for g in range(NF)]
            c2 = [jac[f, 2, g] for g in range(NF)]
            for k in range(2):
                acc = c0[0] * d0[k][0] + c1[0] * d1[k][0]
                oth = c2[0] * qs_[1 - k][0]
                for g in range(1, NF):
                    acc = acc + c0[g] * d0[k][g] + c1[g] * d1[k][g]
                    oth = oth + c2[g] * qs_[1 - k][g]
                flux = acc + oth if k == 0 else acc - oth
                store(f, k, jnp.where(alive, base[k][f] - mk[k] * flux, 0.0))

    def first_pass(i, sums):
        vb, t = i // 8, lax.rem(i, 8)
        v, b = vb // 2, lax.rem(vb, 2)
        r0 = t * 8
        row = iota8 + r0
        inner = jnp.logical_and(row > 0, row != rows[b] - 1)
        box = [jnp.zeros((8, 128), F32)]

        def store(f, k, val):
            fi[v, b, f, k, pl.ds(pl.multiple_of(r0 + 8, 8), 8), :] = val
            box[0] = box[0] + val * val

        advance_tile(st, v, b, t, 1.0, store)
        sq = jnp.where(inner, box[0], 0.0)
        s0, s1 = sums
        return s0 + jnp.where(v == 0, sq, 0.0), s1 + jnp.where(v == 1, sq, 0.0)

    ssq = lax.fori_loop(0, 32, first_pass, (zero8, zero8))

    def faces(i, _):
        b, side, v = i // 4, lax.rem(i // 2, 2), lax.rem(i, 2)
        last = jnp.maximum(rows[b] - 1, 1)
        r = jnp.where(side == 0, 0, last)
        adj = jnp.where(side == 0, 1, last - 1)
        slot = b * 2 + side
        lane_row = b * 8 + side * 2 + v
        for f in range(NF):
            for k in range(2):
                a = st[v, b, f, k, pl.ds(r + 8, 1), :]
                p = fi[v, b, f, k, pl.ds(r + 8, 1), :]
                pay[v, slot, f * 2 + k:f * 2 + k + 1, :] = a
                pay[v, slot, 10 + f * 2 + k:11 + f * 2 + k, :] = p
                own[f, pl.ds(lane_row + 4 * k, 1), :] = a
                own[NF + f, pl.ds(lane_row + 4 * k, 1), :] = p
        for k in range(2):
            m = met[b, k, pl.ds(r, 1), :]
            pay[v, slot, 20 + k:21 + k, :] = m
            pay[v, slot, 22 + k:23 + k, :] = m
            own[10, pl.ds(lane_row + 4 * k, 1), :] = m
            own[11, pl.ds(lane_row + 4 * k, 1), :] = met[b, k, pl.ds(adj, 1), :]
        return 0

    lax.fori_loop(0, 8, faces, 0)
    req = jnp.where(lane8 == 0, nbr[0, 0], jnp.where(lane8 == 1, nbr[0, 1], jnp.where(lane8 == 2, nbr[1, 0], nbr[1, 1])))
    rq[rho] = req

    pl.semaphore_wait(bar, n_part)

    mine = pltpu.make_async_copy(pay.at[c], zb.at[z, c], loc_sem.at[0])
    mine.start()
    z_copies = []
    for j in range(2):
        core = lax.rem(c + j, NC)
        for side, dz in ((0, 1), (1, -1)):
            n = j * 2 + side
            cp = rcopy(pay.at[core], zb.at[z, c], zs.at[n], zr.at[n], zdev(dz, core), x)
            cp.start()
            z_copies.append(cp)
    other = rcopy(pay.at[1 - c], zb.at[z, c], zs.at[4], zr.at[4], zdev(0, 1 - c), x)
    other.start()
    q_copies = []
    for d in range(1, NR):
        cp = rcopy(rq.at[rho], rq.at[rho], qs.at[d - 1], qr.at[d - 1], z * NR + lax.rem(rho + d, NR), x)
        cp.start()
        q_copies.append(cp)

    def second_pass(v):
        def body(i, _):
            b, t = i // 8, lax.rem(i, 8)

            def store(f, k, val):
                se[b * 2 + k, v, f, pl.ds(pl.multiple_of(t * 8, 8), 8), :] = val

            advance_tile(fi, v, b, t, SCALE, store)
            return 0

        lax.fori_loop(0, 16, body, 0)

    sends = []

    def send_second(v):
        for d in (2, 1, 3):
            cp = rcopy(se.at[xdev(d), v], gath.at[2 * x + v], xs.at[v, d - 1], xr.at[v, d - 1], blk, xdev(d))
            cp.start()
            sends.append(cp)

    second_pass(0)
    send_second(0)

    drain = z_copies + [other]

    def ring_step(s, before):
        cps = []
        for j in range(2):
            core = lax.rem(c + j, NC)
            for side, dz in ((0, 1), (1, -1)):
                if s == 3 and side != j:
                    before[j * 2 + side].wait_recv()
                    continue
                n = 5 + (s - 1) * 4 + j * 2 + side
                slot = lax.rem(z - dz * s + NZ, NZ)
                part = zb.at[slot, core]
                before[j * 2 + side].wait_recv()
                cp = rcopy(part, part, zs.at[n], zr.at[n], zdev(dz, c), x)
                cp.start()
                cps.append(cp)
        drain.extend(cps)
        return cps

    ring1 = ring_step(1, z_copies)
    second_pass(1)
    send_second(1)
    ring2 = ring_step(2, ring1)
    mygath = pltpu.make_async_copy(se.at[x], gath.at[pl.ds(2 * x, 2)], loc_sem.at[2])
    mygath.start()
    for cp in q_copies:
        cp.wait_recv()
    tosmem = pltpu.make_async_copy(rq, rqs, loc_sem.at[1])
    tosmem.start()
    ring3 = ring_step(3, ring2)
    mine.wait()
    other.wait_recv()
    tosmem.wait()
    for cp in ring3:
        cp.wait_recv()

    def pick(i, _):
        to, r = i // 4, lax.rem(i, 4)
        bid = rqs[to, 0, r]
        side = lax.rem(r, 2)
        o2[to, r] = zb[bid >> 4, (bid >> 1) & 1, (bid & 1) * 2 + (1 - side)]
        return 0

    lax.fori_loop(0, 4 * NR, pick, 0)
    y_copies = []
    for d in range(1, NR):
        to = lax.rem(rho + d, NR)
        cp = rcopy(o2.at[to], rb.at[rho], ys.at[d - 1], yr.at[d - 1], z * NR + to, x)
        cp.start()
        y_copies.append(cp)
    rb[rho] = o2[rho]
    for cp in y_copies:
        cp.wait_recv()
    drain += y_copies + q_copies

    rev = 127 - lane8

    def unpack(i, _):
        b, side, v = i // 4, lax.rem(i // 2, 2), lax.rem(i, 2)
        r = b * 2 + side
        bid = nbr[b, side]
        f_ = flip[b, side]
        lane_row = b * 8 + side * 2 + v
        src = ((bid >> 2) & 3) * 2 + v
        for h in range(3):
            q = rb[src, r, 8 * h:8 * h + 8, :]
            turned = jnp.take_along_axis(q, rev, axis=1)
            rowh = iota8 + 8 * h
            neg = jnp.logical_or(jnp.logical_or(rowh == 2, rowh == 3), jnp.logical_or(rowh == 12, rowh == 13))
            turned = jnp.where(neg, -turned, turned)
            q = jnp.where(f_ > 0, turned, q)
            for j in range(8):
                w = 8 * h + j
                if w >= 22:
                    continue
                item, k = (w // 2, w % 2)
                gst[item, pl.ds(lane_row + 4 * k, 1), :] = q[j:j + 1, :]
        sign = jnp.where(f_ > 0, -1.0, 1.0) + jnp.zeros((1, 128), F32)
        for k in range(2):
            gst[11, pl.ds(lane_row + 4 * k, 1), :] = sign
        return 0

    lax.fori_loop(0, 8, unpack, 0)

    sig = jnp.where((iota8 >> 1) & 1 == 0, -1.0, 1.0)
    sk = jnp.where(iota8 < 4, 1.0, -1.0)
    odd = iota8 & 1

    def jmul(d, g_, f):
        acc = jac[f, d, 0] * g_[0]
        for g in range(1, NF):
            acc = acc + jac[f, d, g] * g_[g]
        return acc

    def fix(b, sums):
        base = pl.ds(pl.multiple_of(b * 8, 8), 8)
        g0 = [gst[f, base, :] for f in range(NF)]
        gf = [gst[NF + f, base, :] for f in range(NF)]
        gm = gst[10, base, :]
        turn = gst[11, base, :]
        o = [own[f, base, :] for f in range(NF)]
        of = [own[NF + f, base, :] for f in range(NF)]
        m0 = own[10, base, :]
        m1 = own[11, base, :]
        od = [o[f] * turn if f == 1 else o[f] for f in range(NF)]
        g1, c1 = [], []
        total = zero8
        for f in range(NF):
            tf = jmul(1, od, f)
            if f == 1:
                tf = tf * turn
            g1.append(gf[f] + VISC * o[f] + sig * gm * tf)
            cf = VISC * g0[f] - sig * m0 * jmul(1, g0, f)
            c1.append(cf)
            ff = of[f] + cf
            total = total + ff * ff
        e = [pltpu.roll(cf, 127, 1) for cf in c1]
        w = [pltpu.roll(cf, 1, 1) for cf in c1]
        ok = [pltpu.roll(cf, 4, 0) for cf in c1]
        ew = [a - b_ for a, b_ in zip(e, w)]
        for f in range(NF):
            flux = jmul(0, ew, f) + sk * jmul(2, ok, f) + sig * jmul(1, g1, f)
            face = (1.0 - 6.0 * VISC) * c1[f] + VISC * (e[f] + w[f] + ok[f] + g1[f]) - m0 * flux
            near = VISC * c1[f] - sig * m1 * jmul(1, c1, f)
            face = face * SCALE
            near = near * SCALE
            cs[b * 2, f, 0:4, :] = face[0:4]
            cs[b * 2, f, 4:8, :] = near[0:4]
            cs[b * 2 + 1, f, 0:4, :] = face[4:8]
            cs[b * 2 + 1, f, 4:8, :] = near[4:8]
        s0, s1 = sums
        return s0 + jnp.where(odd == 0, total, 0.0), s1 + jnp.where(odd == 1, total, 0.0)

    ssq = lax.fori_loop(0, 2, fix, ssq)
    c_copies = []
    for d in (2, 1, 3):
        cp = rcopy(cs.at[xdev(d)], cb.at[x], cs_s.at[d - 1], cs_r.at[d - 1], blk, xdev(d))
        cp.start()
        c_copies.append(cp)
    cb[x] = cs[x]

    mygath.wait()
    for cp in sends + c_copies:
        cp.wait_recv()
    drain += sends + c_copies

    bq = x // 2
    my_last = jnp.where(bq == 0, rows[0], rows[1]) - 1

    def gram_tile(i, acc):
        f, t = i // 8, lax.rem(i, 8)
        row = iota8 + t * 8
        at = [row == 0, row == my_last, row == 1, row == my_last - 1]
        vals = []
        for v in range(8):
            q = gath[v, f, pl.ds(pl.multiple_of(t * 8, 8), 8), :]
            for n, (typ, side) in enumerate(((0, 0), (0, 1), (1, 0), (1, 1))):
                w = typ * 4 + side * 2 + v % 2
                q = q + jnp.where(at[n], jnp.broadcast_to(cb[v // 2, f, w:w + 1, :], (8, 128)), 0.0)
            gath[v, f, pl.ds(pl.multiple_of(t * 8, 8), 8), :] = q
            vals.append(q)
        res = list(acc)
        for v in range(8):
            for w in range(v + 1):
                res[pair(v, w)] = res[pair(v, w)] + vals[v] * vals[w]
        return tuple(res)

    grams = lax.fori_loop(0, 40, gram_tile, tuple(zero8 for _ in range(36)))
    gacc[...] = jnp.zeros((128, 128), F32)
    for n in range(36):
        gacc[n:n + 1, :] = jnp.sum(grams[n], axis=0, keepdims=True)
    for v in range(2):
        gacc[pl.ds(36 + 2 * x + v, 1), :] = jnp.sum(ssq[v], axis=0, keepdims=True)
    ones8 = jnp.ones((8, 128), F32)
    ar[...] = lax.dot_general(ones8, gacc[...], (((1,), (1,)), ((), ())), precision=HI, preferred_element_type=F32)

    def exchange(src, buf, me, first, dev):
        buf[me] = src[...]
        cps = []
        for d in range(1, 16):
            b_, x_ = dev(d)
            cp = rcopy(src, buf.at[me], as_s.at[first + d - 1], as_r.at[first + d - 1], b_, x_)
            cp.start()
            cps.append(cp)
        for cp in cps:
            cp.wait_recv()
        drain.extend(cps)
        tot = [buf[j] for j in range(16)]
        while len(tot) > 1:
            tot = [a + b_ for a, b_ in zip(tot[::2], tot[1::2])]
        return tot[0]

    ar2[...] = exchange(ar, arx, z * NC + c, 0, zc)
    ar3 = exchange(ar2, ary, (rho // NC) * NX + x, 15, yx)

    r48 = lax.broadcasted_iota(jnp.int32, (48, 128), 0)
    l48 = lax.broadcasted_iota(jnp.int32, (48, 128), 1)
    spread = jnp.where(r48 == l48, jnp.broadcast_to(ar3[0:1, :], (48, 128)), 0.0)
    spl[...] = jnp.dot(spread, jnp.ones((128, 128), F32), precision=HI, preferred_element_type=F32)

    def entry(n):
        return spl[n:n + 1, :]

    s = [1.0 / (SCALE * jnp.sqrt(entry(36 + v) + EPS)) for v in range(8)]
    low = {}
    inv = []
    for j in range(8):
        a = entry(pair(j, j)) * s[j] * s[j]
        for k in range(j):
            a = a - low[j, k] * low[j, k]
        inv.append(lax.rsqrt(a))
        low[j, j] = a * inv[j]
        for i in range(j + 1, 8):
            a = entry(pair(i, j)) * s[i] * s[j]
            for k in range(j):
                a = a - low[i, k] * low[j, k]
            low[i, j] = a * inv[j]
    xx = {}
    for j in range(8):
        xx[j, j] = inv[j]
        for i in range(j + 1, 8):
            a = low[i, j] * xx[j, j]
            for k in range(j + 1, i):
                a = a + low[i, k] * xx[k, j]
            xx[i, j] = -a * inv[i]
    upper = zero8
    for i in range(8):
        for j in range(i + 1):
            mix[pair(i, j)] = jnp.broadcast_to(xx[i, j] * s[j], (8, 128))
            upper = jnp.where(jnp.logical_and(iota8 == j, lane8 == i), jnp.broadcast_to(low[i, j], (8, 128)), upper)
    fac[...] = upper[:, 0:8]

    def combine(i, _):
        f, t = i // 8, lax.rem(i, 8)
        rr = pl.ds(pl.multiple_of(t * 8, 8), 8)
        vals = [gath[v, f, rr, :] for v in range(8)]
        for v in range(8):
            a = mix[pair(v, 0)] * vals[0]
            for w in range(1, v + 1):
                a = a + mix[pair(v, w)] * vals[w]
            bas[v, f, rr, :] = a
        return 0

    lax.fori_loop(0, 40, combine, 0)
    kq = lax.rem(x, 2)
    homes = []
    for v in range(2):
        for d in (2, 1, 3):
            cp = rcopy(bas.at[2 * xdev(d) + v], out.at[v, bq, :, kq], os.at[v, d - 1], orr.at[v, d - 1], blk, xdev(d))
            cp.start()
            homes.append(cp)
    keep = []
    for v in range(2):
        cp = pltpu.make_async_copy(bas.at[2 * x + v], out.at[v, bq, :, kq], loc_sem.at[3 + v])
        cp.start()
        keep.append(cp)
    for cp in keep:
        cp.wait()
    for cp in drain:
        cp.wait_send()
    for cp in homes:
        cp.wait()


def per_device(vectors, metric, jacobians, block_rows, neighbours, flipped):
    vm = pl.BlockSpec(memory_space=pltpu.VMEM)
    hbm = pl.BlockSpec(memory_space=pltpu.HBM)
    dma = pltpu.SemaphoreType.DMA
    return pl.pallas_call(
        kernel,
        out_shape=(jax.ShapeDtypeStruct(vectors.shape, F32), jax.ShapeDtypeStruct((8, 8), F32)),
        in_specs=[hbm] * 6,
        out_specs=(pl.BlockSpec(memory_space=pl.ANY), vm),
        scratch_shapes=[
            pltpu.VMEM(vectors.shape, F32),
            pltpu.VMEM(metric.shape, F32),
            pltpu.SMEM((NF, 3, NF), F32),
            pltpu.SMEM((2,), jnp.int32),
            pltpu.SMEM((2, 2), jnp.int32),
            pltpu.SMEM((2, 2), jnp.int32),
            pltpu.VMEM((2, 2, NF, 2, 80, 128), F32),
            pltpu.VMEM((2, 2, NF, 2, 80, 128), F32),
            pltpu.VMEM((4, 2, NF, 64, 128), F32),
            pltpu.VMEM((8, NF, 64, 128), F32),
            pltpu.VMEM((8, NF, 64, 128), F32),
            pltpu.VMEM((2, 4, 24, 128), F32),
            pltpu.VMEM((NZ, NC, 4, 24, 128), F32),
            pltpu.VMEM((NR, 8, 128), jnp.int32),
            pltpu.SMEM((NR, 8, 128), jnp.int32),
            pltpu.VMEM((NR, 4, 24, 128), F32),
            pltpu.VMEM((NR, 4, 24, 128), F32),
            pltpu.VMEM((12, 16, 128), F32),
            pltpu.VMEM((12, 16, 128), F32),
            pltpu.VMEM((4, NF, 8, 128), F32),
            pltpu.VMEM((4, NF, 8, 128), F32),
            pltpu.VMEM((128, 128), F32),
            pltpu.VMEM((8, 128), F32),
            pltpu.VMEM((8, 128), F32),
            pltpu.VMEM((16, 8, 128), F32),
            pltpu.VMEM((16, 8, 128), F32),
            pltpu.VMEM((48, 128), F32),
            pltpu.VMEM((36, 8, 128), F32),
            dma((5,)), dma((5,)), dma((4,)),
            dma((2, 3)), dma((2, 3)),
            dma((17,)), dma((17,)),
            dma((7,)), dma((7,)),
            dma((7,)), dma((7,)),
            dma((3,)), dma((3,)),
            dma((30,)), dma((30,)),
            dma((2, 3)), dma((2, 3)),
        ],
        compiler_params=pltpu.CompilerParams(collective_id=0, has_side_effects=True, vmem_limit_bytes=62 * 1024 * 1024),
        cost_estimate=pl.CostEstimate(flops=60_000_000, bytes_accessed=4_000_000, transcendentals=0),
    )(vectors, metric, jnp.transpose(jacobians, (1, 0, 2)), block_rows, neighbours, flipped)


def solution(mesh):
    wide = P("vec", "blk", None, None, None, None)
    in_specs = (wide, P("blk", None, None, None), P(), P("blk"), P("blk", None), P("blk", None))
    return jax.shard_map(per_device, mesh=mesh, in_specs=in_specs, out_specs=(wide, P()), check_vma=False)
```

```python
import jax
import jax.numpy as jnp
from jax import lax
from jax.experimental import pallas as pl
from jax.experimental.pallas import tpu as pltpu
from jax.sharding import PartitionSpec as P

MESH = pl.DeviceIdType.MESH
F32 = jnp.float32
HI = lax.Precision.HIGHEST
NF = 5
NZ, NY, NC, NX = 8, 4, 2, 4
NR = NY * NC
VISC = 0.1
EPS = 1e-06
SCALE = 1024.0


DIRECT = [(0, 0, 0, 3), (0, 0, 2, 1), (1, 1, 1, 3), (1, 1, 0, 2), (2, 2, 0, 3), (0, 0, 1, 3), (0, 0, 0, 1), (1, 1, 1, 2), (2, 2, 1, 3),
          (0, 0, 2, 3), (0, 0, 3, 1), (1, 1, 3, 2), (2, 2, 2, 3)]
PASSED = [(1, 0, 1, 2), (3, 0, 3, 2), (2, 1, 2, 3), (0, 1, 0, 3)]
LATE = [(3, 0, 0, 2)]
MOVES = DIRECT + PASSED + LATE


def pair(v, w):
    return v * (v + 1) // 2 + w


def kernel(vec_h, met_h, jac_h, rows_h, nbr_h, flip_h, out, fac,
           vec, met, jac, rows, nbr, flip, st, fi, gath, bas, pay, zb, rq, rqs, o2, rb, own, gst, cb, cb2, gacc, ar, ar2, arx, ary, spl, mix,
           loc_sem, in_sem, vec_sem, xs, xr, zs, zr, qs, qr, ys, yr, cs_s, cs_r, as_s, as_r, ws, wr, cs2_s, cs2_r, out_sem):
    blk = lax.axis_index("blk")
    x = lax.axis_index("vec")
    z = blk // NR
    rho = lax.rem(blk, NR)
    c = lax.rem(blk, NC)
    col = lax.rem(blk, NR)

    def zdev(dz, core):
        zz = lax.rem(z + dz + NZ, NZ)
        return zz * NR + (rho - c) + core

    small = [pltpu.make_async_copy(h, d, in_sem.at[n]) for n, (h, d) in enumerate(
        ((rows_h, rows), (jac_h, jac), (nbr_h, nbr), (flip_h, flip), (met_h, met)))]
    big = [pltpu.make_async_copy(vec_h.at[n // 2, n % 2], vec.at[n // 2, n % 2], vec_sem.at[n]) for n in range(4)]
    for cp in small[:1] + big + small[1:]:
        cp.start()

    bar = pltpu.get_barrier_semaphore()
    def xdev(d):
        return lax.rem(x + d + NX, NX)

    def zc(d):
        m = lax.rem(z * NC + c + d, NZ * NC)
        return (m // NC) * NR + (rho - c) + lax.rem(m, NC), x

    def yx(d):
        m = lax.rem((rho // NC) * NX + x + d, (NR // NC) * NX)
        return z * NR + (m // NX) * NC + c, lax.rem(m, NX)

    def yc(d):
        return z * NR + lax.rem(rho + d, NR), x

    partners = [(zdev(dz, core), x) for dz in (1, -1) for core in range(2)] + [yc(d) for d in range(1, NR)]
    partners += [(blk, xdev(d)) for d in range(1, NX)]
    for b_, x_ in partners:
        pl.semaphore_signal(bar, inc=1, device_id={"blk": b_, "vec": x_}, device_id_type=MESH)
    n_part = len(partners)

    def rcopy(src, dst, ssem, rsem, b_, x_):
        return pltpu.make_async_remote_copy(src_ref=src, dst_ref=dst, send_sem=ssem, recv_sem=rsem,
                                            device_id={"blk": b_, "vec": x_}, device_id_type=MESH)

    iota64 = lax.broadcasted_iota(jnp.int32, (64, 128), 0)
    iota8 = lax.broadcasted_iota(jnp.int32, (8, 128), 0)
    lane8 = lax.broadcasted_iota(jnp.int32, (8, 128), 1)
    zero8 = jnp.zeros((8, 128), F32)

    def fill(i, _):
        vb = i // 10
        v, b = vb // 2, lax.rem(vb, 2)
        fk = lax.rem(i, 10)
        f, k = fk // 2, lax.rem(fk, 2)
        q = vec[v, b, f, k]
        st[v, b, f, k, 8:72, :] = jnp.where(iota64 < rows[b], q, 0.0)
        st[v, b, f, k, 0:8, :] = zero8
        st[v, b, f, k, 72:80, :] = zero8
        fi[v, b, f, k, 0:8, :] = zero8
        fi[v, b, f, k, 72:80, :] = zero8
        return 0

    small[0].wait()
    for n in range(4):
        big[n].wait()
        lax.fori_loop(10 * n, 10 * n + 10, fill, 0)
    for cp in small[1:]:
        cp.wait()

    def advance_tile(src, v, b, t, scale, store):
        r0 = pl.multiple_of(t * 8, 8)
        alive = (iota8 + r0) < rows[b]
        qs_, d0, d1, base = [], [], [], []
        for k in range(2):
            qk = [src[v, b, f, k, pl.ds(r0 + 8, 8), :] for f in range(NF)]
            qs_.append(qk)
        for k in range(2):
            a0, a1, ab = [], [], []
            for f in range(NF):
                q = qs_[k][f]
                e = pltpu.roll(q, 127, 1)
                w = pltpu.roll(q, 1, 1)
                n = src[v, b, f, k, pl.ds(r0 + 9, 8), :]
                s = src[v, b, f, k, pl.ds(r0 + 7, 8), :]
                a0.append(e - w)
                a1.append(n - s)
                ab.append((scale * (1.0 - 6.0 * VISC)) * q + (scale * VISC) * ((e + w) + (n + s) + qs_[1 - k][f]))
            d0.append(a0)
            d1.append(a1)
            base.append(ab)
        mk = [met[b, k, pl.ds(r0, 8), :] * scale for k in range(2)]
        for f in range(NF):
            c0 = [jac[f, 0, g] for g in range(NF)]
            c1 = [jac[f, 1, g] for g in range(NF)]
            c2 = [jac[f, 2, g] for g in range(NF)]
            for k in range(2):
                acc = c0[0] * d0[k][0] + c1[0] * d1[k][0]
                oth = c2[0] * qs_[1 - k][0]
                for g in range(1, NF):
                    acc = acc + c0[g] * d0[k][g] + c1[g] * d1[k][g]
                    oth = oth + c2[g] * qs_[1 - k][g]
                flux = acc + oth if k == 0 else acc - oth
                store(f, k, jnp.where(alive, base[k][f] - mk[k] * flux, 0.0))

    def first_pass(i, sums):
        vb, t = i // 8, lax.rem(i, 8)
        v, b = vb // 2, lax.rem(vb, 2)
        r0 = t * 8
        row = iota8 + r0
        inner = jnp.logical_and(row > 0, row != rows[b] - 1)
        box = [jnp.zeros((8, 128), F32)]

        def store(f, k, val):
            fi[v, b, f, k, pl.ds(pl.multiple_of(r0 + 8, 8), 8), :] = val
            box[0] = box[0] + val * val

        advance_tile(st, v, b, t, 1.0, store)
        sq = jnp.where(inner, box[0], 0.0)
        s0, s1 = sums
        return s0 + jnp.where(v == 0, sq, 0.0), s1 + jnp.where(v == 1, sq, 0.0)

    ssq = lax.fori_loop(0, 32, first_pass, (zero8, zero8))

    def faces(i, _):
        b, side, v = i // 4, lax.rem(i // 2, 2), lax.rem(i, 2)
        last = jnp.maximum(rows[b] - 1, 1)
        r = jnp.where(side == 0, 0, last)
        adj = jnp.where(side == 0, 1, last - 1)
        slot = b * 2 + side
        lane_row = b * 8 + side * 2 + v
        for f in range(NF):
            for k in range(2):
                a = st[v, b, f, k, pl.ds(r + 8, 1), :]
                p = fi[v, b, f, k, pl.ds(r + 8, 1), :]
                pay[v, slot, f * 2 + k:f * 2 + k + 1, :] = a
                pay[v, slot, 10 + f * 2 + k:11 + f * 2 + k, :] = p
                own[f, pl.ds(lane_row + 4 * k, 1), :] = a
                own[NF + f, pl.ds(lane_row + 4 * k, 1), :] = p
        for k in range(2):
            m = met[b, k, pl.ds(r, 1), :]
            pay[v, slot, 20 + k:21 + k, :] = m
            pay[v, slot, 22 + k:23 + k, :] = m
            own[10, pl.ds(lane_row + 4 * k, 1), :] = m
            own[11, pl.ds(lane_row + 4 * k, 1), :] = met[b, k, pl.ds(adj, 1), :]
        return 0

    lax.fori_loop(0, 8, faces, 0)
    req = jnp.where(lane8 == 0, nbr[0, 0], jnp.where(lane8 == 1, nbr[0, 1], jnp.where(lane8 == 2, nbr[1, 0], nbr[1, 1])))
    rq[rho] = req

    pl.semaphore_wait(bar, n_part)

    mine = pltpu.make_async_copy(pay.at[c], zb.at[z, c], loc_sem.at[0])
    mine.start()
    z_copies = []
    for j in range(2):
        core = lax.rem(c + j, NC)
        for side, dz in ((0, 1), (1, -1)):
            n = j * 2 + side
            cp = rcopy(pay.at[core], zb.at[z, c], zs.at[n], zr.at[n], zdev(dz, core), x)
            cp.start()
            z_copies.append(cp)
    other = rcopy(pay.at[1 - c], zb.at[z, c], zs.at[4], zr.at[4], zdev(0, 1 - c), x)
    other.start()
    q_copies = []
    for d in range(1, NR):
        cp = rcopy(rq.at[rho], rq.at[rho], qs.at[d - 1], qr.at[d - 1], z * NR + lax.rem(rho + d, NR), x)
        cp.start()
        q_copies.append(cp)

    def second_pass(v):
        def body(i, _):
            b, t = i // 8, lax.rem(i, 8)

            def store(f, k, val):
                gath[x, b * 2 + k, v, f, pl.ds(pl.multiple_of(t * 8, 8), 8), :] = val

            advance_tile(fi, v, b, t, SCALE, store)
            return 0

        lax.fori_loop(0, 16, body, 0)

    sends = []

    def send_second(v):
        for d in (2, 1, 3):
            here = gath.at[x, xdev(d), v]
            cp = rcopy(here, here, xs.at[v, d - 1], xr.at[v, d - 1], blk, xdev(d))
            cp.start()
            sends.append(cp)

    def move(n):
        frm, src, q, to = MOVES[n]
        part = gath.at[src, q]
        return rcopy(part, part, ws.at[n], wr.at[n], blk, jnp.int32(to))

    def moves(which):
        for n in range(len(MOVES)):
            if MOVES[n] in which:
                @pl.when(x == MOVES[n][0])
                def _():
                    move(n).start()

    second_pass(0)
    send_second(0)

    drain = z_copies + [other]

    def ring_step(s, before):
        cps = []
        for j in range(2):
            core = lax.rem(c + j, NC)
            for side, dz in ((0, 1), (1, -1)):
                if s == 3 and side != j:
                    before[j * 2 + side].wait_recv()
                    continue
                n = 5 + (s - 1) * 4 + j * 2 + side
                slot = lax.rem(z - dz * s + NZ, NZ)
                part = zb.at[slot, core]
                before[j * 2 + side].wait_recv()
                cp = rcopy(part, part, zs.at[n], zr.at[n], zdev(dz, c), x)
                cp.start()
                cps.append(cp)
        drain.extend(cps)
        return cps

    ring1 = ring_step(1, z_copies)
    second_pass(1)
    send_second(1)
    ring2 = ring_step(2, ring1)
    for cp in q_copies:
        cp.wait_recv()
    tosmem = pltpu.make_async_copy(rq, rqs, loc_sem.at[1])
    tosmem.start()
    ring3 = ring_step(3, ring2)
    mine.wait()
    other.wait_recv()
    tosmem.wait()
    for cp in ring3:
        cp.wait_recv()

    def pick(i, _):
        to, r = i // 4, lax.rem(i, 4)
        bid = rqs[to, 0, r]
        side = lax.rem(r, 2)
        o2[to, r] = zb[bid >> 4, (bid >> 1) & 1, (bid & 1) * 2 + (1 - side)]
        return 0

    lax.fori_loop(0, 4 * NR, pick, 0)
    y_copies = []
    for d in range(1, NR):
        to = lax.rem(rho + d, NR)
        cp = rcopy(o2.at[to], rb.at[rho], ys.at[d - 1], yr.at[d - 1], z * NR + to, x)
        cp.start()
        y_copies.append(cp)
    rb[rho] = o2[rho]
    moves(DIRECT)
    for cp in y_copies:
        cp.wait_recv()
    drain += y_copies + q_copies

    rev = 127 - lane8

    def unpack(i, _):
        b, side, v = i // 4, lax.rem(i // 2, 2), lax.rem(i, 2)
        r = b * 2 + side
        bid = nbr[b, side]
        f_ = flip[b, side]
        lane_row = b * 8 + side * 2 + v
        src = ((bid >> 2) & 3) * 2 + v
        for h in range(3):
            q = rb[src, r, 8 * h:8 * h + 8, :]
            turned = jnp.take_along_axis(q, rev, axis=1)
            rowh = iota8 + 8 * h
            neg = jnp.logical_or(jnp.logical_or(rowh == 2, rowh == 3), jnp.logical_or(rowh == 12, rowh == 13))
            turned = jnp.where(neg, -turned, turned)
            q = jnp.where(f_ > 0, turned, q)
            for j in range(8):
                w = 8 * h + j
                if w >= 22:
                    continue
                item, k = (w // 2, w % 2)
                gst[item, pl.ds(lane_row + 4 * k, 1), :] = q[j:j + 1, :]
        sign = jnp.where(f_ > 0, -1.0, 1.0) + jnp.zeros((1, 128), F32)
        for k in range(2):
            gst[11, pl.ds(lane_row + 4 * k, 1), :] = sign
        return 0

    lax.fori_loop(0, 8, unpack, 0)

    sig = jnp.where((iota8 >> 1) & 1 == 0, -1.0, 1.0)
    sk = jnp.where(iota8 < 4, 1.0, -1.0)
    odd = iota8 & 1

    def jmul(d, g_, f):
        acc = jac[f, d, 0] * g_[0]
        for g in range(1, NF):
            acc = acc + jac[f, d, g] * g_[g]
        return acc

    def fix(b, sums):
        base = pl.ds(pl.multiple_of(b * 8, 8), 8)
        g0 = [gst[f, base, :] for f in range(NF)]
        gf = [gst[NF + f, base, :] for f in range(NF)]
        gm = gst[10, base, :]
        turn = gst[11, base, :]
        o = [own[f, base, :] for f in range(NF)]
        of = [own[NF + f, base, :] for f in range(NF)]
        m0 = own[10, base, :]
        m1 = own[11, base, :]
        od = [o[f] * turn if f == 1 else o[f] for f in range(NF)]
        g1, c1 = [], []
        total = zero8
        for f in range(NF):
            tf = jmul(1, od, f)
            if f == 1:
                tf = tf * turn
            g1.append(gf[f] + VISC * o[f] + sig * gm * tf)
            cf = VISC * g0[f] - sig * m0 * jmul(1, g0, f)
            c1.append(cf)
            ff = of[f] + cf
            total = total + ff * ff
        e = [pltpu.roll(cf, 127, 1) for cf in c1]
        w = [pltpu.roll(cf, 1, 1) for cf in c1]
        ok = [pltpu.roll(cf, 4, 0) for cf in c1]
        ew = [a - b_ for a, b_ in zip(e, w)]
        for f in range(NF):
            flux = jmul(0, ew, f) + sk * jmul(2, ok, f) + sig * jmul(1, g1, f)
            face = (1.0 - 6.0 * VISC) * c1[f] + VISC * (e[f] + w[f] + ok[f] + g1[f]) - m0 * flux
            near = VISC * c1[f] - sig * m1 * jmul(1, c1, f)
            face = face * SCALE
            near = near * SCALE
            cb[x, b * 2, f, 0:4, :] = face[0:4]
            cb[x, b * 2, f, 4:8, :] = near[0:4]
            cb[x, b * 2 + 1, f, 0:4, :] = face[4:8]
            cb[x, b * 2 + 1, f, 4:8, :] = near[4:8]
        s0, s1 = sums
        return s0 + jnp.where(odd == 0, total, 0.0), s1 + jnp.where(odd == 1, total, 0.0)

    ssq = lax.fori_loop(0, 2, fix, ssq)
    c_copies = []
    for d in (2, 1, 3):
        here = cb.at[x, xdev(d)]
        cp = rcopy(here, here, cs_s.at[d - 1], cs_r.at[d - 1], blk, xdev(d))
        cp.start()
        c_copies.append(cp)
    for cp in sends:
        cp.wait_recv()
    moves(PASSED)

    for cp in c_copies:
        cp.wait_recv()
    drain += sends + c_copies

    bq = x // 2
    my_last = jnp.where(bq == 0, rows[0], rows[1]) - 1

    def gram_tile(i, acc):
        f, t = i // 8, lax.rem(i, 8)
        row = iota8 + t * 8
        at = [row == 0, row == my_last, row == 1, row == my_last - 1]
        vals = []
        for v in range(8):
            q = gath[v // 2, x, v % 2, f, pl.ds(pl.multiple_of(t * 8, 8), 8), :]
            for n, (typ, side) in enumerate(((0, 0), (0, 1), (1, 0), (1, 1))):
                w = typ * 4 + side * 2 + v % 2
                q = q + jnp.where(at[n], jnp.broadcast_to(cb[v // 2, x, f, w:w + 1, :], (8, 128)), 0.0)
            vals.append(q)
        res = list(acc)
        for v in range(8):
            for w in range(v + 1):
                res[pair(v, w)] = res[pair(v, w)] + vals[v] * vals[w]
        return tuple(res)

    grams = lax.fori_loop(0, 40, gram_tile, tuple(zero8 for _ in range(36)))
    gacc[...] = jnp.zeros((128, 128), F32)
    for n in range(36):
        gacc[n:n + 1, :] = jnp.sum(grams[n], axis=0, keepdims=True)
    for v in range(2):
        gacc[pl.ds(36 + 2 * x + v, 1), :] = jnp.sum(ssq[v], axis=0, keepdims=True)
    ones8 = jnp.ones((8, 128), F32)
    ar[...] = lax.dot_general(ones8, gacc[...], (((1,), (1,)), ((), ())), precision=HI, preferred_element_type=F32)

    def exchange(src, buf, me, first, dev, meanwhile):
        buf[me] = src[...]
        cps = []
        for d in range(1, 16):
            b_, x_ = dev(d)
            cp = rcopy(src, buf.at[me], as_s.at[first + d - 1], as_r.at[first + d - 1], b_, x_)
            cp.start()
            cps.append(cp)
        meanwhile()
        for cp in cps:
            cp.wait_recv()
        drain.extend(cps)
        tot = [buf[j] for j in range(16)]
        while len(tot) > 1:
            tot = [a + b_ for a, b_ in zip(tot[::2], tot[1::2])]
        return tot[0]

    def copies2(act):
        n = 0
        for src in range(NX):
            for to in range(src + 1, NX):
                act(n, src, to, lambda: rcopy(cb.at[src], cb2.at[src], cs2_s.at[n], cs2_r.at[n], blk, jnp.int32(to)))
                n += 1

    def start2(n, src, to, cp):
        @pl.when(x == src)
        def _():
            cp().start()

    def rest():
        copies2(start2)

        @pl.when(x == LATE[0][0])
        def _():
            move(0).wait_recv()
        moves(LATE)

    ar2[...] = exchange(ar, arx, z * NC + c, 0, zc, rest)
    ar3 = exchange(ar2, ary, (rho // NC) * NX + x, 15, yx, lambda: None)

    r48 = lax.broadcasted_iota(jnp.int32, (48, 128), 0)
    l48 = lax.broadcasted_iota(jnp.int32, (48, 128), 1)
    spread = jnp.where(r48 == l48, jnp.broadcast_to(ar3[0:1, :], (48, 128)), 0.0)
    spl[...] = jnp.dot(spread, jnp.ones((128, 128), F32), precision=HI, preferred_element_type=F32)

    def entry(n):
        return spl[n:n + 1, :]

    s = [1.0 / (SCALE * jnp.sqrt(entry(36 + v) + EPS)) for v in range(8)]
    low = {}
    inv = []
    for j in range(8):
        a = entry(pair(j, j)) * s[j] * s[j]
        for k in range(j):
            a = a - low[j, k] * low[j, k]
        inv.append(lax.rsqrt(a))
        low[j, j] = a * inv[j]
        for i in range(j + 1, 8):
            a = entry(pair(i, j)) * s[i] * s[j]
            for k in range(j):
                a = a - low[i, k] * low[j, k]
            low[i, j] = a * inv[j]
    xx = {}
    for j in range(8):
        xx[j, j] = inv[j]
        for i in range(j + 1, 8):
            a = low[i, j] * xx[j, j]
            for k in range(j + 1, i):
                a = a + low[i, k] * xx[k, j]
            xx[i, j] = -a * inv[i]
    upper = zero8
    for i in range(8):
        for j in range(i + 1):
            mix[pair(i, j)] = jnp.broadcast_to(xx[i, j] * s[j], (8, 128))
            upper = jnp.where(jnp.logical_and(iota8 == j, lane8 == i), jnp.broadcast_to(low[i, j], (8, 128)), upper)
    fac[...] = upper[:, 0:8]

    def combine_at(g):
        for n in range(len(MOVES)):
            if MOVES[n][3] == g and (g, MOVES[n]) != (3, MOVES[0]):
                move(n).wait_recv()

        def wait2(n, src, to, cp):
            if to == g:
                cp().wait_recv()

        copies2(wait2)
        odd_row = (iota8 & 1) == 1
        for q in range(4):
            def combine(f, _, q=q):
                b, k = q // 2, q % 2
                last = rows[b] - 1
                fixes = []
                for v in range(2):
                    tot = zero8
                    for src in range(g + 1):
                        lo = mix[pair(2 * g + v, 2 * src)]
                        hi = mix[pair(2 * g + v, 2 * src + 1)] if 2 * src + 1 <= 2 * g + v else 0.0
                        rowsum = cb2[src, q, f] if src < g else cb[g, q, f]
                        tot = tot + jnp.where(odd_row, hi, lo) * rowsum
                    tot = tot + pltpu.roll(tot, 7, 0)
                    fixes.append([jnp.broadcast_to(tot[r:r + 1], (8, 128)) for r in (0, 2, 4, 6)])
                for t in range(8):
                    vals = [gath[w // 2, q, w % 2, f, 8 * t:8 * t + 8, :] for w in range(2 * g + 2)]
                    row = iota8 + 8 * t
                    for v in range(2):
                        a = mix[pair(2 * g + v, 0)] * vals[0]
                        for w in range(1, 2 * g + v + 1):
                            a = a + mix[pair(2 * g + v, w)] * vals[w]
                        if t == 0:
                            a = a + jnp.where(row == 0, fixes[v][0], 0.0) + jnp.where(row == 1, fixes[v][2], 0.0)
                        if t >= 3:
                            a = a + jnp.where(row == last, fixes[v][1], 0.0) + jnp.where(row == last - 1, fixes[v][3], 0.0)
                        bas[v, b, f, k, 8 * t:8 * t + 8, :] = a
                return 0

            lax.fori_loop(0, NF, combine, 0)
            for v in range(2):
                pltpu.make_async_copy(bas.at[v, q // 2, :, q % 2], out.at[v, q // 2, :, q % 2], out_sem.at[v, q]).start()

    for g in range(NX):
        @pl.when(x == g)
        def _():
            combine_at(g)

    for cp in drain:
        cp.wait_send()
    for n in range(len(MOVES)):
        @pl.when(x == MOVES[n][0])
        def _():
            move(n).wait_send()

    def drain2(n, src, to, cp):
        @pl.when(x == src)
        def _():
            cp().wait_send()

    copies2(drain2)
    for v in range(2):
        for q in range(4):
            pltpu.make_async_copy(bas.at[v, q // 2, :, q % 2], out.at[v, q // 2, :, q % 2], out_sem.at[v, q]).wait()


def per_device(vectors, metric, jacobians, block_rows, neighbours, flipped):
    vm = pl.BlockSpec(memory_space=pltpu.VMEM)
    hbm = pl.BlockSpec(memory_space=pltpu.HBM)
    dma = pltpu.SemaphoreType.DMA
    return pl.pallas_call(
        kernel,
        out_shape=(jax.ShapeDtypeStruct(vectors.shape, F32), jax.ShapeDtypeStruct((8, 8), F32)),
        in_specs=[hbm] * 6,
        out_specs=(pl.BlockSpec(memory_space=pl.ANY), vm),
        scratch_shapes=[
            pltpu.VMEM(vectors.shape, F32),
            pltpu.VMEM(metric.shape, F32),
            pltpu.SMEM((NF, 3, NF), F32),
            pltpu.SMEM((2,), jnp.int32),
            pltpu.SMEM((2, 2), jnp.int32),
            pltpu.SMEM((2, 2), jnp.int32),
            pltpu.VMEM((2, 2, NF, 2, 80, 128), F32),
            pltpu.VMEM((2, 2, NF, 2, 80, 128), F32),
            pltpu.VMEM((4, 4, 2, NF, 64, 128), F32),
            pltpu.VMEM(vectors.shape, F32),
            pltpu.VMEM((2, 4, 24, 128), F32),
            pltpu.VMEM((NZ, NC, 4, 24, 128), F32),
            pltpu.VMEM((NR, 8, 128), jnp.int32),
            pltpu.SMEM((NR, 8, 128), jnp.int32),
            pltpu.VMEM((NR, 4, 24, 128), F32),
            pltpu.VMEM((NR, 4, 24, 128), F32),
            pltpu.VMEM((12, 16, 128), F32),
            pltpu.VMEM((12, 16, 128), F32),
            pltpu.VMEM((4, 4, NF, 8, 128), F32),
            pltpu.VMEM((4, 4, NF, 8, 128), F32),
            pltpu.VMEM((128, 128), F32),
            pltpu.VMEM((8, 128), F32),
            pltpu.VMEM((8, 128), F32),
            pltpu.VMEM((16, 8, 128), F32),
            pltpu.VMEM((16, 8, 128), F32),
            pltpu.VMEM((48, 128), F32),
            pltpu.VMEM((36, 8, 128), F32),
            dma((2,)), dma((5,)), dma((4,)),
            dma((2, 3)), dma((2, 3)),
            dma((17,)), dma((17,)),
            dma((7,)), dma((7,)),
            dma((7,)), dma((7,)),
            dma((3,)), dma((3,)),
            dma((30,)), dma((30,)),
            dma((len(MOVES),)), dma((len(MOVES),)),
            dma((6,)), dma((6,)),
            dma((2, 4)),
        ],
        compiler_params=pltpu.CompilerParams(collective_id=0, has_side_effects=True, vmem_limit_bytes=62 * 1024 * 1024),
        cost_estimate=pl.CostEstimate(flops=60_000_000, bytes_accessed=4_000_000, transcendentals=0),
    )(vectors, metric, jnp.transpose(jacobians, (1, 0, 2)), block_rows, neighbours, flipped)


def solution(mesh):
    wide = P("vec", "blk", None, None, None, None)
    in_specs = (wide, P("blk", None, None, None), P(), P("blk"), P("blk", None), P("blk", None))
    return jax.shard_map(per_device, mesh=mesh, in_specs=in_specs, out_specs=(wide, P()), check_vma=False)
```

```python
import jax
import jax.numpy as jnp
from jax import lax
from jax.experimental import pallas as pl
from jax.experimental.pallas import tpu as pltpu
from jax.sharding import PartitionSpec as P

MESH = pl.DeviceIdType.MESH
F32 = jnp.float32
HI = lax.Precision.HIGHEST
NF = 5
NZ, NY, NC, NX = 8, 4, 2, 4
NR = NY * NC
VISC = 0.1
EPS = 1e-06
SCALE = 1024.0


EARLY = [(1, 0, 2), (0, 3, 1), (0, 1, 3), (2, 1, 3)]
LATE = [(0, 0, 2), (1, 1, 3)]
MOVES = EARLY + LATE


def pair(v, w):
    return v * (v + 1) // 2 + w


def kernel(vec_h, met_h, jac_h, rows_h, nbr_h, flip_h, out, fac,
           vec, met, jac, rows, nbr, flip, st, fi, gath, bas, res, pay, zb, rq, rqs, o2, rb, own, gst, cb, gacc, ar, ar2, arx, ary, spl, mix,
           loc_sem, in_sem, vec_sem, xs, xr, zs, zr, qs, qr, ys, yr, cs_s, cs_r, as_s, as_r, ws, wr, cs2_s, cs2_r, os, orr, out_sem):
    blk = lax.axis_index("blk")
    x = lax.axis_index("vec")
    z = blk // NR
    rho = lax.rem(blk, NR)
    c = lax.rem(blk, NC)
    col = lax.rem(blk, NR)

    def zdev(dz, core):
        zz = lax.rem(z + dz + NZ, NZ)
        return zz * NR + (rho - c) + core

    small = [pltpu.make_async_copy(h, d, in_sem.at[n]) for n, (h, d) in enumerate(
        ((rows_h, rows), (jac_h, jac), (nbr_h, nbr), (flip_h, flip), (met_h, met)))]
    big = [pltpu.make_async_copy(vec_h.at[n // 2, n % 2], vec.at[n // 2, n % 2], vec_sem.at[n]) for n in range(4)]
    for cp in small[:1] + big + small[1:]:
        cp.start()

    bar = pltpu.get_barrier_semaphore()
    def xdev(d):
        return lax.rem(x + d + NX, NX)

    def zc(d):
        m = lax.rem(z * NC + c + d, NZ * NC)
        return (m // NC) * NR + (rho - c) + lax.rem(m, NC), x

    def yx(d):
        m = lax.rem((rho // NC) * NX + x + d, (NR // NC) * NX)
        return z * NR + (m // NX) * NC + c, lax.rem(m, NX)

    def yc(d):
        return z * NR + lax.rem(rho + d, NR), x

    partners = [(zdev(dz, core), x) for dz in (1, -1) for core in range(2)] + [yc(d) for d in range(1, NR)]
    partners += [(blk, xdev(d)) for d in range(1, NX)]
    for b_, x_ in partners:
        pl.semaphore_signal(bar, inc=1, device_id={"blk": b_, "vec": x_}, device_id_type=MESH)
    n_part = len(partners)

    def rcopy(src, dst, ssem, rsem, b_, x_):
        return pltpu.make_async_remote_copy(src_ref=src, dst_ref=dst, send_sem=ssem, recv_sem=rsem,
                                            device_id={"blk": b_, "vec": x_}, device_id_type=MESH)

    iota64 = lax.broadcasted_iota(jnp.int32, (64, 128), 0)
    iota8 = lax.broadcasted_iota(jnp.int32, (8, 128), 0)
    lane8 = lax.broadcasted_iota(jnp.int32, (8, 128), 1)
    zero8 = jnp.zeros((8, 128), F32)

    def fill(i, _):
        vb = i // 10
        v, b = vb // 2, lax.rem(vb, 2)
        fk = lax.rem(i, 10)
        f, k = fk // 2, lax.rem(fk, 2)
        q = vec[v, b, f, k]
        st[v, b, f, k, 8:72, :] = jnp.where(iota64 < rows[b], q, 0.0)
        st[v, b, f, k, 0:8, :] = zero8
        st[v, b, f, k, 72:80, :] = zero8
        fi[v, b, f, k, 0:8, :] = zero8
        fi[v, b, f, k, 72:80, :] = zero8
        return 0

    small[0].wait()
    for n in range(4):
        big[n].wait()
        lax.fori_loop(10 * n, 10 * n + 10, fill, 0)
    for cp in small[1:]:
        cp.wait()

    def advance_tile(src, v, b, t, scale, store):
        r0 = pl.multiple_of(t * 8, 8)
        alive = (iota8 + r0) < rows[b]
        qs_, d0, d1, base = [], [], [], []
        for k in range(2):
            qk = [src[v, b, f, k, pl.ds(r0 + 8, 8), :] for f in range(NF)]
            qs_.append(qk)
        for k in range(2):
            a0, a1, ab = [], [], []
            for f in range(NF):
                q = qs_[k][f]
                e = pltpu.roll(q, 127, 1)
                w = pltpu.roll(q, 1, 1)
                n = src[v, b, f, k, pl.ds(r0 + 9, 8), :]
                s = src[v, b, f, k, pl.ds(r0 + 7, 8), :]
                a0.append(e - w)
                a1.append(n - s)
                ab.append((scale * (1.0 - 6.0 * VISC)) * q + (scale * VISC) * ((e + w) + (n + s) + qs_[1 - k][f]))
            d0.append(a0)
            d1.append(a1)
            base.append(ab)
        mk = [met[b, k, pl.ds(r0, 8), :] * scale for k in range(2)]
        for f in range(NF):
            c0 = [jac[f, 0, g] for g in range(NF)]
            c1 = [jac[f, 1, g] for g in range(NF)]
            c2 = [jac[f, 2, g] for g in range(NF)]
            for k in range(2):
                acc = c0[0] * d0[k][0] + c1[0] * d1[k][0]
                oth = c2[0] * qs_[1 - k][0]
                for g in range(1, NF):
                    acc = acc + c0[g] * d0[k][g] + c1[g] * d1[k][g]
                    oth = oth + c2[g] * qs_[1 - k][g]
                flux = acc + oth if k == 0 else acc - oth
                store(f, k, jnp.where(alive, base[k][f] - mk[k] * flux, 0.0))

    def first_pass(i, sums):
        vb, t = i // 8, lax.rem(i, 8)
        v, b = vb // 2, lax.rem(vb, 2)
        r0 = t * 8
        row = iota8 + r0
        inner = jnp.logical_and(row > 0, row != rows[b] - 1)
        box = [jnp.zeros((8, 128), F32)]

        def store(f, k, val):
            fi[v, b, f, k, pl.ds(pl.multiple_of(r0 + 8, 8), 8), :] = val
            box[0] = box[0] + val * val

        advance_tile(st, v, b, t, 1.0, store)
        sq = jnp.where(inner, box[0], 0.0)
        s0, s1 = sums
        return s0 + jnp.where(v == 0, sq, 0.0), s1 + jnp.where(v == 1, sq, 0.0)

    ssq = lax.fori_loop(0, 32, first_pass, (zero8, zero8))

    def faces(i, _):
        b, side, v = i // 4, lax.rem(i // 2, 2), lax.rem(i, 2)
        last = jnp.maximum(rows[b] - 1, 1)
        r = jnp.where(side == 0, 0, last)
        adj = jnp.where(side == 0, 1, last - 1)
        slot = b * 2 + side
        lane_row = b * 8 + side * 2 + v
        for f in range(NF):
            for k in range(2):
                a = st[v, b, f, k, pl.ds(r + 8, 1), :]
                p = fi[v, b, f, k, pl.ds(r + 8, 1), :]
                pay[v, slot, f * 2 + k:f * 2 + k + 1, :] = a
                pay[v, slot, 10 + f * 2 + k:11 + f * 2 + k, :] = p
                own[f, pl.ds(lane_row + 4 * k, 1), :] = a
                own[NF + f, pl.ds(lane_row + 4 * k, 1), :] = p
        for k in range(2):
            m = met[b, k, pl.ds(r, 1), :]
            pay[v, slot, 20 + k:21 + k, :] = m
            pay[v, slot, 22 + k:23 + k, :] = m
            own[10, pl.ds(lane_row + 4 * k, 1), :] = m
            own[11, pl.ds(lane_row + 4 * k, 1), :] = met[b, k, pl.ds(adj, 1), :]
        return 0

    lax.fori_loop(0, 8, faces, 0)
    req = jnp.where(lane8 == 0, nbr[0, 0], jnp.where(lane8 == 1, nbr[0, 1], jnp.where(lane8 == 2, nbr[1, 0], nbr[1, 1])))
    rq[rho] = req

    pl.semaphore_wait(bar, n_part)

    mine = pltpu.make_async_copy(pay.at[c], zb.at[z, c], loc_sem.at[0])
    mine.start()
    z_copies = []
    for j in range(2):
        core = lax.rem(c + j, NC)
        for side, dz in ((0, 1), (1, -1)):
            n = j * 2 + side
            cp = rcopy(pay.at[core], zb.at[z, c], zs.at[n], zr.at[n], zdev(dz, core), x)
            cp.start()
            z_copies.append(cp)
    other = rcopy(pay.at[1 - c], zb.at[z, c], zs.at[4], zr.at[4], zdev(0, 1 - c), x)
    other.start()
    q_copies = []
    for d in range(1, NR):
        cp = rcopy(rq.at[rho], rq.at[rho], qs.at[d - 1], qr.at[d - 1], z * NR + lax.rem(rho + d, NR), x)
        cp.start()
        q_copies.append(cp)

    def second_pass(v):
        def body(i, _):
            b, t = i // 8, lax.rem(i, 8)

            def store(f, k, val):
                gath[x, b * 2 + k, v, f, pl.ds(pl.multiple_of(t * 8, 8), 8), :] = val

            advance_tile(fi, v, b, t, SCALE, store)
            return 0

        lax.fori_loop(0, 16, body, 0)

    sends = []

    def send_second(v):
        for d in (2, 1, 3):
            here = gath.at[x, xdev(d), v]
            cp = rcopy(here, here, xs.at[v, d - 1], xr.at[v, d - 1], blk, xdev(d))
            cp.start()
            sends.append(cp)

    def move(n):
        src, q, to = MOVES[n]
        part = gath.at[src, q]
        return rcopy(part, part, ws.at[n], wr.at[n], blk, jnp.int32(to))

    def fix_move(n):
        src, q, to = MOVES[n]
        part = cb.at[src, q]
        return rcopy(part, part, cs2_s.at[n], cs2_r.at[n], blk, jnp.int32(to))

    def moves(make, which):
        for n in range(len(MOVES)):
            if MOVES[n] in which:
                @pl.when(x == MOVES[n][0])
                def _():
                    make(n).start()

    second_pass(0)
    send_second(0)

    drain = z_copies + [other]

    def ring_step(s, before):
        cps = []
        for j in range(2):
            core = lax.rem(c + j, NC)
            for side, dz in ((0, 1), (1, -1)):
                if s == 3 and side != j:
                    before[j * 2 + side].wait_recv()
                    continue
                n = 5 + (s - 1) * 4 + j * 2 + side
                slot = lax.rem(z - dz * s + NZ, NZ)
                part = zb.at[slot, core]
                before[j * 2 + side].wait_recv()
                cp = rcopy(part, part, zs.at[n], zr.at[n], zdev(dz, c), x)
                cp.start()
                cps.append(cp)
        drain.extend(cps)
        return cps

    ring1 = ring_step(1, z_copies)
    second_pass(1)
    send_second(1)
    moves(move, EARLY)
    ring2 = ring_step(2, ring1)
    for cp in q_copies:
        cp.wait_recv()
    tosmem = pltpu.make_async_copy(rq, rqs, loc_sem.at[1])
    tosmem.start()
    ring3 = ring_step(3, ring2)
    mine.wait()
    other.wait_recv()
    tosmem.wait()
    for cp in ring3:
        cp.wait_recv()

    def pick(i, _):
        to, r = i // 4, lax.rem(i, 4)
        bid = rqs[to, 0, r]
        side = lax.rem(r, 2)
        o2[to, r] = zb[bid >> 4, (bid >> 1) & 1, (bid & 1) * 2 + (1 - side)]
        return 0

    lax.fori_loop(0, 4 * NR, pick, 0)
    y_copies = []
    for d in range(1, NR):
        to = lax.rem(rho + d, NR)
        cp = rcopy(o2.at[to], rb.at[rho], ys.at[d - 1], yr.at[d - 1], z * NR + to, x)
        cp.start()
        y_copies.append(cp)
    rb[rho] = o2[rho]
    for cp in y_copies:
        cp.wait_recv()
    drain += y_copies + q_copies

    rev = 127 - lane8

    def unpack(i, _):
        b, side, v = i // 4, lax.rem(i // 2, 2), lax.rem(i, 2)
        r = b * 2 + side
        bid = nbr[b, side]
        f_ = flip[b, side]
        lane_row = b * 8 + side * 2 + v
        src = ((bid >> 2) & 3) * 2 + v
        for h in range(3):
            q = rb[src, r, 8 * h:8 * h + 8, :]
            turned = jnp.take_along_axis(q, rev, axis=1)
            rowh = iota8 + 8 * h
            neg = jnp.logical_or(jnp.logical_or(rowh == 2, rowh == 3), jnp.logical_or(rowh == 12, rowh == 13))
            turned = jnp.where(neg, -turned, turned)
            q = jnp.where(f_ > 0, turned, q)
            for j in range(8):
                w = 8 * h + j
                if w >= 22:
                    continue
                item, k = (w // 2, w % 2)
                gst[item, pl.ds(lane_row + 4 * k, 1), :] = q[j:j + 1, :]
        sign = jnp.where(f_ > 0, -1.0, 1.0) + jnp.zeros((1, 128), F32)
        for k in range(2):
            gst[11, pl.ds(lane_row + 4 * k, 1), :] = sign
        return 0

    lax.fori_loop(0, 8, unpack, 0)

    sig = jnp.where((iota8 >> 1) & 1 == 0, -1.0, 1.0)
    sk = jnp.where(iota8 < 4, 1.0, -1.0)
    odd = iota8 & 1

    def jmul(d, g_, f):
        acc = jac[f, d, 0] * g_[0]
        for g in range(1, NF):
            acc = acc + jac[f, d, g] * g_[g]
        return acc

    def fix(b, sums):
        base = pl.ds(pl.multiple_of(b * 8, 8), 8)
        g0 = [gst[f, base, :] for f in range(NF)]
        gf = [gst[NF + f, base, :] for f in range(NF)]
        gm = gst[10, base, :]
        turn = gst[11, base, :]
        o = [own[f, base, :] for f in range(NF)]
        of = [own[NF + f, base, :] for f in range(NF)]
        m0 = own[10, base, :]
        m1 = own[11, base, :]
        od = [o[f] * turn if f == 1 else o[f] for f in range(NF)]
        g1, c1 = [], []
        total = zero8
        for f in range(NF):
            tf = jmul(1, od, f)
            if f == 1:
                tf = tf * turn
            g1.append(gf[f] + VISC * o[f] + sig * gm * tf)
            cf = VISC * g0[f] - sig * m0 * jmul(1, g0, f)
            c1.append(cf)
            ff = of[f] + cf
            total = total + ff * ff
        e = [pltpu.roll(cf, 127, 1) for cf in c1]
        w = [pltpu.roll(cf, 1, 1) for cf in c1]
        ok = [pltpu.roll(cf, 4, 0) for cf in c1]
        ew = [a - b_ for a, b_ in zip(e, w)]
        for f in range(NF):
            flux = jmul(0, ew, f) + sk * jmul(2, ok, f) + sig * jmul(1, g1, f)
            face = (1.0 - 6.0 * VISC) * c1[f] + VISC * (e[f] + w[f] + ok[f] + g1[f]) - m0 * flux
            near = VISC * c1[f] - sig * m1 * jmul(1, c1, f)
            face = face * SCALE
            near = near * SCALE
            cb[x, b * 2, f, 0:4, :] = face[0:4]
            cb[x, b * 2, f, 4:8, :] = near[0:4]
            cb[x, b * 2 + 1, f, 0:4, :] = face[4:8]
            cb[x, b * 2 + 1, f, 4:8, :] = near[4:8]
        s0, s1 = sums
        return s0 + jnp.where(odd == 0, total, 0.0), s1 + jnp.where(odd == 1, total, 0.0)

    ssq = lax.fori_loop(0, 2, fix, ssq)
    c_copies = []
    for d in (2, 1, 3):
        here = cb.at[x, xdev(d)]
        cp = rcopy(here, here, cs_s.at[d - 1], cs_r.at[d - 1], blk, xdev(d))
        cp.start()
        c_copies.append(cp)
    moves(fix_move, MOVES)
    moves(move, LATE)
    for cp in sends:
        cp.wait_recv()

    for cp in c_copies:
        cp.wait_recv()
    drain += sends + c_copies

    bq = x // 2
    my_last = jnp.where(bq == 0, rows[0], rows[1]) - 1

    def gram_tile(i, acc):
        f, t = i // 8, lax.rem(i, 8)
        row = iota8 + t * 8
        at = [row == 0, row == my_last, row == 1, row == my_last - 1]
        vals = []
        for v in range(8):
            q = gath[v // 2, x, v % 2, f, pl.ds(pl.multiple_of(t * 8, 8), 8), :]
            for n, (typ, side) in enumerate(((0, 0), (0, 1), (1, 0), (1, 1))):
                w = typ * 4 + side * 2 + v % 2
                q = q + jnp.where(at[n], jnp.broadcast_to(cb[v // 2, x, f, w:w + 1, :], (8, 128)), 0.0)
            vals.append(q)
        res = list(acc)
        for v in range(8):
            for w in range(v + 1):
                res[pair(v, w)] = res[pair(v, w)] + vals[v] * vals[w]
        return tuple(res)

    grams = lax.fori_loop(0, 40, gram_tile, tuple(zero8 for _ in range(36)))
    gacc[...] = jnp.zeros((128, 128), F32)
    for n in range(36):
        gacc[n:n + 1, :] = jnp.sum(grams[n], axis=0, keepdims=True)
    for v in range(2):
        gacc[pl.ds(36 + 2 * x + v, 1), :] = jnp.sum(ssq[v], axis=0, keepdims=True)
    ones8 = jnp.ones((8, 128), F32)
    ar[...] = lax.dot_general(ones8, gacc[...], (((1,), (1,)), ((), ())), precision=HI, preferred_element_type=F32)

    def exchange(src, buf, me, first, dev):
        buf[me] = src[...]
        cps = []
        for d in range(1, 16):
            b_, x_ = dev(d)
            cp = rcopy(src, buf.at[me], as_s.at[first + d - 1], as_r.at[first + d - 1], b_, x_)
            cp.start()
            cps.append(cp)
        for cp in cps:
            cp.wait_recv()
        drain.extend(cps)
        tot = [buf[j] for j in range(16)]
        while len(tot) > 1:
            tot = [a + b_ for a, b_ in zip(tot[::2], tot[1::2])]
        return tot[0]

    ar2[...] = exchange(ar, arx, z * NC + c, 0, zc)
    ar3 = exchange(ar2, ary, (rho // NC) * NX + x, 15, yx)

    r48 = lax.broadcasted_iota(jnp.int32, (48, 128), 0)
    l48 = lax.broadcasted_iota(jnp.int32, (48, 128), 1)
    spread = jnp.where(r48 == l48, jnp.broadcast_to(ar3[0:1, :], (48, 128)), 0.0)
    spl[...] = jnp.dot(spread, jnp.ones((128, 128), F32), precision=HI, preferred_element_type=F32)

    def entry(n):
        return spl[n:n + 1, :]

    s = [1.0 / (SCALE * jnp.sqrt(entry(36 + v) + EPS)) for v in range(8)]
    low = {}
    inv = []
    for j in range(8):
        a = entry(pair(j, j)) * s[j] * s[j]
        for k in range(j):
            a = a - low[j, k] * low[j, k]
        inv.append(lax.rsqrt(a))
        low[j, j] = a * inv[j]
        for i in range(j + 1, 8):
            a = entry(pair(i, j)) * s[i] * s[j]
            for k in range(j):
                a = a - low[i, k] * low[j, k]
            low[i, j] = a * inv[j]
    xx = {}
    for j in range(8):
        xx[j, j] = inv[j]
        for i in range(j + 1, 8):
            a = low[i, j] * xx[j, j]
            for k in range(j + 1, i):
                a = a + low[i, k] * xx[k, j]
            xx[i, j] = -a * inv[i]
    upper = zero8
    for i in range(8):
        for j in range(i + 1):
            mix[pair(i, j)] = jnp.broadcast_to(xx[i, j] * s[j], (8, 128))
            upper = jnp.where(jnp.logical_and(iota8 == j, lane8 == i), jnp.broadcast_to(low[i, j], (8, 128)), upper)
    fac[...] = upper[:, 0:8]

    odd_row = (iota8 & 1) == 1

    def combine(q, outs, put):
        top = max(outs) // 2 + 1

        def body(f, _):
            last = rows[q // 2] - 1
            fixes = []
            for o in outs:
                tot = zero8
                for src in range(o // 2 + 1):
                    lo = mix[pair(o, 2 * src)]
                    hi = mix[pair(o, 2 * src + 1)] if 2 * src + 1 <= o else 0.0
                    tot = tot + jnp.where(odd_row, hi, lo) * cb[src, q, f]
                tot = tot + pltpu.roll(tot, 7, 0)
                fixes.append([jnp.broadcast_to(tot[r:r + 1], (8, 128)) for r in (0, 2, 4, 6)])
            for t in range(8):
                vals = [gath[w // 2, q, w % 2, f, 8 * t:8 * t + 8, :] for w in range(2 * top)]
                row = iota8 + 8 * t
                for n, o in enumerate(outs):
                    a = mix[pair(o, 0)] * vals[0]
                    for w in range(1, o + 1):
                        a = a + mix[pair(o, w)] * vals[w]
                    if t == 0:
                        a = a + jnp.where(row == 0, fixes[n][0], 0.0) + jnp.where(row == 1, fixes[n][2], 0.0)
                    if t >= 3:
                        a = a + jnp.where(row == last, fixes[n][1], 0.0) + jnp.where(row == last - 1, fixes[n][3], 0.0)
                    put(n, f, t, a)
            return 0

        lax.fori_loop(0, NF, body, 0)

    def home(i, v, q, to):
        return rcopy(res.at[i, v], out.at[v, q // 2, :, q % 2], os.at[i, v], orr.at[i, v], blk, jnp.int32(to))

    def own_copy(v, q):
        there = out.at[v, q // 2, :, q % 2]
        return pltpu.make_async_copy(bas.at[v, q // 2, :, q % 2], there, out_sem.at[v, q])

    def finish(g):
        beside = [(i, (g + d) % NX) for i, d in ((0, 1), (1, -1)) if (g + d) % NX > 0]
        for i, to in beside:
            def put(n, f, t, a, i=i):
                res[i, n, f, 8 * t:8 * t + 8, :] = a

            combine(g, [2 * to, 2 * to + 1], put)
            for v in range(2):
                home(i, v, g, to).start()
        mine_q = [g, (g + 2) % NX] if g > 0 else [0, 1, 2, 3]
        for q in mine_q:
            if q != g:
                for n in range(len(MOVES)):
                    if MOVES[n][1:] == (q, g):
                        move(n).wait_recv()
                        fix_move(n).wait_recv()

            def put_own(n, f, t, a, q=q):
                bas[n, q // 2, f, q % 2, 8 * t:8 * t + 8, :] = a

            combine(q, [2 * g, 2 * g + 1], put_own)
            for v in range(2):
                own_copy(v, q).start()
        for n in range(len(MOVES)):
            if MOVES[n][0] == g:
                move(n).wait_send()
                fix_move(n).wait_send()
        for q in mine_q:
            for v in range(2):
                own_copy(v, q).wait()
        for i, to in beside:
            for v in range(2):
                home(i, v, g, to).wait_send()
        if g > 0:
            for i, frm in ((0, (g - 1) % NX), (1, (g + 1) % NX)):
                for v in range(2):
                    home(i, v, frm, g).wait_recv()

    for cp in drain:
        cp.wait_send()
    for g in range(NX):
        @pl.when(x == g)
        def _():
            finish(g)


def per_device(vectors, metric, jacobians, block_rows, neighbours, flipped):
    vm = pl.BlockSpec(memory_space=pltpu.VMEM)
    hbm = pl.BlockSpec(memory_space=pltpu.HBM)
    dma = pltpu.SemaphoreType.DMA
    return pl.pallas_call(
        kernel,
        out_shape=(jax.ShapeDtypeStruct(vectors.shape, F32), jax.ShapeDtypeStruct((8, 8), F32)),
        in_specs=[hbm] * 6,
        out_specs=(pl.BlockSpec(memory_space=pl.ANY), vm),
        scratch_shapes=[
            pltpu.VMEM(vectors.shape, F32),
            pltpu.VMEM(metric.shape, F32),
            pltpu.SMEM((NF, 3, NF), F32),
            pltpu.SMEM((2,), jnp.int32),
            pltpu.SMEM((2, 2), jnp.int32),
            pltpu.SMEM((2, 2), jnp.int32),
            pltpu.VMEM((2, 2, NF, 2, 80, 128), F32),
            pltpu.VMEM((2, 2, NF, 2, 80, 128), F32),
            pltpu.VMEM((4, 4, 2, NF, 64, 128), F32),
            pltpu.VMEM(vectors.shape, F32),
            pltpu.VMEM((2, 2, NF, 64, 128), F32),
            pltpu.VMEM((2, 4, 24, 128), F32),
            pltpu.VMEM((NZ, NC, 4, 24, 128), F32),
            pltpu.VMEM((NR, 8, 128), jnp.int32),
            pltpu.SMEM((NR, 8, 128), jnp.int32),
            pltpu.VMEM((NR, 4, 24, 128), F32),
            pltpu.VMEM((NR, 4, 24, 128), F32),
            pltpu.VMEM((12, 16, 128), F32),
            pltpu.VMEM((12, 16, 128), F32),
            pltpu.VMEM((4, 4, NF, 8, 128), F32),
            pltpu.VMEM((128, 128), F32),
            pltpu.VMEM((8, 128), F32),
            pltpu.VMEM((8, 128), F32),
            pltpu.VMEM((16, 8, 128), F32),
            pltpu.VMEM((16, 8, 128), F32),
            pltpu.VMEM((48, 128), F32),
            pltpu.VMEM((36, 8, 128), F32),
            dma((2,)), dma((5,)), dma((4,)),
            dma((2, 3)), dma((2, 3)),
            dma((17,)), dma((17,)),
            dma((7,)), dma((7,)),
            dma((7,)), dma((7,)),
            dma((3,)), dma((3,)),
            dma((30,)), dma((30,)),
            dma((len(MOVES),)), dma((len(MOVES),)),
            dma((6,)), dma((6,)),
            dma((2, 2)), dma((2, 2)),
            dma((2, 4)),
        ],
        compiler_params=pltpu.CompilerParams(collective_id=0, has_side_effects=True, vmem_limit_bytes=62 * 1024 * 1024),
        cost_estimate=pl.CostEstimate(flops=60_000_000, bytes_accessed=4_000_000, transcendentals=0),
    )(vectors, metric, jnp.transpose(jacobians, (1, 0, 2)), block_rows, neighbours, flipped)


def solution(mesh):
    wide = P("vec", "blk", None, None, None, None)
    in_specs = (wide, P("blk", None, None, None), P(), P("blk"), P("blk", None), P("blk", None))
    return jax.shard_map(per_device, mesh=mesh, in_specs=in_specs, out_specs=(wide, P()), check_vma=False)
```

```python
import jax
import jax.numpy as jnp
from jax import lax
from jax.experimental import pallas as pl
from jax.experimental.pallas import tpu as pltpu
from jax.sharding import PartitionSpec as P

MESH = pl.DeviceIdType.MESH
F32 = jnp.float32
HI = lax.Precision.HIGHEST
NF = 5
NZ, NY, NC, NX = 8, 4, 2, 4
NR = NY * NC
VISC = 0.1
EPS = 1e-06
SCALE = 1024.0


EARLY = [(1, 0, 2), (0, 3, 1), (0, 1, 3), (2, 1, 3)]
LATE = [(0, 0, 2), (1, 1, 3)]
MOVES = EARLY + LATE


def pair(v, w):
    return v * (v + 1) // 2 + w


def kernel(vec_h, met_h, jac_h, rows_h, nbr_h, flip_h, out, fac,
           vec, met, jac, rows, nbr, flip, st, fi, gath, bas, res, pay, zb, rq, rqs, o2, rb, own, gst, cb, gacc, ar, ar2, arx, ary, spl, mix,
           loc_sem, in_sem, vec_sem, xs, xr, zs, zr, qs, qr, ys, yr, cs_s, cs_r, as_s, as_r, ws, wr, cs2_s, cs2_r, os, orr, out_sem):
    blk = lax.axis_index("blk")
    x = lax.axis_index("vec")
    z = blk // NR
    rho = lax.rem(blk, NR)
    c = lax.rem(blk, NC)
    col = lax.rem(blk, NR)

    def zdev(dz, core):
        zz = lax.rem(z + dz + NZ, NZ)
        return zz * NR + (rho - c) + core

    small = [pltpu.make_async_copy(h, d, in_sem.at[n]) for n, (h, d) in enumerate(
        ((rows_h, rows), (jac_h, jac), (nbr_h, nbr), (flip_h, flip), (met_h, met)))]
    big = [pltpu.make_async_copy(vec_h.at[n // 2, n % 2], vec.at[n // 2, n % 2], vec_sem.at[n]) for n in range(4)]
    for cp in small[:1] + big + small[1:]:
        cp.start()

    bar = pltpu.get_barrier_semaphore()
    def xdev(d):
        return lax.rem(x + d + NX, NX)

    def zc(d):
        m = lax.rem(z * NC + c + d, NZ * NC)
        return (m // NC) * NR + (rho - c) + lax.rem(m, NC), x

    def yx(d):
        m = lax.rem((rho // NC) * NX + x + d, (NR // NC) * NX)
        return z * NR + (m // NX) * NC + c, lax.rem(m, NX)

    def yc(d):
        return z * NR + lax.rem(rho + d, NR), x

    partners = [(zdev(dz, core), x) for dz in (1, -1) for core in range(2)] + [yc(d) for d in range(1, NR)]
    partners += [(blk, xdev(d)) for d in range(1, NX)]
    for b_, x_ in partners:
        pl.semaphore_signal(bar, inc=1, device_id={"blk": b_, "vec": x_}, device_id_type=MESH)
    n_part = len(partners)

    def rcopy(src, dst, ssem, rsem, b_, x_):
        return pltpu.make_async_remote_copy(src_ref=src, dst_ref=dst, send_sem=ssem, recv_sem=rsem,
                                            device_id={"blk": b_, "vec": x_}, device_id_type=MESH)

    iota64 = lax.broadcasted_iota(jnp.int32, (64, 128), 0)
    iota8 = lax.broadcasted_iota(jnp.int32, (8, 128), 0)
    lane8 = lax.broadcasted_iota(jnp.int32, (8, 128), 1)
    zero8 = jnp.zeros((8, 128), F32)

    for cp in small + big:
        cp.wait()

    sig = jnp.where((iota8 >> 1) & 1 == 0, -1.0, 1.0)
    sk = jnp.where(iota8 < 4, 1.0, -1.0)
    odd = iota8 & 1

    def jmul(d, g_, f):
        acc = jac[f, d, 0] * g_[0]
        for g in range(1, NF):
            acc = acc + jac[f, d, g] * g_[g]
        return acc

    def faces(i, _):
        b, side, v = i // 4, lax.rem(i // 2, 2), lax.rem(i, 2)
        last = jnp.maximum(rows[b] - 1, 1)
        r = jnp.where(side == 0, 0, last)
        adj = jnp.where(side == 0, 1, last - 1)
        slot = b * 2 + side
        lane_row = b * 8 + side * 2 + v
        for f in range(NF):
            for k in range(2):
                a = vec[v, b, f, k, pl.ds(r, 1), :]
                pay[v, slot, f * 2 + k:f * 2 + k + 1, :] = a
                own[f, pl.ds(lane_row + 4 * k, 1), :] = a
                gst[f, pl.ds(lane_row + 4 * k, 1), :] = vec[v, b, f, k, pl.ds(adj, 1), :]
        for k in range(2):
            m = met[b, k, pl.ds(r, 1), :]
            pay[v, slot, 20 + k:21 + k, :] = m
            pay[v, slot, 22 + k:23 + k, :] = m
            own[10, pl.ds(lane_row + 4 * k, 1), :] = m
            own[11, pl.ds(lane_row + 4 * k, 1), :] = met[b, k, pl.ds(adj, 1), :]
        return 0

    lax.fori_loop(0, 8, faces, 0)

    def face_step(b, _):
        base = pl.ds(pl.multiple_of(b * 8, 8), 8)
        q = [own[f, base, :] for f in range(NF)]
        near = [gst[f, base, :] for f in range(NF)]
        m0 = own[10, base, :]
        e = [pltpu.roll(a, 127, 1) for a in q]
        w = [pltpu.roll(a, 1, 1) for a in q]
        ok = [pltpu.roll(a, 4, 0) for a in q]
        ew = [a - b_ for a, b_ in zip(e, w)]
        for f in range(NF):
            flux = jmul(0, ew, f) + sk * jmul(2, ok, f) - sig * jmul(1, near, f)
            own[NF + f, base, :] = (1.0 - 6.0 * VISC) * q[f] + VISC * (e[f] + w[f] + ok[f] + near[f]) - m0 * flux
        return 0

    lax.fori_loop(0, 2, face_step, 0)

    def pack(i, _):
        b, side, v = i // 4, lax.rem(i // 2, 2), lax.rem(i, 2)
        lane_row = b * 8 + side * 2 + v
        for f in range(NF):
            for k in range(2):
                pay[v, b * 2 + side, 10 + f * 2 + k:11 + f * 2 + k, :] = own[NF + f, pl.ds(lane_row + 4 * k, 1), :]
        return 0

    lax.fori_loop(0, 8, pack, 0)
    req = jnp.where(lane8 == 0, nbr[0, 0], jnp.where(lane8 == 1, nbr[0, 1], jnp.where(lane8 == 2, nbr[1, 0], nbr[1, 1])))
    rq[rho] = req

    pl.semaphore_wait(bar, n_part)

    mine = pltpu.make_async_copy(pay.at[c], zb.at[z, c], loc_sem.at[0])
    mine.start()
    z_copies = []
    for j in range(2):
        core = lax.rem(c + j, NC)
        for h in range(2):
            for side, dz in ((0, 1), (1, -1)):
                n = j * 4 + h * 2 + side
                half = pl.ds(2 * h, 2)
                cp = rcopy(pay.at[core, half], zb.at[z, c, half], zs.at[n], zr.at[n], zdev(dz, core), x)
                cp.start()
                z_copies.append(cp)
    other = rcopy(pay.at[1 - c], zb.at[z, c], zs.at[8], zr.at[8], zdev(0, 1 - c), x)
    other.start()
    q_copies = []
    for d in range(1, NR):
        cp = rcopy(rq.at[rho], rq.at[rho], qs.at[d - 1], qr.at[d - 1], z * NR + lax.rem(rho + d, NR), x)
        cp.start()
        q_copies.append(cp)

    def fill(i, _):
        vb = i // 10
        v, b = vb // 2, lax.rem(vb, 2)
        fk = lax.rem(i, 10)
        f, k = fk // 2, lax.rem(fk, 2)
        q = vec[v, b, f, k]
        st[v, b, f, k, 8:72, :] = jnp.where(iota64 < rows[b], q, 0.0)
        st[v, b, f, k, 0:8, :] = zero8
        st[v, b, f, k, 72:80, :] = zero8
        fi[v, b, f, k, 0:8, :] = zero8
        fi[v, b, f, k, 72:80, :] = zero8
        return 0

    lax.fori_loop(0, 40, fill, 0)

    def advance_tile(src, v, b, t, scale, store):
        r0 = pl.multiple_of(t * 8, 8)
        alive = (iota8 + r0) < rows[b]
        qs_, d0, d1, base = [], [], [], []
        for k in range(2):
            qk = [src[v, b, f, k, pl.ds(r0 + 8, 8), :] for f in range(NF)]
            qs_.append(qk)
        for k in range(2):
            a0, a1, ab = [], [], []
            for f in range(NF):
                q = qs_[k][f]
                e = pltpu.roll(q, 127, 1)
                w = pltpu.roll(q, 1, 1)
                n = src[v, b, f, k, pl.ds(r0 + 9, 8), :]
                s = src[v, b, f, k, pl.ds(r0 + 7, 8), :]
                a0.append(e - w)
                a1.append(n - s)
                ab.append((scale * (1.0 - 6.0 * VISC)) * q + (scale * VISC) * ((e + w) + (n + s) + qs_[1 - k][f]))
            d0.append(a0)
            d1.append(a1)
            base.append(ab)
        mk = [met[b, k, pl.ds(r0, 8), :] * scale for k in range(2)]
        for f in range(NF):
            c0 = [jac[f, 0, g] for g in range(NF)]
            c1 = [jac[f, 1, g] for g in range(NF)]
            c2 = [jac[f, 2, g] for g in range(NF)]
            for k in range(2):
                acc = c0[0] * d0[k][0] + c1[0] * d1[k][0]
                oth = c2[0] * qs_[1 - k][0]
                for g in range(1, NF):
                    acc = acc + c0[g] * d0[k][g] + c1[g] * d1[k][g]
                    oth = oth + c2[g] * qs_[1 - k][g]
                flux = acc + oth if k == 0 else acc - oth
                store(f, k, jnp.where(alive, base[k][f] - mk[k] * flux, 0.0))

    def first_pass(i, sums):
        vb, t = i // 8, lax.rem(i, 8)
        v, b = vb // 2, lax.rem(vb, 2)
        r0 = t * 8
        row = iota8 + r0
        inner = jnp.logical_and(row > 0, row != rows[b] - 1)
        box = [jnp.zeros((8, 128), F32)]

        def store(f, k, val):
            fi[v, b, f, k, pl.ds(pl.multiple_of(r0 + 8, 8), 8), :] = val
            box[0] = box[0] + val * val

        advance_tile(st, v, b, t, 1.0, store)
        sq = jnp.where(inner, box[0], 0.0)
        s0, s1 = sums
        return s0 + jnp.where(v == 0, sq, 0.0), s1 + jnp.where(v == 1, sq, 0.0)

    ssq = lax.fori_loop(0, 32, first_pass, (zero8, zero8))

    def second_pass(v):
        def body(i, _):
            b, t = i // 8, lax.rem(i, 8)

            def store(f, k, val):
                gath[x, b * 2 + k, v, f, pl.ds(pl.multiple_of(t * 8, 8), 8), :] = val

            advance_tile(fi, v, b, t, SCALE, store)
            return 0

        lax.fori_loop(0, 16, body, 0)

    sends = []

    def send_second(v):
        for d in (2, 1, 3):
            here = gath.at[x, xdev(d), v]
            cp = rcopy(here, here, xs.at[v, d - 1], xr.at[v, d - 1], blk, xdev(d))
            cp.start()
            sends.append(cp)

    def move(n):
        src, q, to = MOVES[n]
        part = gath.at[src, q]
        return rcopy(part, part, ws.at[n], wr.at[n], blk, jnp.int32(to))

    def fix_move(n):
        src, q, to = MOVES[n]
        part = cb.at[src, q]
        return rcopy(part, part, cs2_s.at[n], cs2_r.at[n], blk, jnp.int32(to))

    def moves(make, which):
        for n in range(len(MOVES)):
            if MOVES[n] in which:
                @pl.when(x == MOVES[n][0])
                def _():
                    make(n).start()

    drain = z_copies + [other]

    def ring_step(s, before):
        cps = []
        for j in range(2):
            core = lax.rem(c + j, NC)
            for h in range(2):
                for side, dz in ((0, 1), (1, -1)):
                    m = j * 4 + h * 2 + side
                    before[m].wait_recv()
                    if s == 3 and side != j:
                        continue
                    n = 9 + (s - 1) * 8 + m
                    part = zb.at[lax.rem(z - dz * s + NZ, NZ), core, pl.ds(2 * h, 2)]
                    cp = rcopy(part, part, zs.at[n], zr.at[n], zdev(dz, c), x)
                    cp.start()
                    cps.append(cp)
        drain.extend(cps)
        return cps

    ring1 = ring_step(1, z_copies)
    second_pass(0)
    send_second(0)

    second_pass(1)
    send_second(1)
    ring2 = ring_step(2, ring1)
    for cp in q_copies:
        cp.wait_recv()
    tosmem = pltpu.make_async_copy(rq, rqs, loc_sem.at[1])
    tosmem.start()
    ring3 = ring_step(3, ring2)
    mine.wait()
    other.wait_recv()
    tosmem.wait()
    for cp in ring3:
        cp.wait_recv()

    def pick(i, _):
        to, r = i // 4, lax.rem(i, 4)
        bid = rqs[to, 0, r]
        side = lax.rem(r, 2)
        o2[to, r] = zb[bid >> 4, (bid >> 1) & 1, (bid & 1) * 2 + (1 - side)]
        return 0

    lax.fori_loop(0, 4 * NR, pick, 0)
    y_copies = []
    for d in range(1, NR):
        to = lax.rem(rho + d, NR)
        cp = rcopy(o2.at[to], rb.at[rho], ys.at[d - 1], yr.at[d - 1], z * NR + to, x)
        cp.start()
        y_copies.append(cp)
    rb[rho] = o2[rho]
    for cp in y_copies:
        cp.wait_recv()
    drain += y_copies + q_copies

    rev = 127 - lane8

    def unpack(i, _):
        b, side, v = i // 4, lax.rem(i // 2, 2), lax.rem(i, 2)
        r = b * 2 + side
        bid = nbr[b, side]
        f_ = flip[b, side]
        lane_row = b * 8 + side * 2 + v
        src = ((bid >> 2) & 3) * 2 + v
        for h in range(3):
            q = rb[src, r, 8 * h:8 * h + 8, :]
            turned = jnp.take_along_axis(q, rev, axis=1)
            rowh = iota8 + 8 * h
            neg = jnp.logical_or(jnp.logical_or(rowh == 2, rowh == 3), jnp.logical_or(rowh == 12, rowh == 13))
            turned = jnp.where(neg, -turned, turned)
            q = jnp.where(f_ > 0, turned, q)
            for j in range(8):
                w = 8 * h + j
                if w >= 22:
                    continue
                item, k = (w // 2, w % 2)
                gst[item, pl.ds(lane_row + 4 * k, 1), :] = q[j:j + 1, :]
        sign = jnp.where(f_ > 0, -1.0, 1.0) + jnp.zeros((1, 128), F32)
        for k in range(2):
            gst[11, pl.ds(lane_row + 4 * k, 1), :] = sign
        return 0

    lax.fori_loop(0, 8, unpack, 0)

    def fix(b, sums):
        base = pl.ds(pl.multiple_of(b * 8, 8), 8)
        g0 = [gst[f, base, :] for f in range(NF)]
        gf = [gst[NF + f, base, :] for f in range(NF)]
        gm = gst[10, base, :]
        turn = gst[11, base, :]
        o = [own[f, base, :] for f in range(NF)]
        of = [own[NF + f, base, :] for f in range(NF)]
        m0 = own[10, base, :]
        m1 = own[11, base, :]
        od = [o[f] * turn if f == 1 else o[f] for f in range(NF)]
        g1, c1 = [], []
        total = zero8
        for f in range(NF):
            tf = jmul(1, od, f)
            if f == 1:
                tf = tf * turn
            g1.append(gf[f] + VISC * o[f] + sig * gm * tf)
            cf = VISC * g0[f] - sig * m0 * jmul(1, g0, f)
            c1.append(cf)
            ff = of[f] + cf
            total = total + ff * ff
        e = [pltpu.roll(cf, 127, 1) for cf in c1]
        w = [pltpu.roll(cf, 1, 1) for cf in c1]
        ok = [pltpu.roll(cf, 4, 0) for cf in c1]
        ew = [a - b_ for a, b_ in zip(e, w)]
        for f in range(NF):
            flux = jmul(0, ew, f) + sk * jmul(2, ok, f) + sig * jmul(1, g1, f)
            face = (1.0 - 6.0 * VISC) * c1[f] + VISC * (e[f] + w[f] + ok[f] + g1[f]) - m0 * flux
            near = VISC * c1[f] - sig * m1 * jmul(1, c1, f)
            face = face * SCALE
            near = near * SCALE
            cb[x, b * 2, f, 0:4, :] = face[0:4]
            cb[x, b * 2, f, 4:8, :] = near[0:4]
            cb[x, b * 2 + 1, f, 0:4, :] = face[4:8]
            cb[x, b * 2 + 1, f, 4:8, :] = near[4:8]
        s0, s1 = sums
        return s0 + jnp.where(odd == 0, total, 0.0), s1 + jnp.where(odd == 1, total, 0.0)

    ssq = lax.fori_loop(0, 2, fix, ssq)
    c_copies = []
    for d in (2, 1, 3):
        here = cb.at[x, xdev(d)]
        cp = rcopy(here, here, cs_s.at[d - 1], cs_r.at[d - 1], blk, xdev(d))
        cp.start()
        c_copies.append(cp)
    moves(fix_move, MOVES)
    moves(move, EARLY)
    for cp in sends:
        cp.wait_recv()

    for cp in c_copies:
        cp.wait_recv()
    drain += sends + c_copies

    bq = x // 2
    my_last = jnp.where(bq == 0, rows[0], rows[1]) - 1

    def gram_tile(i, acc):
        f, t = i // 8, lax.rem(i, 8)
        row = iota8 + t * 8
        at = [row == 0, row == my_last, row == 1, row == my_last - 1]
        vals = []
        for v in range(8):
            q = gath[v // 2, x, v % 2, f, pl.ds(pl.multiple_of(t * 8, 8), 8), :]
            for n, (typ, side) in enumerate(((0, 0), (0, 1), (1, 0), (1, 1))):
                w = typ * 4 + side * 2 + v % 2
                q = q + jnp.where(at[n], jnp.broadcast_to(cb[v // 2, x, f, w:w + 1, :], (8, 128)), 0.0)
            vals.append(q)
        res = list(acc)
        for v in range(8):
            for w in range(v + 1):
                res[pair(v, w)] = res[pair(v, w)] + vals[v] * vals[w]
        return tuple(res)

    grams = lax.fori_loop(0, 40, gram_tile, tuple(zero8 for _ in range(36)))
    gacc[...] = jnp.zeros((128, 128), F32)
    for n in range(36):
        gacc[n:n + 1, :] = jnp.sum(grams[n], axis=0, keepdims=True)
    for v in range(2):
        gacc[pl.ds(36 + 2 * x + v, 1), :] = jnp.sum(ssq[v], axis=0, keepdims=True)
    ones8 = jnp.ones((8, 128), F32)
    ar[...] = lax.dot_general(ones8, gacc[...], (((1,), (1,)), ((), ())), precision=HI, preferred_element_type=F32)

    def exchange(src, buf, me, first, dev, then):
        buf[me] = src[...]
        cps = []
        for d in range(1, 16):
            b_, x_ = dev(d)
            cp = rcopy(src, buf.at[me], as_s.at[first + d - 1], as_r.at[first + d - 1], b_, x_)
            cp.start()
            cps.append(cp)
        then()
        for cp in cps:
            cp.wait_recv()
        drain.extend(cps)
        tot = [buf[j] for j in range(16)]
        while len(tot) > 1:
            tot = [a + b_ for a, b_ in zip(tot[::2], tot[1::2])]
        return tot[0]

    ar2[...] = exchange(ar, arx, z * NC + c, 0, zc, lambda: None)
    ar3 = exchange(ar2, ary, (rho // NC) * NX + x, 15, yx, lambda: moves(move, LATE))

    r48 = lax.broadcasted_iota(jnp.int32, (48, 128), 0)
    l48 = lax.broadcasted_iota(jnp.int32, (48, 128), 1)
    spread = jnp.where(r48 == l48, jnp.broadcast_to(ar3[0:1, :], (48, 128)), 0.0)
    spl[...] = jnp.dot(spread, jnp.ones((128, 128), F32), precision=HI, preferred_element_type=F32)

    def entry(n):
        return spl[n:n + 1, :]

    s = [1.0 / (SCALE * jnp.sqrt(entry(36 + v) + EPS)) for v in range(8)]
    low = {}
    inv = []
    for j in range(8):
        a = entry(pair(j, j)) * s[j] * s[j]
        for k in range(j):
            a = a - low[j, k] * low[j, k]
        inv.append(lax.rsqrt(a))
        low[j, j] = a * inv[j]
        for i in range(j + 1, 8):
            a = entry(pair(i, j)) * s[i] * s[j]
            for k in range(j):
                a = a - low[i, k] * low[j, k]
            low[i, j] = a * inv[j]
    xx = {}
    for j in range(8):
        xx[j, j] = inv[j]
        for i in range(j + 1, 8):
            a = low[i, j] * xx[j, j]
            for k in range(j + 1, i):
                a = a + low[i, k] * xx[k, j]
            xx[i, j] = -a * inv[i]
    upper = zero8
    for i in range(8):
        for j in range(i + 1):
            mix[pair(i, j)] = jnp.broadcast_to(xx[i, j] * s[j], (8, 128))
            upper = jnp.where(jnp.logical_and(iota8 == j, lane8 == i), jnp.broadcast_to(low[i, j], (8, 128)), upper)
    fac[...] = upper[:, 0:8]

    odd_row = (iota8 & 1) == 1

    def combine(q, outs, put):
        top = max(outs) // 2 + 1

        def body(f, _):
            last = rows[q // 2] - 1
            fixes = []
            for o in outs:
                tot = zero8
                for src in range(o // 2 + 1):
                    lo = mix[pair(o, 2 * src)]
                    hi = mix[pair(o, 2 * src + 1)] if 2 * src + 1 <= o else 0.0
                    tot = tot + jnp.where(odd_row, hi, lo) * cb[src, q, f]
                tot = tot + pltpu.roll(tot, 7, 0)
                fixes.append([jnp.broadcast_to(tot[r:r + 1], (8, 128)) for r in (0, 2, 4, 6)])
            for t in range(8):
                vals = [gath[w // 2, q, w % 2, f, 8 * t:8 * t + 8, :] for w in range(2 * top)]
                row = iota8 + 8 * t
                for n, o in enumerate(outs):
                    a = mix[pair(o, 0)] * vals[0]
                    for w in range(1, o + 1):
                        a = a + mix[pair(o, w)] * vals[w]
                    if t == 0:
                        a = a + jnp.where(row == 0, fixes[n][0], 0.0) + jnp.where(row == 1, fixes[n][2], 0.0)
                    if t >= 3:
                        a = a + jnp.where(row == last, fixes[n][1], 0.0) + jnp.where(row == last - 1, fixes[n][3], 0.0)
                    put(n, f, t, a)
            return 0

        lax.fori_loop(0, NF, body, 0)

    def home(i, v, q, to):
        return rcopy(res.at[i, v], out.at[v, q // 2, :, q % 2], os.at[i, v], orr.at[i, v], blk, jnp.int32(to))

    def own_copy(v, q):
        there = out.at[v, q // 2, :, q % 2]
        return pltpu.make_async_copy(bas.at[v, q // 2, :, q % 2], there, out_sem.at[v, q])

    def finish(g):
        beside = [(i, (g + d) % NX) for i, d in ((0, 1), (1, -1)) if (g + d) % NX > 0]
        for i, to in beside:
            def put(n, f, t, a, i=i):
                res[i, n, f, 8 * t:8 * t + 8, :] = a

            combine(g, [2 * to, 2 * to + 1], put)
            for v in range(2):
                home(i, v, g, to).start()
        mine_q = [g, (g + 2) % NX] if g > 0 else [0, 1, 2, 3]
        for q in mine_q:
            if q != g:
                for n in range(len(MOVES)):
                    if MOVES[n][1:] == (q, g):
                        move(n).wait_recv()
                        fix_move(n).wait_recv()

            def put_own(n, f, t, a, q=q):
                bas[n, q // 2, f, q % 2, 8 * t:8 * t + 8, :] = a

            combine(q, [2 * g, 2 * g + 1], put_own)
            for v in range(2):
                own_copy(v, q).start()
        for n in range(len(MOVES)):
            if MOVES[n][0] == g:
                move(n).wait_send()
                fix_move(n).wait_send()
        for q in mine_q:
            for v in range(2):
                own_copy(v, q).wait()
        for i, to in beside:
            for v in range(2):
                home(i, v, g, to).wait_send()
        if g > 0:
            for i, frm in ((0, (g - 1) % NX), (1, (g + 1) % NX)):
                for v in range(2):
                    home(i, v, frm, g).wait_recv()

    for cp in drain:
        cp.wait_send()
    for g in range(NX):
        @pl.when(x == g)
        def _():
            finish(g)


def per_device(vectors, metric, jacobians, block_rows, neighbours, flipped):
    vm = pl.BlockSpec(memory_space=pltpu.VMEM)
    hbm = pl.BlockSpec(memory_space=pltpu.HBM)
    dma = pltpu.SemaphoreType.DMA
    return pl.pallas_call(
        kernel,
        out_shape=(pltpu.VMEM(vectors.shape, F32), jax.ShapeDtypeStruct((8, 8), F32)),
        in_specs=[hbm] * 6,
        out_specs=(pl.BlockSpec(memory_space=pl.ANY), vm),
        scratch_shapes=[
            pltpu.VMEM(vectors.shape, F32),
            pltpu.VMEM(metric.shape, F32),
            pltpu.SMEM((NF, 3, NF), F32),
            pltpu.SMEM((2,), jnp.int32),
            pltpu.SMEM((2, 2), jnp.int32),
            pltpu.SMEM((2, 2), jnp.int32),
            pltpu.VMEM((2, 2, NF, 2, 80, 128), F32),
            pltpu.VMEM((2, 2, NF, 2, 80, 128), F32),
            pltpu.VMEM((4, 4, 2, NF, 64, 128), F32),
            pltpu.VMEM(vectors.shape, F32),
            pltpu.VMEM((2, 2, NF, 64, 128), F32),
            pltpu.VMEM((2, 4, 24, 128), F32),
            pltpu.VMEM((NZ, NC, 4, 24, 128), F32),
            pltpu.VMEM((NR, 8, 128), jnp.int32),
            pltpu.SMEM((NR, 8, 128), jnp.int32),
            pltpu.VMEM((NR, 4, 24, 128), F32),
            pltpu.VMEM((NR, 4, 24, 128), F32),
            pltpu.VMEM((12, 16, 128), F32),
            pltpu.VMEM((12, 16, 128), F32),
            pltpu.VMEM((4, 4, NF, 8, 128), F32),
            pltpu.VMEM((128, 128), F32),
            pltpu.VMEM((8, 128), F32),
            pltpu.VMEM((8, 128), F32),
            pltpu.VMEM((16, 8, 128), F32),
            pltpu.VMEM((16, 8, 128), F32),
            pltpu.VMEM((48, 128), F32),
            pltpu.VMEM((36, 8, 128), F32),
            dma((2,)), dma((5,)), dma((4,)),
            dma((2, 3)), dma((2, 3)),
            dma((33,)), dma((33,)),
            dma((7,)), dma((7,)),
            dma((7,)), dma((7,)),
            dma((3,)), dma((3,)),
            dma((30,)), dma((30,)),
            dma((len(MOVES),)), dma((len(MOVES),)),
            dma((6,)), dma((6,)),
            dma((2, 2)), dma((2, 2)),
            dma((2, 4)),
        ],
        compiler_params=pltpu.CompilerParams(collective_id=0, has_side_effects=True, vmem_limit_bytes=60 * 1024 * 1024),
        cost_estimate=pl.CostEstimate(flops=60_000_000, bytes_accessed=4_000_000, transcendentals=0),
    )(vectors, metric, jnp.transpose(jacobians, (1, 0, 2)), block_rows, neighbours, flipped)


def solution(mesh):
    wide = P("vec", "blk", None, None, None, None)
    in_specs = (wide, P("blk", None, None, None), P(), P("blk"), P("blk", None), P("blk", None))
    return jax.shard_map(per_device, mesh=mesh, in_specs=in_specs, out_specs=(wide, P()), check_vma=False)
```

```python
import jax
import jax.numpy as jnp
from jax import lax
from jax.experimental import pallas as pl
from jax.experimental.pallas import tpu as pltpu
from jax.sharding import PartitionSpec as P

MESH = pl.DeviceIdType.MESH
F32 = jnp.float32
HI = lax.Precision.HIGHEST
NF = 5
NZ, NY, NC, NX = 8, 4, 2, 4
NR = NY * NC
VISC = 0.1
EPS = 1e-06
SCALE = 1024.0


EARLY = [(1, 0, 2), (0, 3, 1), (0, 1, 3), (2, 1, 3)]
FAR = [(0, 0, 2), (1, 1, 3)]
MOVES = EARLY + FAR


def pair(v, w):
    return v * (v + 1) // 2 + w


def kernel(vec_h, met_h, jac_h, rows_h, nbr_h, flip_h, out, fac,
           vec, met, jac, rows, nbr, flip, st, fi, gath, bas, res, pay, zb, rq, rqs, o2, rb, own, gst, cb, edge, near, gacc, ar, ar2, arx, ary, spl, mix,
           loc_sem, in_sem, vec_sem, xs, xr, zs, zr, qs, qr, ys, yr, cs_s, cs_r, as_s, as_r, ws, wr, cs2_s, cs2_r, os, orr, out_sem):
    blk = lax.axis_index("blk")
    x = lax.axis_index("vec")
    z = blk // NR
    rho = lax.rem(blk, NR)
    c = lax.rem(blk, NC)
    col = lax.rem(blk, NR)

    def zdev(dz, core):
        zz = lax.rem(z + dz + NZ, NZ)
        return zz * NR + (rho - c) + core

    small = [pltpu.make_async_copy(h, d, in_sem.at[n]) for n, (h, d) in enumerate(
        ((rows_h, rows), (jac_h, jac), (nbr_h, nbr), (flip_h, flip), (met_h, met)))]
    big = [pltpu.make_async_copy(vec_h.at[n // 2, n % 2], vec.at[n // 2, n % 2], vec_sem.at[n]) for n in range(4)]
    for cp in small[:1] + big + small[1:]:
        cp.start()

    bar = pltpu.get_barrier_semaphore()
    def xdev(d):
        return lax.rem(x + d + NX, NX)

    def zc(d):
        m = lax.rem(z * NC + c + d, NZ * NC)
        return (m // NC) * NR + (rho - c) + lax.rem(m, NC), x

    def yx(d):
        m = lax.rem((rho // NC) * NX + x + d, (NR // NC) * NX)
        return z * NR + (m // NX) * NC + c, lax.rem(m, NX)

    def yc(d):
        return z * NR + lax.rem(rho + d, NR), x

    partners = [(zdev(dz, core), x) for dz in (1, -1) for core in range(2)] + [yc(d) for d in range(1, NR)]
    partners += [(blk, xdev(d)) for d in range(1, NX)]
    for b_, x_ in partners:
        pl.semaphore_signal(bar, inc=1, device_id={"blk": b_, "vec": x_}, device_id_type=MESH)
    n_part = len(partners)

    def rcopy(src, dst, ssem, rsem, b_, x_):
        return pltpu.make_async_remote_copy(src_ref=src, dst_ref=dst, send_sem=ssem, recv_sem=rsem,
                                            device_id={"blk": b_, "vec": x_}, device_id_type=MESH)

    iota64 = lax.broadcasted_iota(jnp.int32, (64, 128), 0)
    iota8 = lax.broadcasted_iota(jnp.int32, (8, 128), 0)
    lane8 = lax.broadcasted_iota(jnp.int32, (8, 128), 1)
    zero8 = jnp.zeros((8, 128), F32)

    for cp in small + big:
        cp.wait()

    sig = jnp.where((iota8 >> 1) & 1 == 0, -1.0, 1.0)
    sk = jnp.where(iota8 < 4, 1.0, -1.0)
    odd = iota8 & 1

    def jmul(d, g_, f):
        acc = jac[f, d, 0] * g_[0]
        for g in range(1, NF):
            acc = acc + jac[f, d, g] * g_[g]
        return acc

    def faces(i, _):
        b, side, v = i // 4, lax.rem(i // 2, 2), lax.rem(i, 2)
        last = jnp.maximum(rows[b] - 1, 1)
        r = jnp.where(side == 0, 0, last)
        adj = jnp.where(side == 0, 1, last - 1)
        slot = b * 2 + side
        lane_row = b * 8 + side * 2 + v
        for f in range(NF):
            for k in range(2):
                a = vec[v, b, f, k, pl.ds(r, 1), :]
                pay[v, slot, f * 2 + k:f * 2 + k + 1, :] = a
                own[f, pl.ds(lane_row + 4 * k, 1), :] = a
                gst[f, pl.ds(lane_row + 4 * k, 1), :] = vec[v, b, f, k, pl.ds(adj, 1), :]
        for k in range(2):
            m = met[b, k, pl.ds(r, 1), :]
            pay[v, slot, 20 + k:21 + k, :] = m
            pay[v, slot, 22 + k:23 + k, :] = m
            own[10, pl.ds(lane_row + 4 * k, 1), :] = m
            own[11, pl.ds(lane_row + 4 * k, 1), :] = met[b, k, pl.ds(adj, 1), :]
        return 0

    lax.fori_loop(0, 8, faces, 0)

    def face_step(b, _):
        base = pl.ds(pl.multiple_of(b * 8, 8), 8)
        q = [own[f, base, :] for f in range(NF)]
        inside = [gst[f, base, :] for f in range(NF)]
        m0 = own[10, base, :]
        e = [pltpu.roll(a, 127, 1) for a in q]
        w = [pltpu.roll(a, 1, 1) for a in q]
        ok = [pltpu.roll(a, 4, 0) for a in q]
        ew = [a - b_ for a, b_ in zip(e, w)]
        for f in range(NF):
            flux = jmul(0, ew, f) + sk * jmul(2, ok, f) - sig * jmul(1, inside, f)
            own[NF + f, base, :] = (1.0 - 6.0 * VISC) * q[f] + VISC * (e[f] + w[f] + ok[f] + inside[f]) - m0 * flux
        return 0

    lax.fori_loop(0, 2, face_step, 0)

    def pack(i, _):
        b, side, v = i // 4, lax.rem(i // 2, 2), lax.rem(i, 2)
        lane_row = b * 8 + side * 2 + v
        for f in range(NF):
            for k in range(2):
                pay[v, b * 2 + side, 10 + f * 2 + k:11 + f * 2 + k, :] = own[NF + f, pl.ds(lane_row + 4 * k, 1), :]
        return 0

    lax.fori_loop(0, 8, pack, 0)
    req = jnp.where(lane8 == 0, nbr[0, 0], jnp.where(lane8 == 1, nbr[0, 1], jnp.where(lane8 == 2, nbr[1, 0], nbr[1, 1])))
    rq[rho] = req

    pl.semaphore_wait(bar, n_part)

    mine = pltpu.make_async_copy(pay.at[c], zb.at[z, c], loc_sem.at[0])
    mine.start()
    z_copies = []
    for j in range(2):
        core = lax.rem(c + j, NC)
        for h in range(2):
            for side, dz in ((0, 1), (1, -1)):
                n = j * 4 + h * 2 + side
                half = pl.ds(2 * h, 2)
                cp = rcopy(pay.at[core, half], zb.at[z, c, half], zs.at[n], zr.at[n], zdev(dz, core), x)
                cp.start()
                z_copies.append(cp)
    other = rcopy(pay.at[1 - c], zb.at[z, c], zs.at[8], zr.at[8], zdev(0, 1 - c), x)
    other.start()
    q_copies = []
    for d in range(1, NR):
        cp = rcopy(rq.at[rho], rq.at[rho], qs.at[d - 1], qr.at[d - 1], z * NR + lax.rem(rho + d, NR), x)
        cp.start()
        q_copies.append(cp)

    def fill(i, _):
        vb = i // 10
        v, b = vb // 2, lax.rem(vb, 2)
        fk = lax.rem(i, 10)
        f, k = fk // 2, lax.rem(fk, 2)
        q = vec[v, b, f, k]
        st[v, b, f, k, 8:72, :] = jnp.where(iota64 < rows[b], q, 0.0)
        st[v, b, f, k, 0:8, :] = zero8
        st[v, b, f, k, 72:80, :] = zero8
        fi[v, b, f, k, 0:8, :] = zero8
        fi[v, b, f, k, 72:80, :] = zero8
        return 0

    lax.fori_loop(0, 20, fill, 0)

    def advance_tile(src, v, b, t, scale, store):
        r0 = pl.multiple_of(t * 8, 8)
        alive = (iota8 + r0) < rows[b]
        qs_, d0, d1, base = [], [], [], []
        for k in range(2):
            qk = [src[v, b, f, k, pl.ds(r0 + 8, 8), :] for f in range(NF)]
            qs_.append(qk)
        for k in range(2):
            a0, a1, ab = [], [], []
            for f in range(NF):
                q = qs_[k][f]
                e = pltpu.roll(q, 127, 1)
                w = pltpu.roll(q, 1, 1)
                n = src[v, b, f, k, pl.ds(r0 + 9, 8), :]
                s = src[v, b, f, k, pl.ds(r0 + 7, 8), :]
                a0.append(e - w)
                a1.append(n - s)
                ab.append((scale * (1.0 - 6.0 * VISC)) * q + (scale * VISC) * ((e + w) + (n + s) + qs_[1 - k][f]))
            d0.append(a0)
            d1.append(a1)
            base.append(ab)
        mk = [met[b, k, pl.ds(r0, 8), :] * scale for k in range(2)]
        for f in range(NF):
            c0 = [jac[f, 0, g] for g in range(NF)]
            c1 = [jac[f, 1, g] for g in range(NF)]
            c2 = [jac[f, 2, g] for g in range(NF)]
            for k in range(2):
                acc = c0[0] * d0[k][0] + c1[0] * d1[k][0]
                oth = c2[0] * qs_[1 - k][0]
                for g in range(1, NF):
                    acc = acc + c0[g] * d0[k][g] + c1[g] * d1[k][g]
                    oth = oth + c2[g] * qs_[1 - k][g]
                flux = acc + oth if k == 0 else acc - oth
                store(f, k, jnp.where(alive, base[k][f] - mk[k] * flux, 0.0))

    def first_pass(i, sums):
        vb, t = i // 8, lax.rem(i, 8)
        v, b = vb // 2, lax.rem(vb, 2)
        r0 = t * 8
        row = iota8 + r0
        inner = jnp.logical_and(row > 0, row != rows[b] - 1)
        box = [jnp.zeros((8, 128), F32)]

        def store(f, k, val):
            fi[v, b, f, k, pl.ds(pl.multiple_of(r0 + 8, 8), 8), :] = val
            box[0] = box[0] + val * val

        advance_tile(st, v, b, t, 1.0, store)
        sq = jnp.where(inner, box[0], 0.0)
        s0, s1 = sums
        return s0 + jnp.where(v == 0, sq, 0.0), s1 + jnp.where(v == 1, sq, 0.0)

    ssq = lax.fori_loop(0, 16, first_pass, (zero8, zero8))

    def second_pass(v):
        def body(i, _):
            b, t = i // 8, lax.rem(i, 8)

            def store(f, k, val):
                gath[x, b * 2 + k, v, f, pl.ds(pl.multiple_of(t * 8, 8), 8), :] = val

            advance_tile(fi, v, b, t, SCALE, store)
            return 0

        lax.fori_loop(0, 16, body, 0)

    sends = []

    def send_second(v):
        for d in (2, 1, 3):
            here = gath.at[x, xdev(d), v]
            cp = rcopy(here, here, xs.at[v, d - 1], xr.at[v, d - 1], blk, xdev(d))
            cp.start()
            sends.append(cp)

    def move(n, v):
        src, q, to = MOVES[n]
        part = gath.at[src, q, v]
        return rcopy(part, part, ws.at[n, v], wr.at[n, v], blk, jnp.int32(to))

    def fix_move(n):
        src, q, to = MOVES[n]
        part = cb.at[src, q]
        return rcopy(part, part, cs2_s.at[n], cs2_r.at[n], blk, jnp.int32(to))

    def moves(which, vs):
        for n in range(len(MOVES)):
            if MOVES[n] in which:
                @pl.when(x == MOVES[n][0])
                def _():
                    for v in vs:
                        move(n, v).start()

    def fix_moves():
        for n in range(len(MOVES)):
            @pl.when(x == MOVES[n][0])
            def _():
                fix_move(n).start()

    drain = z_copies + [other]

    def ring_step(s, before):
        cps = []
        for j in range(2):
            core = lax.rem(c + j, NC)
            for h in range(2):
                for side, dz in ((0, 1), (1, -1)):
                    m = j * 4 + h * 2 + side
                    before[m].wait_recv()
                    if s == 3 and side != j:
                        continue
                    n = 9 + (s - 1) * 8 + m
                    part = zb.at[lax.rem(z - dz * s + NZ, NZ), core, pl.ds(2 * h, 2)]
                    cp = rcopy(part, part, zs.at[n], zr.at[n], zdev(dz, c), x)
                    cp.start()
                    cps.append(cp)
        drain.extend(cps)
        return cps

    second_pass(0)
    send_second(0)
    ring1 = ring_step(1, z_copies)
    lax.fori_loop(20, 40, fill, 0)
    ssq = lax.fori_loop(16, 32, first_pass, ssq)

    second_pass(1)
    send_second(1)
    moves(FAR, (0,))
    ring2 = ring_step(2, ring1)
    for cp in q_copies:
        cp.wait_recv()
    tosmem = pltpu.make_async_copy(rq, rqs, loc_sem.at[1])
    tosmem.start()
    ring3 = ring_step(3, ring2)
    mine.wait()
    other.wait_recv()
    tosmem.wait()
    for cp in ring3:
        cp.wait_recv()

    def pick(i, _):
        to, r = i // 4, lax.rem(i, 4)
        bid = rqs[to, 0, r]
        side = lax.rem(r, 2)
        o2[to, r] = zb[bid >> 4, (bid >> 1) & 1, (bid & 1) * 2 + (1 - side)]
        return 0

    lax.fori_loop(0, 4 * NR, pick, 0)
    y_copies = []
    for d in range(1, NR):
        to = lax.rem(rho + d, NR)
        cp = rcopy(o2.at[to], rb.at[rho], ys.at[d - 1], yr.at[d - 1], z * NR + to, x)
        cp.start()
        y_copies.append(cp)
    rb[rho] = o2[rho]
    for cp in y_copies:
        cp.wait_recv()
    drain += y_copies + q_copies

    rev = 127 - lane8

    def unpack(i, _):
        b, side, v = i // 4, lax.rem(i // 2, 2), lax.rem(i, 2)
        r = b * 2 + side
        bid = nbr[b, side]
        f_ = flip[b, side]
        lane_row = b * 8 + side * 2 + v
        src = ((bid >> 2) & 3) * 2 + v
        for h in range(3):
            q = rb[src, r, 8 * h:8 * h + 8, :]
            turned = jnp.take_along_axis(q, rev, axis=1)
            rowh = iota8 + 8 * h
            neg = jnp.logical_or(jnp.logical_or(rowh == 2, rowh == 3), jnp.logical_or(rowh == 12, rowh == 13))
            turned = jnp.where(neg, -turned, turned)
            q = jnp.where(f_ > 0, turned, q)
            for j in range(8):
                w = 8 * h + j
                if w >= 22:
                    continue
                item, k = (w // 2, w % 2)
                gst[item, pl.ds(lane_row + 4 * k, 1), :] = q[j:j + 1, :]
        sign = jnp.where(f_ > 0, -1.0, 1.0) + jnp.zeros((1, 128), F32)
        for k in range(2):
            gst[11, pl.ds(lane_row + 4 * k, 1), :] = sign
        return 0

    lax.fori_loop(0, 8, unpack, 0)

    def fix(b, sums):
        base = pl.ds(pl.multiple_of(b * 8, 8), 8)
        g0 = [gst[f, base, :] for f in range(NF)]
        gf = [gst[NF + f, base, :] for f in range(NF)]
        gm = gst[10, base, :]
        turn = gst[11, base, :]
        o = [own[f, base, :] for f in range(NF)]
        of = [own[NF + f, base, :] for f in range(NF)]
        m0 = own[10, base, :]
        m1 = own[11, base, :]
        od = [o[f] * turn if f == 1 else o[f] for f in range(NF)]
        g1, c1 = [], []
        total = zero8
        for f in range(NF):
            tf = jmul(1, od, f)
            if f == 1:
                tf = tf * turn
            g1.append(gf[f] + VISC * o[f] + sig * gm * tf)
            cf = VISC * g0[f] - sig * m0 * jmul(1, g0, f)
            c1.append(cf)
            ff = of[f] + cf
            total = total + ff * ff
        e = [pltpu.roll(cf, 127, 1) for cf in c1]
        w = [pltpu.roll(cf, 1, 1) for cf in c1]
        ok = [pltpu.roll(cf, 4, 0) for cf in c1]
        ew = [a - b_ for a, b_ in zip(e, w)]
        for f in range(NF):
            flux = jmul(0, ew, f) + sk * jmul(2, ok, f) + sig * jmul(1, g1, f)
            face = (1.0 - 6.0 * VISC) * c1[f] + VISC * (e[f] + w[f] + ok[f] + g1[f]) - m0 * flux
            near = VISC * c1[f] - sig * m1 * jmul(1, c1, f)
            face = face * SCALE
            near = near * SCALE
            cb[x, b * 2, f, 0:4, :] = face[0:4]
            cb[x, b * 2, f, 4:8, :] = near[0:4]
            cb[x, b * 2 + 1, f, 0:4, :] = face[4:8]
            cb[x, b * 2 + 1, f, 4:8, :] = near[4:8]
        s0, s1 = sums
        return s0 + jnp.where(odd == 0, total, 0.0), s1 + jnp.where(odd == 1, total, 0.0)

    ssq = lax.fori_loop(0, 2, fix, ssq)
    c_copies = []
    for d in (2, 1, 3):
        here = cb.at[x, xdev(d)]
        cp = rcopy(here, here, cs_s.at[d - 1], cs_r.at[d - 1], blk, xdev(d))
        cp.start()
        c_copies.append(cp)
    fix_moves()
    moves(EARLY, (0, 1))
    for cp in sends:
        cp.wait_recv()

    bq = x // 2
    my_last = jnp.where(bq == 0, rows[0], rows[1]) - 1
    safe_last = jnp.maximum(my_last, 1)

    def products(acc, left, right):
        res = list(acc)
        for v in range(8):
            for w in range(v + 1):
                res[pair(v, w)] = res[pair(v, w)] + left[v] * right[w]
        return tuple(res)

    def gram_tile(i, acc):
        f, t = i // 8, lax.rem(i, 8)
        row = iota8 + t * 8
        inner = jnp.logical_and(row > 1, jnp.logical_or(row < my_last - 1, row > my_last))
        vals = [gath[v // 2, x, v % 2, f, pl.ds(pl.multiple_of(t * 8, 8), 8), :] for v in range(8)]
        for v in range(8):
            near[v, f, pl.ds(pl.multiple_of(t * 8, 8), 8), :] = vals[v]
        return products(acc, [jnp.where(inner, q, 0.0) for q in vals], vals)

    grams = lax.fori_loop(0, 40, gram_tile, tuple(zero8 for _ in range(36)))

    def edges(i, _):
        f, v = i // 8, lax.rem(i, 8)
        for j, r in enumerate((0, safe_last, 1, safe_last - 1)):
            edge[v // 2, f, pl.ds(2 * j + lax.rem(v, 2), 1), :] = near[v, f, pl.ds(r, 1), :]
        return 0

    lax.fori_loop(0, 40, edges, 0)
    for cp in c_copies:
        cp.wait_recv()
    drain += sends + c_copies
    odd_row = (iota8 & 1) == 1

    def gram_edge(f, acc):
        vals = []
        for src in range(NX):
            both = edge[src, f] + cb[src, x, f]
            vals.append(jnp.where(odd_row, 0.0, both))
            vals.append(jnp.where(odd_row, 0.0, pltpu.roll(both, 7, 0)))
        return products(acc, vals, vals)

    grams = lax.fori_loop(0, NF, gram_edge, grams)
    gacc[...] = jnp.zeros((128, 128), F32)
    for n in range(36):
        gacc[n:n + 1, :] = jnp.sum(grams[n], axis=0, keepdims=True)
    for v in range(2):
        gacc[pl.ds(36 + 2 * x + v, 1), :] = jnp.sum(ssq[v], axis=0, keepdims=True)
    ones8 = jnp.ones((8, 128), F32)
    ar[...] = lax.dot_general(ones8, gacc[...], (((1,), (1,)), ((), ())), precision=HI, preferred_element_type=F32)[0:1, :]

    def exchange(src, buf, me, first, dev, then):
        buf[me] = src[...]
        cps = []
        for d in range(1, 16):
            b_, x_ = dev(d)
            cp = rcopy(src, buf.at[me], as_s.at[first + d - 1], as_r.at[first + d - 1], b_, x_)
            cp.start()
            cps.append(cp)
        then()
        for cp in cps:
            cp.wait_recv()
        drain.extend(cps)
        tot = [buf[j] for j in range(16)]
        while len(tot) > 1:
            tot = [a + b_ for a, b_ in zip(tot[::2], tot[1::2])]
        return tot[0]

    ar2[...] = exchange(ar, arx, z * NC + c, 0, zc, lambda: None)
    ar3 = exchange(ar2, ary, (rho // NC) * NX + x, 15, yx, lambda: moves(FAR, (1,)))

    r48 = lax.broadcasted_iota(jnp.int32, (48, 128), 0)
    l48 = lax.broadcasted_iota(jnp.int32, (48, 128), 1)
    spread = jnp.where(r48 == l48, jnp.broadcast_to(ar3[0:1, :], (48, 128)), 0.0)
    spl[...] = jnp.dot(spread, jnp.ones((128, 128), F32), precision=HI, preferred_element_type=F32)

    def entry(n):
        return spl[n:n + 1, :]

    s = [1.0 / (SCALE * jnp.sqrt(entry(36 + v) + EPS)) for v in range(8)]
    low = {}
    inv = []
    for j in range(8):
        a = entry(pair(j, j)) * s[j] * s[j]
        for k in range(j):
            a = a - low[j, k] * low[j, k]
        inv.append(lax.rsqrt(a))
        low[j, j] = a * inv[j]
        for i in range(j + 1, 8):
            a = entry(pair(i, j)) * s[i] * s[j]
            for k in range(j):
                a = a - low[i, k] * low[j, k]
            low[i, j] = a * inv[j]
    xx = {}
    for j in range(8):
        xx[j, j] = inv[j]
        for i in range(j + 1, 8):
            a = low[i, j] * xx[j, j]
            for k in range(j + 1, i):
                a = a + low[i, k] * xx[k, j]
            xx[i, j] = -a * inv[i]
    upper = zero8
    for i in range(8):
        for j in range(i + 1):
            mix[pair(i, j)] = jnp.broadcast_to(xx[i, j] * s[j], (8, 128))
            upper = jnp.where(jnp.logical_and(iota8 == j, lane8 == i), jnp.broadcast_to(low[i, j], (8, 128)), upper)
    fac[...] = upper[:, 0:8]

    def combine(q, outs, put):
        top = max(outs) // 2 + 1

        def body(f, _):
            last = rows[q // 2] - 1
            fixes = []
            for o in outs:
                tot = zero8
                for src in range(o // 2 + 1):
                    lo = mix[pair(o, 2 * src)]
                    hi = mix[pair(o, 2 * src + 1)] if 2 * src + 1 <= o else 0.0
                    tot = tot + jnp.where(odd_row, hi, lo) * cb[src, q, f]
                tot = tot + pltpu.roll(tot, 7, 0)
                fixes.append([jnp.broadcast_to(tot[r:r + 1], (8, 128)) for r in (0, 2, 4, 6)])
            for t in range(8):
                vals = [gath[w // 2, q, w % 2, f, 8 * t:8 * t + 8, :] for w in range(2 * top)]
                row = iota8 + 8 * t
                for n, o in enumerate(outs):
                    a = mix[pair(o, 0)] * vals[0]
                    for w in range(1, o + 1):
                        a = a + mix[pair(o, w)] * vals[w]
                    if t == 0:
                        a = a + jnp.where(row == 0, fixes[n][0], 0.0) + jnp.where(row == 1, fixes[n][2], 0.0)
                    if t >= 3:
                        a = a + jnp.where(row == last, fixes[n][1], 0.0) + jnp.where(row == last - 1, fixes[n][3], 0.0)
                    put(n, f, t, a)
            return 0

        lax.fori_loop(0, NF, body, 0)

    def home(i, v, q, to):
        return rcopy(res.at[i, v], out.at[v, q // 2, :, q % 2], os.at[i, v], orr.at[i, v], blk, jnp.int32(to))

    def own_copy(v, q):
        there = out.at[v, q // 2, :, q % 2]
        return pltpu.make_async_copy(bas.at[v, q // 2, :, q % 2], there, out_sem.at[v, q])

    def finish(g):
        beside = [(i, (g + d) % NX) for i, d in ((0, 1), (1, -1)) if (g + d) % NX > 0]
        for i, to in beside:
            def put(n, f, t, a, i=i):
                res[i, n, f, 8 * t:8 * t + 8, :] = a

            combine(g, [2 * to, 2 * to + 1], put)
            for v in range(2):
                home(i, v, g, to).start()
        mine_q = [g, (g + 2) % NX] if g > 0 else [0, 1, 2, 3]
        for q in mine_q:
            if q != g:
                for n in range(len(MOVES)):
                    if MOVES[n][1:] == (q, g):
                        move(n, 0).wait_recv()
                        move(n, 1).wait_recv()
                        fix_move(n).wait_recv()

            def put_own(n, f, t, a, q=q):
                bas[n, q // 2, f, q % 2, 8 * t:8 * t + 8, :] = a

            combine(q, [2 * g, 2 * g + 1], put_own)
            for v in range(2):
                own_copy(v, q).start()
        for n in range(len(MOVES)):
            if MOVES[n][0] == g:
                move(n, 0).wait_send()
                move(n, 1).wait_send()
                fix_move(n).wait_send()
        for q in mine_q:
            for v in range(2):
                own_copy(v, q).wait()
        for i, to in beside:
            for v in range(2):
                home(i, v, g, to).wait_send()
        if g > 0:
            for i, frm in ((0, (g - 1) % NX), (1, (g + 1) % NX)):
                for v in range(2):
                    home(i, v, frm, g).wait_recv()

    for cp in drain:
        cp.wait_send()
    for g in range(NX):
        @pl.when(x == g)
        def _():
            finish(g)


def per_device(vectors, metric, jacobians, block_rows, neighbours, flipped):
    vm = pl.BlockSpec(memory_space=pltpu.VMEM)
    hbm = pl.BlockSpec(memory_space=pltpu.HBM)
    dma = pltpu.SemaphoreType.DMA
    return pl.pallas_call(
        kernel,
        out_shape=(pltpu.VMEM(vectors.shape, F32), jax.ShapeDtypeStruct((8, 8), F32)),
        in_specs=[hbm] * 6,
        out_specs=(pl.BlockSpec(memory_space=pl.ANY), vm),
        scratch_shapes=[
            pltpu.VMEM(vectors.shape, F32),
            pltpu.VMEM(metric.shape, F32),
            pltpu.SMEM((NF, 3, NF), F32),
            pltpu.SMEM((2,), jnp.int32),
            pltpu.SMEM((2, 2), jnp.int32),
            pltpu.SMEM((2, 2), jnp.int32),
            pltpu.VMEM((2, 2, NF, 2, 80, 128), F32),
            pltpu.VMEM((2, 2, NF, 2, 80, 128), F32),
            pltpu.VMEM((4, 4, 2, NF, 64, 128), F32),
            pltpu.VMEM(vectors.shape, F32),
            pltpu.VMEM((2, 2, NF, 64, 128), F32),
            pltpu.VMEM((2, 4, 24, 128), F32),
            pltpu.VMEM((NZ, NC, 4, 24, 128), F32),
            pltpu.VMEM((NR, 8, 128), jnp.int32),
            pltpu.SMEM((NR, 8, 128), jnp.int32),
            pltpu.VMEM((NR, 4, 24, 128), F32),
            pltpu.VMEM((NR, 4, 24, 128), F32),
            pltpu.VMEM((12, 16, 128), F32),
            pltpu.VMEM((12, 16, 128), F32),
            pltpu.VMEM((4, 4, NF, 8, 128), F32),
            pltpu.VMEM((4, NF, 8, 128), F32),
            pltpu.VMEM((8, NF, 64, 128), F32),
            pltpu.VMEM((128, 128), F32),
            pltpu.VMEM((1, 128), F32),
            pltpu.VMEM((1, 128), F32),
            pltpu.VMEM((16, 1, 128), F32),
            pltpu.VMEM((16, 1, 128), F32),
            pltpu.VMEM((48, 128), F32),
            pltpu.VMEM((36, 8, 128), F32),
            dma((2,)), dma((5,)), dma((4,)),
            dma((2, 3)), dma((2, 3)),
            dma((33,)), dma((33,)),
            dma((7,)), dma((7,)),
            dma((7,)), dma((7,)),
            dma((3,)), dma((3,)),
            dma((30,)), dma((30,)),
            dma((len(MOVES), 2)), dma((len(MOVES), 2)),
            dma((6,)), dma((6,)),
            dma((2, 2)), dma((2, 2)),
            dma((2, 4)),
        ],
        compiler_params=pltpu.CompilerParams(collective_id=0, has_side_effects=True, vmem_limit_bytes=60 * 1024 * 1024),
        cost_estimate=pl.CostEstimate(flops=60_000_000, bytes_accessed=4_000_000, transcendentals=0),
    )(vectors, metric, jnp.transpose(jacobians, (1, 0, 2)), block_rows, neighbours, flipped)


def solution(mesh):
    wide = P("vec", "blk", None, None, None, None)
    in_specs = (wide, P("blk", None, None, None), P(), P("blk"), P("blk", None), P("blk", None))
    return jax.shard_map(per_device, mesh=mesh, in_specs=in_specs, out_specs=(wide, P()), check_vma=False)
```

```python
import jax
import jax.numpy as jnp
from jax import lax
from jax.experimental import pallas as pl
from jax.experimental.pallas import tpu as pltpu
from jax.sharding import PartitionSpec as P

MESH = pl.DeviceIdType.MESH
F32 = jnp.float32
HI = lax.Precision.HIGHEST
NF = 5
NZ, NY, NC, NX = 8, 4, 2, 4
NR = NY * NC
VISC = 0.1
EPS = 1e-06
SCALE = 1024.0


EARLY = [(1, 0, 2), (0, 3, 1), (0, 1, 3), (2, 1, 3)]
FAR = [(0, 0, 2), (1, 1, 3)]
MOVES = EARLY + FAR


def pair(v, w):
    return v * (v + 1) // 2 + w


def kernel(vec_h, met_h, jac_h, rows_h, nbr_h, flip_h, out, fac,
           vec, met, jac, rows, nbr, flip, st, fi, gath, bas, res, pay, zb, rq, rqs, o2, rb, own, gst, cb, edge, near, gacc, ar, ar2, arx, ary, spl, mix,
           loc_sem, in_sem, vec_sem, xs, xr, zs, zr, qs, qr, ys, yr, cs_s, cs_r, as_s, as_r, ws, wr, cs2_s, cs2_r, os, orr, out_sem):
    blk = lax.axis_index("blk")
    x = lax.axis_index("vec")
    z = blk // NR
    rho = lax.rem(blk, NR)
    c = lax.rem(blk, NC)
    col = lax.rem(blk, NR)

    def zdev(dz, core):
        zz = lax.rem(z + dz + NZ, NZ)
        return zz * NR + (rho - c) + core

    small = [pltpu.make_async_copy(h, d, in_sem.at[n]) for n, (h, d) in enumerate(
        ((rows_h, rows), (jac_h, jac), (nbr_h, nbr), (flip_h, flip), (met_h, met)))]
    big = [pltpu.make_async_copy(vec_h.at[n // 2, n % 2], vec.at[n // 2, n % 2], vec_sem.at[n]) for n in range(4)]
    for cp in small[:1] + big + small[1:]:
        cp.start()

    bar = pltpu.get_barrier_semaphore()
    def xdev(d):
        return lax.rem(x + d + NX, NX)

    def zc(d):
        m = lax.rem(z * NC + c + d, NZ * NC)
        return (m // NC) * NR + (rho - c) + lax.rem(m, NC), x

    def yx(d):
        m = lax.rem((rho // NC) * NX + x + d, (NR // NC) * NX)
        return z * NR + (m // NX) * NC + c, lax.rem(m, NX)

    def yc(d):
        return z * NR + lax.rem(rho + d, NR), x

    partners = [(zdev(dz, core), x) for dz in (1, -1) for core in range(2)] + [yc(d) for d in range(1, NR)]
    partners += [(blk, xdev(d)) for d in range(1, NX)]
    for b_, x_ in partners:
        pl.semaphore_signal(bar, inc=1, device_id={"blk": b_, "vec": x_}, device_id_type=MESH)
    n_part = len(partners)

    def rcopy(src, dst, ssem, rsem, b_, x_):
        return pltpu.make_async_remote_copy(src_ref=src, dst_ref=dst, send_sem=ssem, recv_sem=rsem,
                                            device_id={"blk": b_, "vec": x_}, device_id_type=MESH)

    iota64 = lax.broadcasted_iota(jnp.int32, (64, 128), 0)
    iota8 = lax.broadcasted_iota(jnp.int32, (8, 128), 0)
    lane8 = lax.broadcasted_iota(jnp.int32, (8, 128), 1)
    zero8 = jnp.zeros((8, 128), F32)

    for cp in small + big:
        cp.wait()

    sig = jnp.where((iota8 >> 1) & 1 == 0, -1.0, 1.0)
    sk = jnp.where(iota8 < 4, 1.0, -1.0)
    odd = iota8 & 1

    def jmul(d, g_, f):
        acc = jac[f, d, 0] * g_[0]
        for g in range(1, NF):
            acc = acc + jac[f, d, g] * g_[g]
        return acc

    def faces(i, _):
        b, side, v = i // 4, lax.rem(i // 2, 2), lax.rem(i, 2)
        last = jnp.maximum(rows[b] - 1, 1)
        r = jnp.where(side == 0, 0, last)
        adj = jnp.where(side == 0, 1, last - 1)
        slot = b * 2 + side
        lane_row = b * 8 + side * 2 + v
        for f in range(NF):
            for k in range(2):
                a = vec[v, b, f, k, pl.ds(r, 1), :]
                pay[v, slot, f * 2 + k:f * 2 + k + 1, :] = a
                own[f, pl.ds(lane_row + 4 * k, 1), :] = a
                gst[f, pl.ds(lane_row + 4 * k, 1), :] = vec[v, b, f, k, pl.ds(adj, 1), :]
        for k in range(2):
            m = met[b, k, pl.ds(r, 1), :]
            pay[v, slot, 20 + k:21 + k, :] = m
            pay[v, slot, 22 + k:23 + k, :] = m
            own[10, pl.ds(lane_row + 4 * k, 1), :] = m
            own[11, pl.ds(lane_row + 4 * k, 1), :] = met[b, k, pl.ds(adj, 1), :]
        return 0

    lax.fori_loop(0, 8, faces, 0)

    def face_step(b, _):
        base = pl.ds(pl.multiple_of(b * 8, 8), 8)
        q = [own[f, base, :] for f in range(NF)]
        inside = [gst[f, base, :] for f in range(NF)]
        m0 = own[10, base, :]
        e = [pltpu.roll(a, 127, 1) for a in q]
        w = [pltpu.roll(a, 1, 1) for a in q]
        ok = [pltpu.roll(a, 4, 0) for a in q]
        ew = [a - b_ for a, b_ in zip(e, w)]
        for f in range(NF):
            flux = jmul(0, ew, f) + sk * jmul(2, ok, f) - sig * jmul(1, inside, f)
            own[NF + f, base, :] = (1.0 - 6.0 * VISC) * q[f] + VISC * (e[f] + w[f] + ok[f] + inside[f]) - m0 * flux
        return 0

    lax.fori_loop(0, 2, face_step, 0)

    def pack(i, _):
        b, side, v = i // 4, lax.rem(i // 2, 2), lax.rem(i, 2)
        lane_row = b * 8 + side * 2 + v
        for f in range(NF):
            for k in range(2):
                pay[v, b * 2 + side, 10 + f * 2 + k:11 + f * 2 + k, :] = own[NF + f, pl.ds(lane_row + 4 * k, 1), :]
        return 0

    lax.fori_loop(0, 8, pack, 0)
    req = jnp.where(lane8 == 0, nbr[0, 0], jnp.where(lane8 == 1, nbr[0, 1], jnp.where(lane8 == 2, nbr[1, 0], nbr[1, 1])))
    rq[rho] = req

    pl.semaphore_wait(bar, n_part)

    mine = pltpu.make_async_copy(pay.at[c], zb.at[z, c], loc_sem.at[0])
    mine.start()
    z_copies = []
    for j in range(2):
        core = lax.rem(c + j, NC)
        for h in range(2):
            for side, dz in ((0, 1), (1, -1)):
                n = j * 4 + h * 2 + side
                half = pl.ds(2 * h, 2)
                cp = rcopy(pay.at[core, half], zb.at[z, c, half], zs.at[n], zr.at[n], zdev(dz, core), x)
                cp.start()
                z_copies.append(cp)
    other = rcopy(pay.at[1 - c], zb.at[z, c], zs.at[8], zr.at[8], zdev(0, 1 - c), x)
    other.start()
    q_copies = []
    for d in range(1, NR):
        cp = rcopy(rq.at[rho], rq.at[rho], qs.at[d - 1], qr.at[d - 1], z * NR + lax.rem(rho + d, NR), x)
        cp.start()
        q_copies.append(cp)

    def fill(i, _):
        vb = i // 10
        v, b = vb // 2, lax.rem(vb, 2)
        fk = lax.rem(i, 10)
        f, k = fk // 2, lax.rem(fk, 2)
        q = vec[v, b, f, k]
        st[v, b, f, k, 8:72, :] = jnp.where(iota64 < rows[b], q, 0.0)
        st[v, b, f, k, 0:8, :] = zero8
        st[v, b, f, k, 72:80, :] = zero8
        fi[v, b, f, k, 0:8, :] = zero8
        fi[v, b, f, k, 72:80, :] = zero8
        return 0

    lax.fori_loop(0, 20, fill, 0)

    def advance_tile(src, v, b, t, scale, store):
        r0 = pl.multiple_of(t * 8, 8)
        alive = (iota8 + r0) < rows[b]
        qs_, d0, d1, base = [], [], [], []
        for k in range(2):
            qk = [src[v, b, f, k, pl.ds(r0 + 8, 8), :] for f in range(NF)]
            qs_.append(qk)
        for k in range(2):
            a0, a1, ab = [], [], []
            for f in range(NF):
                q = qs_[k][f]
                e = pltpu.roll(q, 127, 1)
                w = pltpu.roll(q, 1, 1)
                n = src[v, b, f, k, pl.ds(r0 + 9, 8), :]
                s = src[v, b, f, k, pl.ds(r0 + 7, 8), :]
                a0.append(e - w)
                a1.append(n - s)
                ab.append((scale * (1.0 - 6.0 * VISC)) * q + (scale * VISC) * ((e + w) + (n + s) + qs_[1 - k][f]))
            d0.append(a0)
            d1.append(a1)
            base.append(ab)
        mk = [met[b, k, pl.ds(r0, 8), :] * scale for k in range(2)]
        for f in range(NF):
            c0 = [jac[f, 0, g] for g in range(NF)]
            c1 = [jac[f, 1, g] for g in range(NF)]
            c2 = [jac[f, 2, g] for g in range(NF)]
            for k in range(2):
                acc = c0[0] * d0[k][0] + c1[0] * d1[k][0]
                oth = c2[0] * qs_[1 - k][0]
                for g in range(1, NF):
                    acc = acc + c0[g] * d0[k][g] + c1[g] * d1[k][g]
                    oth = oth + c2[g] * qs_[1 - k][g]
                flux = acc + oth if k == 0 else acc - oth
                store(f, k, jnp.where(alive, base[k][f] - mk[k] * flux, 0.0))

    def first_pass(i, sums):
        vb, t = i // 8, lax.rem(i, 8)
        v, b = vb // 2, lax.rem(vb, 2)
        r0 = t * 8
        row = iota8 + r0
        inner = jnp.logical_and(row > 0, row != rows[b] - 1)
        box = [jnp.zeros((8, 128), F32)]

        def store(f, k, val):
            fi[v, b, f, k, pl.ds(pl.multiple_of(r0 + 8, 8), 8), :] = val
            box[0] = box[0] + val * val

        advance_tile(st, v, b, t, 1.0, store)
        sq = jnp.where(inner, box[0], 0.0)
        s0, s1 = sums
        return s0 + jnp.where(v == 0, sq, 0.0), s1 + jnp.where(v == 1, sq, 0.0)

    ssq = lax.fori_loop(0, 16, first_pass, (zero8, zero8))

    def second_pass(v):
        def body(i, _):
            b, t = i // 8, lax.rem(i, 8)

            def store(f, k, val):
                gath[x, b * 2 + k, v, f, pl.ds(pl.multiple_of(t * 8, 8), 8), :] = val

            advance_tile(fi, v, b, t, SCALE, store)
            return 0

        lax.fori_loop(0, 16, body, 0)

    sends = []

    def send_second(v):
        for d in (2, 1, 3):
            here = gath.at[x, xdev(d), v]
            cp = rcopy(here, here, xs.at[v, d - 1], xr.at[v, d - 1], blk, xdev(d))
            cp.start()
            sends.append(cp)

    def move(n, v):
        src, q, to = MOVES[n]
        part = gath.at[src, q, v]
        return rcopy(part, part, ws.at[n, v], wr.at[n, v], blk, jnp.int32(to))

    def fix_move(n):
        src, q, to = MOVES[n]
        part = cb.at[src, q]
        return rcopy(part, part, cs2_s.at[n], cs2_r.at[n], blk, jnp.int32(to))

    def moves(which, vs):
        for n in range(len(MOVES)):
            if MOVES[n] in which:
                @pl.when(x == MOVES[n][0])
                def _():
                    for v in vs:
                        move(n, v).start()

    def fix_moves():
        for n in range(len(MOVES)):
            @pl.when(x == MOVES[n][0])
            def _():
                fix_move(n).start()

    drain = z_copies + [other]

    def ring_step(s, before):
        cps = []
        for j in range(2):
            core = lax.rem(c + j, NC)
            for h in range(2):
                for side, dz in ((0, 1), (1, -1)):
                    m = j * 4 + h * 2 + side
                    before[m].wait_recv()
                    if s == 3 and side != j:
                        continue
                    n = 9 + (s - 1) * 8 + m
                    part = zb.at[lax.rem(z - dz * s + NZ, NZ), core, pl.ds(2 * h, 2)]
                    cp = rcopy(part, part, zs.at[n], zr.at[n], zdev(dz, c), x)
                    cp.start()
                    cps.append(cp)
        drain.extend(cps)
        return cps

    second_pass(0)
    send_second(0)
    ring1 = ring_step(1, z_copies)
    lax.fori_loop(20, 40, fill, 0)
    ssq = lax.fori_loop(16, 32, first_pass, ssq)

    second_pass(1)
    send_second(1)
    moves(FAR, (0,))
    ring2 = ring_step(2, ring1)
    for cp in q_copies:
        cp.wait_recv()
    tosmem = pltpu.make_async_copy(rq, rqs, loc_sem.at[1])
    tosmem.start()
    ring3 = ring_step(3, ring2)
    mine.wait()
    other.wait_recv()
    tosmem.wait()
    for cp in ring3:
        cp.wait_recv()

    def pick(i, _):
        to, r = i // 4, lax.rem(i, 4)
        bid = rqs[to, 0, r]
        side = lax.rem(r, 2)
        o2[to, r] = zb[bid >> 4, (bid >> 1) & 1, (bid & 1) * 2 + (1 - side)]
        return 0

    y_copies = []
    for d in (4, 5, 3, 2, 6, 1, 7):
        to = lax.rem(rho + d, NR)
        lax.fori_loop(4 * to, 4 * to + 4, pick, 0)
        cp = rcopy(o2.at[to], rb.at[rho], ys.at[d - 1], yr.at[d - 1], z * NR + to, x)
        cp.start()
        y_copies.append(cp)
    lax.fori_loop(4 * rho, 4 * rho + 4, pick, 0)
    rb[rho] = o2[rho]
    for cp in y_copies:
        cp.wait_recv()
    drain += y_copies + q_copies

    rev = 127 - lane8

    def unpack(i, _):
        b, side, v = i // 4, lax.rem(i // 2, 2), lax.rem(i, 2)
        r = b * 2 + side
        bid = nbr[b, side]
        f_ = flip[b, side]
        lane_row = b * 8 + side * 2 + v
        src = ((bid >> 2) & 3) * 2 + v
        for h in range(3):
            q = rb[src, r, 8 * h:8 * h + 8, :]
            turned = jnp.take_along_axis(q, rev, axis=1)
            rowh = iota8 + 8 * h
            neg = jnp.logical_or(jnp.logical_or(rowh == 2, rowh == 3), jnp.logical_or(rowh == 12, rowh == 13))
            turned = jnp.where(neg, -turned, turned)
            q = jnp.where(f_ > 0, turned, q)
            for j in range(8):
                w = 8 * h + j
                if w >= 22:
                    continue
                item, k = (w // 2, w % 2)
                gst[item, pl.ds(lane_row + 4 * k, 1), :] = q[j:j + 1, :]
        sign = jnp.where(f_ > 0, -1.0, 1.0) + jnp.zeros((1, 128), F32)
        for k in range(2):
            gst[11, pl.ds(lane_row + 4 * k, 1), :] = sign
        return 0

    lax.fori_loop(0, 8, unpack, 0)

    def fix(b, sums):
        base = pl.ds(pl.multiple_of(b * 8, 8), 8)
        g0 = [gst[f, base, :] for f in range(NF)]
        gf = [gst[NF + f, base, :] for f in range(NF)]
        gm = gst[10, base, :]
        turn = gst[11, base, :]
        o = [own[f, base, :] for f in range(NF)]
        of = [own[NF + f, base, :] for f in range(NF)]
        m0 = own[10, base, :]
        m1 = own[11, base, :]
        od = [o[f] * turn if f == 1 else o[f] for f in range(NF)]
        g1, c1 = [], []
        total = zero8
        for f in range(NF):
            tf = jmul(1, od, f)
            if f == 1:
                tf = tf * turn
            g1.append(gf[f] + VISC * o[f] + sig * gm * tf)
            cf = VISC * g0[f] - sig * m0 * jmul(1, g0, f)
            c1.append(cf)
            ff = of[f] + cf
            total = total + ff * ff
        e = [pltpu.roll(cf, 127, 1) for cf in c1]
        w = [pltpu.roll(cf, 1, 1) for cf in c1]
        ok = [pltpu.roll(cf, 4, 0) for cf in c1]
        ew = [a - b_ for a, b_ in zip(e, w)]
        for f in range(NF):
            flux = jmul(0, ew, f) + sk * jmul(2, ok, f) + sig * jmul(1, g1, f)
            face = (1.0 - 6.0 * VISC) * c1[f] + VISC * (e[f] + w[f] + ok[f] + g1[f]) - m0 * flux
            near = VISC * c1[f] - sig * m1 * jmul(1, c1, f)
            face = face * SCALE
            near = near * SCALE
            cb[x, b * 2, f, 0:4, :] = face[0:4]
            cb[x, b * 2, f, 4:8, :] = near[0:4]
            cb[x, b * 2 + 1, f, 0:4, :] = face[4:8]
            cb[x, b * 2 + 1, f, 4:8, :] = near[4:8]
        s0, s1 = sums
        return s0 + jnp.where(odd == 0, total, 0.0), s1 + jnp.where(odd == 1, total, 0.0)

    ssq = lax.fori_loop(0, 2, fix, ssq)
    c_copies = []
    for d in (2, 1, 3):
        here = cb.at[x, xdev(d)]
        cp = rcopy(here, here, cs_s.at[d - 1], cs_r.at[d - 1], blk, xdev(d))
        cp.start()
        c_copies.append(cp)
    fix_moves()
    moves(EARLY, (0, 1))
    for cp in sends:
        cp.wait_recv()

    bq = x // 2
    my_last = jnp.where(bq == 0, rows[0], rows[1]) - 1
    safe_last = jnp.maximum(my_last, 1)

    def products(acc, left, right):
        res = list(acc)
        for v in range(8):
            for w in range(v + 1):
                res[pair(v, w)] = res[pair(v, w)] + left[v] * right[w]
        return tuple(res)

    def gram_tile(i, acc):
        f, t = i // 8, lax.rem(i, 8)
        row = iota8 + t * 8
        inner = jnp.logical_and(row > 1, jnp.logical_or(row < my_last - 1, row > my_last))
        vals = [gath[v // 2, x, v % 2, f, pl.ds(pl.multiple_of(t * 8, 8), 8), :] for v in range(8)]
        for v in range(8):
            near[v, f, pl.ds(pl.multiple_of(t * 8, 8), 8), :] = vals[v]
        return products(acc, [jnp.where(inner, q, 0.0) for q in vals], vals)

    grams = lax.fori_loop(0, 40, gram_tile, tuple(zero8 for _ in range(36)))

    def edges(i, _):
        f, v = i // 8, lax.rem(i, 8)
        for j, r in enumerate((0, safe_last, 1, safe_last - 1)):
            edge[v // 2, f, pl.ds(2 * j + lax.rem(v, 2), 1), :] = near[v, f, pl.ds(r, 1), :]
        return 0

    lax.fori_loop(0, 40, edges, 0)
    for cp in c_copies:
        cp.wait_recv()
    drain += sends + c_copies
    odd_row = (iota8 & 1) == 1

    def gram_edge(f, acc):
        vals = []
        for src in range(NX):
            both = edge[src, f] + cb[src, x, f]
            vals.append(jnp.where(odd_row, 0.0, both))
            vals.append(jnp.where(odd_row, 0.0, pltpu.roll(both, 7, 0)))
        return products(acc, vals, vals)

    grams = lax.fori_loop(0, NF, gram_edge, grams)
    gacc[...] = jnp.zeros((128, 128), F32)
    for n in range(36):
        gacc[n:n + 1, :] = jnp.sum(grams[n], axis=0, keepdims=True)
    for v in range(2):
        gacc[pl.ds(36 + 2 * x + v, 1), :] = jnp.sum(ssq[v], axis=0, keepdims=True)
    ones8 = jnp.ones((8, 128), F32)
    ar[...] = lax.dot_general(ones8, gacc[...], (((1,), (1,)), ((), ())), precision=HI, preferred_element_type=F32)[0:1, :]

    def exchange(src, buf, me, first, dev, then):
        buf[me] = src[...]
        cps = []
        for d in range(1, 16):
            b_, x_ = dev(d)
            cp = rcopy(src, buf.at[me], as_s.at[first + d - 1], as_r.at[first + d - 1], b_, x_)
            cp.start()
            cps.append(cp)
        then()
        for cp in cps:
            cp.wait_recv()
        drain.extend(cps)
        tot = [buf[j] for j in range(16)]
        while len(tot) > 1:
            tot = [a + b_ for a, b_ in zip(tot[::2], tot[1::2])]
        return tot[0]

    ar2[...] = exchange(ar, arx, z * NC + c, 0, zc, lambda: None)
    ar3 = exchange(ar2, ary, (rho // NC) * NX + x, 15, yx, lambda: moves(FAR, (1,)))

    r48 = lax.broadcasted_iota(jnp.int32, (48, 128), 0)
    l48 = lax.broadcasted_iota(jnp.int32, (48, 128), 1)
    spread = jnp.where(r48 == l48, jnp.broadcast_to(ar3[0:1, :], (48, 128)), 0.0)
    spl[...] = jnp.dot(spread, jnp.ones((128, 128), F32), precision=HI, preferred_element_type=F32)

    def entry(n):
        return spl[n:n + 1, :]

    s = [1.0 / (SCALE * jnp.sqrt(entry(36 + v) + EPS)) for v in range(8)]
    low = {}
    inv = []
    for j in range(8):
        a = entry(pair(j, j)) * s[j] * s[j]
        for k in range(j):
            a = a - low[j, k] * low[j, k]
        inv.append(lax.rsqrt(a))
        low[j, j] = a * inv[j]
        for i in range(j + 1, 8):
            a = entry(pair(i, j)) * s[i] * s[j]
            for k in range(j):
                a = a - low[i, k] * low[j, k]
            low[i, j] = a * inv[j]
    xx = {}
    for j in range(8):
        xx[j, j] = inv[j]
        for i in range(j + 1, 8):
            a = low[i, j] * xx[j, j]
            for k in range(j + 1, i):
                a = a + low[i, k] * xx[k, j]
            xx[i, j] = -a * inv[i]
    upper = zero8
    for i in range(8):
        for j in range(i + 1):
            mix[pair(i, j)] = jnp.broadcast_to(xx[i, j] * s[j], (8, 128))
            upper = jnp.where(jnp.logical_and(iota8 == j, lane8 == i), jnp.broadcast_to(low[i, j], (8, 128)), upper)
    fac[...] = upper[:, 0:8]

    def combine(q, outs, put):
        top = max(outs) // 2 + 1

        def body(f, _):
            last = rows[q // 2] - 1
            fixes = []
            for o in outs:
                tot = zero8
                for src in range(o // 2 + 1):
                    lo = mix[pair(o, 2 * src)]
                    hi = mix[pair(o, 2 * src + 1)] if 2 * src + 1 <= o else 0.0
                    tot = tot + jnp.where(odd_row, hi, lo) * cb[src, q, f]
                tot = tot + pltpu.roll(tot, 7, 0)
                fixes.append([jnp.broadcast_to(tot[r:r + 1], (8, 128)) for r in (0, 2, 4, 6)])
            for t in range(8):
                vals = [gath[w // 2, q, w % 2, f, 8 * t:8 * t + 8, :] for w in range(2 * top)]
                row = iota8 + 8 * t
                for n, o in enumerate(outs):
                    a = mix[pair(o, 0)] * vals[0]
                    for w in range(1, o + 1):
                        a = a + mix[pair(o, w)] * vals[w]
                    if t == 0:
                        a = a + jnp.where(row == 0, fixes[n][0], 0.0) + jnp.where(row == 1, fixes[n][2], 0.0)
                    if t >= 3:
                        a = a + jnp.where(row == last, fixes[n][1], 0.0) + jnp.where(row == last - 1, fixes[n][3], 0.0)
                    put(n, f, t, a)
            return 0

        lax.fori_loop(0, NF, body, 0)

    def home(i, v, q, to):
        return rcopy(res.at[i, v], out.at[v, q // 2, :, q % 2], os.at[i, v], orr.at[i, v], blk, jnp.int32(to))

    def own_copy(v, q):
        there = out.at[v, q // 2, :, q % 2]
        return pltpu.make_async_copy(bas.at[v, q // 2, :, q % 2], there, out_sem.at[v, q])

    def finish(g):
        beside = [(i, (g + d) % NX) for i, d in ((0, 1), (1, -1)) if (g + d) % NX > 0]
        for i, to in beside:
            def put(n, f, t, a, i=i):
                res[i, n, f, 8 * t:8 * t + 8, :] = a

            combine(g, [2 * to, 2 * to + 1], put)
            for v in range(2):
                home(i, v, g, to).start()
        mine_q = [g, (g + 2) % NX] if g > 0 else [0, 1, 2, 3]
        for q in mine_q:
            if q != g:
                for n in range(len(MOVES)):
                    if MOVES[n][1:] == (q, g):
                        move(n, 0).wait_recv()
                        move(n, 1).wait_recv()
                        fix_move(n).wait_recv()

            def put_own(n, f, t, a, q=q):
                bas[n, q // 2, f, q % 2, 8 * t:8 * t + 8, :] = a

            combine(q, [2 * g, 2 * g + 1], put_own)
            for v in range(2):
                own_copy(v, q).start()
        for n in range(len(MOVES)):
            if MOVES[n][0] == g:
                move(n, 0).wait_send()
                move(n, 1).wait_send()
                fix_move(n).wait_send()
        for q in mine_q:
            for v in range(2):
                own_copy(v, q).wait()
        for i, to in beside:
            for v in range(2):
                home(i, v, g, to).wait_send()
        if g > 0:
            for i, frm in ((0, (g - 1) % NX), (1, (g + 1) % NX)):
                for v in range(2):
                    home(i, v, frm, g).wait_recv()

    for cp in drain:
        cp.wait_send()
    for g in range(NX):
        @pl.when(x == g)
        def _():
            finish(g)


def per_device(vectors, metric, jacobians, block_rows, neighbours, flipped):
    vm = pl.BlockSpec(memory_space=pltpu.VMEM)
    hbm = pl.BlockSpec(memory_space=pltpu.HBM)
    dma = pltpu.SemaphoreType.DMA
    return pl.pallas_call(
        kernel,
        out_shape=(pltpu.VMEM(vectors.shape, F32), jax.ShapeDtypeStruct((8, 8), F32)),
        in_specs=[hbm] * 6,
        out_specs=(pl.BlockSpec(memory_space=pl.ANY), vm),
        scratch_shapes=[
            pltpu.VMEM(vectors.shape, F32),
            pltpu.VMEM(metric.shape, F32),
            pltpu.SMEM((NF, 3, NF), F32),
            pltpu.SMEM((2,), jnp.int32),
            pltpu.SMEM((2, 2), jnp.int32),
            pltpu.SMEM((2, 2), jnp.int32),
            pltpu.VMEM((2, 2, NF, 2, 80, 128), F32),
            pltpu.VMEM((2, 2, NF, 2, 80, 128), F32),
            pltpu.VMEM((4, 4, 2, NF, 64, 128), F32),
            pltpu.VMEM(vectors.shape, F32),
            pltpu.VMEM((2, 2, NF, 64, 128), F32),
            pltpu.VMEM((2, 4, 24, 128), F32),
            pltpu.VMEM((NZ, NC, 4, 24, 128), F32),
            pltpu.VMEM((NR, 8, 128), jnp.int32),
            pltpu.SMEM((NR, 8, 128), jnp.int32),
            pltpu.VMEM((NR, 4, 24, 128), F32),
            pltpu.VMEM((NR, 4, 24, 128), F32),
            pltpu.VMEM((12, 16, 128), F32),
            pltpu.VMEM((12, 16, 128), F32),
            pltpu.VMEM((4, 4, NF, 8, 128), F32),
            pltpu.VMEM((4, NF, 8, 128), F32),
            pltpu.VMEM((8, NF, 64, 128), F32),
            pltpu.VMEM((128, 128), F32),
            pltpu.VMEM((1, 128), F32),
            pltpu.VMEM((1, 128), F32),
            pltpu.VMEM((16, 1, 128), F32),
            pltpu.VMEM((16, 1, 128), F32),
            pltpu.VMEM((48, 128), F32),
            pltpu.VMEM((36, 8, 128), F32),
            dma((2,)), dma((5,)), dma((4,)),
            dma((2, 3)), dma((2, 3)),
            dma((33,)), dma((33,)),
            dma((7,)), dma((7,)),
            dma((7,)), dma((7,)),
            dma((3,)), dma((3,)),
            dma((30,)), dma((30,)),
            dma((len(MOVES), 2)), dma((len(MOVES), 2)),
            dma((6,)), dma((6,)),
            dma((2, 2)), dma((2, 2)),
            dma((2, 4)),
        ],
        compiler_params=pltpu.CompilerParams(collective_id=0, has_side_effects=True, vmem_limit_bytes=60 * 1024 * 1024),
        cost_estimate=pl.CostEstimate(flops=60_000_000, bytes_accessed=4_000_000, transcendentals=0),
    )(vectors, metric, jnp.transpose(jacobians, (1, 0, 2)), block_rows, neighbours, flipped)


def solution(mesh):
    wide = P("vec", "blk", None, None, None, None)
    in_specs = (wide, P("blk", None, None, None), P(), P("blk"), P("blk", None), P("blk", None))
    return jax.shard_map(per_device, mesh=mesh, in_specs=in_specs, out_specs=(wide, P()), check_vma=False)
```

```python
import jax
import jax.numpy as jnp
from jax import lax
from jax.experimental import pallas as pl
from jax.experimental.pallas import tpu as pltpu
from jax.sharding import PartitionSpec as P

MESH = pl.DeviceIdType.MESH
F32 = jnp.float32
HI = lax.Precision.HIGHEST
NF = 5
NZ, NY, NC, NX = 8, 4, 2, 4
NR = NY * NC
VISC = 0.1
EPS = 1e-06
SCALE = 1024.0


EARLY = [(1, 0, 2), (0, 3, 1), (0, 1, 3), (2, 1, 3)]
FAR = [(0, 0, 2), (1, 1, 3)]
MOVES = EARLY + FAR


def pair(v, w):
    return v * (v + 1) // 2 + w


def kernel(vec_h, met_h, jac_h, rows_h, nbr_h, flip_h, out, fac,
           vec, met, jac, rows, nbr, flip, st, fi, gath, bas, res, pay, zb, rq, rqs, o2, rb, own, gst, cb, edge, near, gacc, ar, ar2, arx, ary, spl, mix,
           loc_sem, in_sem, vec_sem, xs, xr, zs, zr, qs, qr, ys, yr, cs_s, cs_r, as_s, as_r, ws, wr, cs2_s, cs2_r, os, orr, out_sem):
    blk = lax.axis_index("blk")
    x = lax.axis_index("vec")
    z = blk // NR
    rho = lax.rem(blk, NR)
    c = lax.rem(blk, NC)
    col = lax.rem(blk, NR)

    def zdev(dz, core):
        zz = lax.rem(z + dz + NZ, NZ)
        return zz * NR + (rho - c) + core

    small = [pltpu.make_async_copy(h, d, in_sem.at[n]) for n, (h, d) in enumerate(
        ((rows_h, rows), (jac_h, jac), (nbr_h, nbr), (flip_h, flip), (met_h, met)))]
    big = [pltpu.make_async_copy(vec_h.at[n // 2, n % 2], vec.at[n // 2, n % 2], vec_sem.at[n]) for n in range(4)]
    for cp in small[:1] + big + small[1:]:
        cp.start()

    bar = pltpu.get_barrier_semaphore()
    def xdev(d):
        return lax.rem(x + d + NX, NX)

    def zc(d):
        m = lax.rem(z * NC + c + d, NZ * NC)
        return (m // NC) * NR + (rho - c) + lax.rem(m, NC), x

    def yx(d):
        m = lax.rem((rho // NC) * NX + x + d, (NR // NC) * NX)
        return z * NR + (m // NX) * NC + c, lax.rem(m, NX)

    def yc(d):
        return z * NR + lax.rem(rho + d, NR), x

    partners = [(zdev(dz, core), x) for dz in (1, -1) for core in range(2)] + [yc(d) for d in range(1, NR)]
    partners += [(blk, xdev(d)) for d in range(1, NX)]
    for b_, x_ in partners:
        pl.semaphore_signal(bar, inc=1, device_id={"blk": b_, "vec": x_}, device_id_type=MESH)
    n_part = len(partners)

    def rcopy(src, dst, ssem, rsem, b_, x_):
        return pltpu.make_async_remote_copy(src_ref=src, dst_ref=dst, send_sem=ssem, recv_sem=rsem,
                                            device_id={"blk": b_, "vec": x_}, device_id_type=MESH)

    iota64 = lax.broadcasted_iota(jnp.int32, (64, 128), 0)
    iota8 = lax.broadcasted_iota(jnp.int32, (8, 128), 0)
    lane8 = lax.broadcasted_iota(jnp.int32, (8, 128), 1)
    zero8 = jnp.zeros((8, 128), F32)

    for cp in small + big:
        cp.wait()

    sig = jnp.where((iota8 >> 1) & 1 == 0, -1.0, 1.0)
    sk = jnp.where(iota8 < 4, 1.0, -1.0)
    odd = iota8 & 1

    def jmul(d, g_, f):
        acc = jac[f, d, 0] * g_[0]
        for g in range(1, NF):
            acc = acc + jac[f, d, g] * g_[g]
        return acc

    def faces(i, _):
        b, side, v = i // 4, lax.rem(i // 2, 2), lax.rem(i, 2)
        last = jnp.maximum(rows[b] - 1, 1)
        r = jnp.where(side == 0, 0, last)
        adj = jnp.where(side == 0, 1, last - 1)
        slot = b * 2 + side
        lane_row = b * 8 + side * 2 + v
        for f in range(NF):
            for k in range(2):
                a = vec[v, b, f, k, pl.ds(r, 1), :]
                pay[v, slot, f * 2 + k:f * 2 + k + 1, :] = a
                own[f, pl.ds(lane_row + 4 * k, 1), :] = a
                gst[f, pl.ds(lane_row + 4 * k, 1), :] = vec[v, b, f, k, pl.ds(adj, 1), :]
        for k in range(2):
            m = met[b, k, pl.ds(r, 1), :]
            pay[v, slot, 20 + k:21 + k, :] = m
            pay[v, slot, 22 + k:23 + k, :] = m
            own[10, pl.ds(lane_row + 4 * k, 1), :] = m
            own[11, pl.ds(lane_row + 4 * k, 1), :] = met[b, k, pl.ds(adj, 1), :]
        return 0

    lax.fori_loop(0, 8, faces, 0)

    def face_step(b, _):
        base = pl.ds(pl.multiple_of(b * 8, 8), 8)
        q = [own[f, base, :] for f in range(NF)]
        inside = [gst[f, base, :] for f in range(NF)]
        m0 = own[10, base, :]
        e = [pltpu.roll(a, 127, 1) for a in q]
        w = [pltpu.roll(a, 1, 1) for a in q]
        ok = [pltpu.roll(a, 4, 0) for a in q]
        ew = [a - b_ for a, b_ in zip(e, w)]
        for f in range(NF):
            flux = jmul(0, ew, f) + sk * jmul(2, ok, f) - sig * jmul(1, inside, f)
            own[NF + f, base, :] = (1.0 - 6.0 * VISC) * q[f] + VISC * (e[f] + w[f] + ok[f] + inside[f]) - m0 * flux
        return 0

    lax.fori_loop(0, 2, face_step, 0)

    def pack(i, _):
        b, side, v = i // 4, lax.rem(i // 2, 2), lax.rem(i, 2)
        lane_row = b * 8 + side * 2 + v
        for f in range(NF):
            for k in range(2):
                pay[v, b * 2 + side, 10 + f * 2 + k:11 + f * 2 + k, :] = own[NF + f, pl.ds(lane_row + 4 * k, 1), :]
        return 0

    lax.fori_loop(0, 8, pack, 0)
    req = jnp.where(lane8 == 0, nbr[0, 0], jnp.where(lane8 == 1, nbr[0, 1], jnp.where(lane8 == 2, nbr[1, 0], nbr[1, 1])))
    rq[rho] = req

    pl.semaphore_wait(bar, n_part)

    mine = pltpu.make_async_copy(pay.at[c], zb.at[z, c], loc_sem.at[0])
    mine.start()
    z_copies = []
    for j in range(2):
        core = lax.rem(c + j, NC)
        for h in range(2):
            for side, dz in ((0, 1), (1, -1)):
                n = j * 4 + h * 2 + side
                half = pl.ds(2 * h, 2)
                cp = rcopy(pay.at[core, half], zb.at[z, c, half], zs.at[n], zr.at[n], zdev(dz, core), x)
                cp.start()
                z_copies.append(cp)
    other = rcopy(pay.at[1 - c], zb.at[z, c], zs.at[8], zr.at[8], zdev(0, 1 - c), x)
    other.start()
    q_copies = []
    for d in range(1, NR):
        cp = rcopy(rq.at[rho], rq.at[rho], qs.at[d - 1], qr.at[d - 1], z * NR + lax.rem(rho + d, NR), x)
        cp.start()
        q_copies.append(cp)

    def fill(i, _):
        vb = i // 10
        v, b = vb // 2, lax.rem(vb, 2)
        fk = lax.rem(i, 10)
        f, k = fk // 2, lax.rem(fk, 2)
        q = vec[v, b, f, k]
        st[v, b, f, k, 8:72, :] = jnp.where(iota64 < rows[b], q, 0.0)
        st[v, b, f, k, 0:8, :] = zero8
        st[v, b, f, k, 72:80, :] = zero8
        fi[v, b, f, k, 0:8, :] = zero8
        fi[v, b, f, k, 72:80, :] = zero8
        return 0

    lax.fori_loop(0, 20, fill, 0)

    def advance_tile(src, v, b, t, scale, store):
        r0 = pl.multiple_of(t * 8, 8)
        alive = (iota8 + r0) < rows[b]
        qs_, d0, d1, base = [], [], [], []
        for k in range(2):
            qk = [src[v, b, f, k, pl.ds(r0 + 8, 8), :] for f in range(NF)]
            qs_.append(qk)
        for k in range(2):
            a0, a1, ab = [], [], []
            for f in range(NF):
                q = qs_[k][f]
                e = pltpu.roll(q, 127, 1)
                w = pltpu.roll(q, 1, 1)
                n = src[v, b, f, k, pl.ds(r0 + 9, 8), :]
                s = src[v, b, f, k, pl.ds(r0 + 7, 8), :]
                a0.append(e - w)
                a1.append(n - s)
                ab.append((scale * (1.0 - 6.0 * VISC)) * q + (scale * VISC) * ((e + w) + (n + s) + qs_[1 - k][f]))
            d0.append(a0)
            d1.append(a1)
            base.append(ab)
        mk = [met[b, k, pl.ds(r0, 8), :] * scale for k in range(2)]
        for f in range(NF):
            c0 = [jac[f, 0, g] for g in range(NF)]
            c1 = [jac[f, 1, g] for g in range(NF)]
            c2 = [jac[f, 2, g] for g in range(NF)]
            for k in range(2):
                acc = c0[0] * d0[k][0] + c1[0] * d1[k][0]
                oth = c2[0] * qs_[1 - k][0]
                for g in range(1, NF):
                    acc = acc + c0[g] * d0[k][g] + c1[g] * d1[k][g]
                    oth = oth + c2[g] * qs_[1 - k][g]
                flux = acc + oth if k == 0 else acc - oth
                store(f, k, jnp.where(alive, base[k][f] - mk[k] * flux, 0.0))

    def first_pass(i, sums):
        vb, t = i // 8, lax.rem(i, 8)
        v, b = vb // 2, lax.rem(vb, 2)
        r0 = t * 8
        row = iota8 + r0
        inner = jnp.logical_and(row > 0, row != rows[b] - 1)
        box = [jnp.zeros((8, 128), F32)]

        def store(f, k, val):
            fi[v, b, f, k, pl.ds(pl.multiple_of(r0 + 8, 8), 8), :] = val
            box[0] = box[0] + val * val

        advance_tile(st, v, b, t, 1.0, store)
        sq = jnp.where(inner, box[0], 0.0)
        s0, s1 = sums
        return s0 + jnp.where(v == 0, sq, 0.0), s1 + jnp.where(v == 1, sq, 0.0)

    ssq = lax.fori_loop(0, 16, first_pass, (zero8, zero8))

    def second_pass(v):
        def body(i, _):
            b, t = i // 8, lax.rem(i, 8)

            def store(f, k, val):
                gath[x, b * 2 + k, v, f, pl.ds(pl.multiple_of(t * 8, 8), 8), :] = val

            advance_tile(fi, v, b, t, SCALE, store)
            return 0

        lax.fori_loop(0, 16, body, 0)

    sends = []

    def send_second(v):
        for d in (2, 1, 3):
            here = gath.at[x, xdev(d), v]
            cp = rcopy(here, here, xs.at[v, d - 1], xr.at[v, d - 1], blk, xdev(d))
            cp.start()
            sends.append(cp)

    def move(n, v):
        src, q, to = MOVES[n]
        part = gath.at[src, q, v]
        return rcopy(part, part, ws.at[n, v], wr.at[n, v], blk, jnp.int32(to))

    def fix_move(n):
        src, q, to = MOVES[n]
        part = cb.at[src, q]
        return rcopy(part, part, cs2_s.at[n], cs2_r.at[n], blk, jnp.int32(to))

    def moves(which, vs):
        for n in range(len(MOVES)):
            if MOVES[n] in which:
                @pl.when(x == MOVES[n][0])
                def _():
                    for v in vs:
                        move(n, v).start()

    def fix_moves():
        for n in range(len(MOVES)):
            @pl.when(x == MOVES[n][0])
            def _():
                fix_move(n).start()

    drain = z_copies + [other]

    def ring_step(s, before):
        cps = []
        for j in range(2):
            core = lax.rem(c + j, NC)
            for h in range(2):
                for side, dz in ((0, 1), (1, -1)):
                    m = j * 4 + h * 2 + side
                    before[m].wait_recv()
                    if s == 3 and side != j:
                        continue
                    n = 9 + (s - 1) * 8 + m
                    part = zb.at[lax.rem(z - dz * s + NZ, NZ), core, pl.ds(2 * h, 2)]
                    cp = rcopy(part, part, zs.at[n], zr.at[n], zdev(dz, c), x)
                    cp.start()
                    cps.append(cp)
        drain.extend(cps)
        return cps

    second_pass(0)
    send_second(0)
    ring1 = ring_step(1, z_copies)
    lax.fori_loop(20, 40, fill, 0)
    ssq = lax.fori_loop(16, 32, first_pass, ssq)

    second_pass(1)
    send_second(1)
    moves(FAR, (0,))
    ring2 = ring_step(2, ring1)
    for cp in q_copies:
        cp.wait_recv()
    tosmem = pltpu.make_async_copy(rq, rqs, loc_sem.at[1])
    tosmem.start()
    ring3 = ring_step(3, ring2)
    mine.wait()
    other.wait_recv()
    tosmem.wait()
    for cp in ring3:
        cp.wait_recv()

    def pick(i, _):
        to, r = i // 4, lax.rem(i, 4)
        bid = rqs[to, 0, r]
        side = lax.rem(r, 2)
        o2[to, r] = zb[bid >> 4, (bid >> 1) & 1, (bid & 1) * 2 + (1 - side)]
        return 0

    y_copies = []
    for d in (4, 5, 3, 2, 6, 1, 7):
        to = lax.rem(rho + d, NR)
        lax.fori_loop(4 * to, 4 * to + 4, pick, 0)
        cp = rcopy(o2.at[to], rb.at[rho], ys.at[d - 1], yr.at[d - 1], z * NR + to, x)
        cp.start()
        y_copies.append(cp)
    lax.fori_loop(4 * rho, 4 * rho + 4, pick, 0)
    rb[rho] = o2[rho]
    for cp in y_copies:
        cp.wait_recv()
    drain += y_copies + q_copies

    rev = 127 - lane8

    def unpack(i, _):
        b, side, v = i // 4, lax.rem(i // 2, 2), lax.rem(i, 2)
        r = b * 2 + side
        bid = nbr[b, side]
        f_ = flip[b, side]
        lane_row = b * 8 + side * 2 + v
        src = ((bid >> 2) & 3) * 2 + v
        for h in range(3):
            q = rb[src, r, 8 * h:8 * h + 8, :]
            turned = jnp.take_along_axis(q, rev, axis=1)
            rowh = iota8 + 8 * h
            neg = jnp.logical_or(jnp.logical_or(rowh == 2, rowh == 3), jnp.logical_or(rowh == 12, rowh == 13))
            turned = jnp.where(neg, -turned, turned)
            q = jnp.where(f_ > 0, turned, q)
            for j in range(8):
                w = 8 * h + j
                if w >= 22:
                    continue
                item, k = (w // 2, w % 2)
                gst[item, pl.ds(lane_row + 4 * k, 1), :] = q[j:j + 1, :]
        sign = jnp.where(f_ > 0, -1.0, 1.0) + jnp.zeros((1, 128), F32)
        for k in range(2):
            gst[11, pl.ds(lane_row + 4 * k, 1), :] = sign
        return 0

    lax.fori_loop(0, 8, unpack, 0)

    def fix(b, sums):
        base = pl.ds(pl.multiple_of(b * 8, 8), 8)
        g0 = [gst[f, base, :] for f in range(NF)]
        gf = [gst[NF + f, base, :] for f in range(NF)]
        gm = gst[10, base, :]
        turn = gst[11, base, :]
        o = [own[f, base, :] for f in range(NF)]
        of = [own[NF + f, base, :] for f in range(NF)]
        m0 = own[10, base, :]
        m1 = own[11, base, :]
        od = [o[f] * turn if f == 1 else o[f] for f in range(NF)]
        g1, c1 = [], []
        total = zero8
        for f in range(NF):
            tf = jmul(1, od, f)
            if f == 1:
                tf = tf * turn
            g1.append(gf[f] + VISC * o[f] + sig * gm * tf)
            cf = VISC * g0[f] - sig * m0 * jmul(1, g0, f)
            c1.append(cf)
            ff = of[f] + cf
            total = total + ff * ff
        e = [pltpu.roll(cf, 127, 1) for cf in c1]
        w = [pltpu.roll(cf, 1, 1) for cf in c1]
        ok = [pltpu.roll(cf, 4, 0) for cf in c1]
        ew = [a - b_ for a, b_ in zip(e, w)]
        for f in range(NF):
            flux = jmul(0, ew, f) + sk * jmul(2, ok, f) + sig * jmul(1, g1, f)
            face = (1.0 - 6.0 * VISC) * c1[f] + VISC * (e[f] + w[f] + ok[f] + g1[f]) - m0 * flux
            near = VISC * c1[f] - sig * m1 * jmul(1, c1, f)
            face = face * SCALE
            near = near * SCALE
            cb[x, b * 2, f, 0:4, :] = face[0:4]
            cb[x, b * 2, f, 4:8, :] = near[0:4]
            cb[x, b * 2 + 1, f, 0:4, :] = face[4:8]
            cb[x, b * 2 + 1, f, 4:8, :] = near[4:8]
        s0, s1 = sums
        return s0 + jnp.where(odd == 0, total, 0.0), s1 + jnp.where(odd == 1, total, 0.0)

    ssq = lax.fori_loop(0, 2, fix, ssq)
    c_copies = []
    for d in (2, 1, 3):
        here = cb.at[x, xdev(d)]
        cp = rcopy(here, here, cs_s.at[d - 1], cs_r.at[d - 1], blk, xdev(d))
        cp.start()
        c_copies.append(cp)
    fix_moves()
    moves(EARLY, (0, 1))
    for cp in sends:
        cp.wait_recv()

    bq = x // 2
    my_last = jnp.where(bq == 0, rows[0], rows[1]) - 1
    safe_last = jnp.maximum(my_last, 1)

    def products(acc, left, right):
        res = list(acc)
        for v in range(8):
            for w in range(v + 1):
                res[pair(v, w)] = res[pair(v, w)] + left[v] * right[w]
        return tuple(res)

    def gram_tile(i, acc):
        f, t = i // 8, lax.rem(i, 8)
        row = iota8 + t * 8
        inner = jnp.logical_and(row > 1, jnp.logical_or(row < my_last - 1, row > my_last))
        vals = [gath[v // 2, x, v % 2, f, pl.ds(pl.multiple_of(t * 8, 8), 8), :] for v in range(8)]
        for v in range(8):
            near[v, f, pl.ds(pl.multiple_of(t * 8, 8), 8), :] = vals[v]
        return products(acc, [jnp.where(inner, q, 0.0) for q in vals], vals)

    grams = lax.fori_loop(0, 40, gram_tile, tuple(zero8 for _ in range(36)))

    def edges(i, _):
        f, v = i // 8, lax.rem(i, 8)
        for j, r in enumerate((0, safe_last, 1, safe_last - 1)):
            edge[v // 2, f, pl.ds(2 * j + lax.rem(v, 2), 1), :] = near[v, f, pl.ds(r, 1), :]
        return 0

    lax.fori_loop(0, 40, edges, 0)
    for cp in c_copies:
        cp.wait_recv()
    drain += sends + c_copies
    odd_row = (iota8 & 1) == 1

    def gram_edge(f, acc):
        vals = []
        for src in range(NX):
            both = edge[src, f] + cb[src, x, f]
            vals.append(jnp.where(odd_row, 0.0, both))
            vals.append(jnp.where(odd_row, 0.0, pltpu.roll(both, 7, 0)))
        return products(acc, vals, vals)

    grams = lax.fori_loop(0, NF, gram_edge, grams)
    gacc[...] = jnp.zeros((128, 128), F32)
    for n in range(36):
        gacc[n:n + 1, :] = jnp.sum(grams[n], axis=0, keepdims=True)
    for v in range(2):
        gacc[pl.ds(36 + 2 * x + v, 1), :] = jnp.sum(ssq[v], axis=0, keepdims=True)
    ones8 = jnp.ones((8, 128), F32)
    ar[...] = lax.dot_general(ones8, gacc[...], (((1,), (1,)), ((), ())), precision=HI, preferred_element_type=F32)[0:1, :]

    def exchange(src, buf, me, first, dev, then):
        buf[me] = src[...]
        cps = []
        for d in range(1, 16):
            b_, x_ = dev(d)
            cp = rcopy(src, buf.at[me], as_s.at[first + d - 1], as_r.at[first + d - 1], b_, x_)
            cp.start()
            cps.append(cp)
        then()
        for cp in cps:
            cp.wait_recv()
        drain.extend(cps)
        tot = [buf[j] for j in range(16)]
        while len(tot) > 1:
            tot = [a + b_ for a, b_ in zip(tot[::2], tot[1::2])]
        return tot[0]

    ar2[...] = exchange(ar, arx, z * NC + c, 0, zc, lambda: None)
    ar3 = exchange(ar2, ary, (rho // NC) * NX + x, 15, yx, lambda: moves(FAR, (1,)))

    r48 = lax.broadcasted_iota(jnp.int32, (48, 128), 0)
    l48 = lax.broadcasted_iota(jnp.int32, (48, 128), 1)
    spread = jnp.where(r48 == l48, jnp.broadcast_to(ar3[0:1, :], (48, 128)), 0.0)
    spl[...] = jnp.dot(spread, jnp.ones((128, 128), F32), precision=HI, preferred_element_type=F32)

    def entry(n):
        return spl[n:n + 1, :]

    s = [1.0 / (SCALE * jnp.sqrt(entry(36 + v) + EPS)) for v in range(8)]
    low = {}
    inv = []
    for j in range(8):
        a = entry(pair(j, j)) * s[j] * s[j]
        for k in range(j):
            a = a - low[j, k] * low[j, k]
        inv.append(lax.rsqrt(a))
        low[j, j] = a * inv[j]
        for i in range(j + 1, 8):
            a = entry(pair(i, j)) * s[i] * s[j]
            for k in range(j):
                a = a - low[i, k] * low[j, k]
            low[i, j] = a * inv[j]
    xx = {}
    for j in range(8):
        xx[j, j] = inv[j]
        for i in range(j + 1, 8):
            a = low[i, j] * xx[j, j]
            for k in range(j + 1, i):
                a = a + low[i, k] * xx[k, j]
            xx[i, j] = -a * inv[i]
    upper = zero8
    for i in range(8):
        for j in range(i + 1):
            mix[pair(i, j)] = jnp.broadcast_to(xx[i, j] * s[j], (8, 128))
            upper = jnp.where(jnp.logical_and(iota8 == j, lane8 == i), jnp.broadcast_to(low[i, j], (8, 128)), upper)
    fac[...] = upper[:, 0:8]

    def combine(q, outs, put):
        top = max(outs) // 2 + 1

        def body(f, _):
            last = rows[q // 2] - 1
            fixes = []
            for o in outs:
                tot = zero8
                for src in range(o // 2 + 1):
                    lo = mix[pair(o, 2 * src)]
                    hi = mix[pair(o, 2 * src + 1)] if 2 * src + 1 <= o else 0.0
                    tot = tot + jnp.where(odd_row, hi, lo) * cb[src, q, f]
                tot = tot + pltpu.roll(tot, 7, 0)
                fixes.append([jnp.broadcast_to(tot[r:r + 1], (8, 128)) for r in (0, 2, 4, 6)])
            for t in range(8):
                vals = [gath[w // 2, q, w % 2, f, 8 * t:8 * t + 8, :] for w in range(2 * top)]
                row = iota8 + 8 * t
                for n, o in enumerate(outs):
                    a = mix[pair(o, 0)] * vals[0]
                    for w in range(1, o + 1):
                        a = a + mix[pair(o, w)] * vals[w]
                    if t == 0:
                        a = a + jnp.where(row == 0, fixes[n][0], 0.0) + jnp.where(row == 1, fixes[n][2], 0.0)
                    if t >= 3:
                        a = a + jnp.where(row == last, fixes[n][1], 0.0) + jnp.where(row == last - 1, fixes[n][3], 0.0)
                    put(n, f, t, a)
            return 0

        lax.fori_loop(0, NF, body, 0)

    def home(i, v, q, to):
        return rcopy(res.at[i, v], out.at[v, q // 2, :, q % 2], os.at[i, v], orr.at[i, v], blk, jnp.int32(to))

    def own_copy(v, q):
        there = out.at[v, q // 2, :, q % 2]
        return pltpu.make_async_copy(bas.at[v, q // 2, :, q % 2], there, out_sem.at[v, q])

    def targets(g):
        beside = [(i, (g + d) % NX) for i, d in ((0, 1), (1, -1)) if (g + d) % NX > 0]
        return beside, [g, (g + 2) % NX] if g > 0 else [0, 1, 2, 3]

    def finish(g):
        beside, mine_q = targets(g)
        for i, to in beside:
            def put(n, f, t, a, i=i):
                res[i, n, f, 8 * t:8 * t + 8, :] = a

            combine(g, [2 * to, 2 * to + 1], put)
            for v in range(2):
                home(i, v, g, to).start()
        for q in mine_q:
            if q != g:
                for n in range(len(MOVES)):
                    if MOVES[n][1:] == (q, g):
                        move(n, 0).wait_recv()
                        move(n, 1).wait_recv()
                        fix_move(n).wait_recv()

            def put_own(n, f, t, a, q=q):
                bas[n, q // 2, f, q % 2, 8 * t:8 * t + 8, :] = a

            combine(q, [2 * g, 2 * g + 1], put_own)
            for v in range(2):
                own_copy(v, q).start()

    def settle(g):
        beside, mine_q = targets(g)
        for n in range(len(MOVES)):
            if MOVES[n][0] == g:
                move(n, 0).wait_send()
                move(n, 1).wait_send()
                fix_move(n).wait_send()
        for q in mine_q:
            for v in range(2):
                own_copy(v, q).wait()
        for i, to in beside:
            for v in range(2):
                home(i, v, g, to).wait_send()
        if g > 0:
            for i, frm in ((0, (g - 1) % NX), (1, (g + 1) % NX)):
                for v in range(2):
                    home(i, v, frm, g).wait_recv()

    for g in range(NX):
        @pl.when(x == g)
        def _():
            finish(g)

    for cp in drain:
        cp.wait_send()
    for g in range(NX):
        @pl.when(x == g)
        def _():
            settle(g)


def per_device(vectors, metric, jacobians, block_rows, neighbours, flipped):
    vm = pl.BlockSpec(memory_space=pltpu.VMEM)
    hbm = pl.BlockSpec(memory_space=pltpu.HBM)
    dma = pltpu.SemaphoreType.DMA
    return pl.pallas_call(
        kernel,
        out_shape=(pltpu.VMEM(vectors.shape, F32), jax.ShapeDtypeStruct((8, 8), F32)),
        in_specs=[hbm] * 6,
        out_specs=(pl.BlockSpec(memory_space=pl.ANY), vm),
        scratch_shapes=[
            pltpu.VMEM(vectors.shape, F32),
            pltpu.VMEM(metric.shape, F32),
            pltpu.SMEM((NF, 3, NF), F32),
            pltpu.SMEM((2,), jnp.int32),
            pltpu.SMEM((2, 2), jnp.int32),
            pltpu.SMEM((2, 2), jnp.int32),
            pltpu.VMEM((2, 2, NF, 2, 80, 128), F32),
            pltpu.VMEM((2, 2, NF, 2, 80, 128), F32),
            pltpu.VMEM((4, 4, 2, NF, 64, 128), F32),
            pltpu.VMEM(vectors.shape, F32),
            pltpu.VMEM((2, 2, NF, 64, 128), F32),
            pltpu.VMEM((2, 4, 24, 128), F32),
            pltpu.VMEM((NZ, NC, 4, 24, 128), F32),
            pltpu.VMEM((NR, 8, 128), jnp.int32),
            pltpu.SMEM((NR, 8, 128), jnp.int32),
            pltpu.VMEM((NR, 4, 24, 128), F32),
            pltpu.VMEM((NR, 4, 24, 128), F32),
            pltpu.VMEM((12, 16, 128), F32),
            pltpu.VMEM((12, 16, 128), F32),
            pltpu.VMEM((4, 4, NF, 8, 128), F32),
            pltpu.VMEM((4, NF, 8, 128), F32),
            pltpu.VMEM((8, NF, 64, 128), F32),
            pltpu.VMEM((128, 128), F32),
            pltpu.VMEM((1, 128), F32),
            pltpu.VMEM((1, 128), F32),
            pltpu.VMEM((16, 1, 128), F32),
            pltpu.VMEM((16, 1, 128), F32),
            pltpu.VMEM((48, 128), F32),
            pltpu.VMEM((36, 8, 128), F32),
            dma((2,)), dma((5,)), dma((4,)),
            dma((2, 3)), dma((2, 3)),
            dma((33,)), dma((33,)),
            dma((7,)), dma((7,)),
            dma((7,)), dma((7,)),
            dma((3,)), dma((3,)),
            dma((30,)), dma((30,)),
            dma((len(MOVES), 2)), dma((len(MOVES), 2)),
            dma((6,)), dma((6,)),
            dma((2, 2)), dma((2, 2)),
            dma((2, 4)),
        ],
        compiler_params=pltpu.CompilerParams(collective_id=0, has_side_effects=True, vmem_limit_bytes=60 * 1024 * 1024),
        cost_estimate=pl.CostEstimate(flops=60_000_000, bytes_accessed=4_000_000, transcendentals=0),
    )(vectors, metric, jnp.transpose(jacobians, (1, 0, 2)), block_rows, neighbours, flipped)


def solution(mesh):
    wide = P("vec", "blk", None, None, None, None)
    in_specs = (wide, P("blk", None, None, None), P(), P("blk"), P("blk", None), P("blk", None))
    return jax.shard_map(per_device, mesh=mesh, in_specs=in_specs, out_specs=(wide, P()), check_vma=False)
```

```python
import jax
import jax.numpy as jnp
from jax import lax
from jax.experimental import pallas as pl
from jax.experimental.pallas import tpu as pltpu
from jax.sharding import PartitionSpec as P

MESH = pl.DeviceIdType.MESH
F32 = jnp.float32
HI = lax.Precision.HIGHEST
NF = 5
NZ, NY, NC, NX = 8, 4, 2, 4
NR = NY * NC
VISC = 0.1
EPS = 1e-06
SCALE = 1024.0


EARLY = [(1, 0, 2), (0, 3, 1), (0, 1, 3), (2, 1, 3)]
FAR = [(0, 0, 2), (1, 1, 3)]
MOVES = EARLY + FAR


def pair(v, w):
    return v * (v + 1) // 2 + w


def kernel(vec_h, met_h, jac_h, rows_h, nbr_h, flip_h, out, fac,
           vec, met, jac, rows, nbr, flip, st, fi, gath, bas, res, pay, zb, rq, rqs, o2, rb, own, gst, cb, edge, near, gacc, ar, ar2, arx, ary, spl, mix,
           loc_sem, in_sem, vec_sem, xs, xr, zs, zr, qs, qr, ys, yr, cs_s, cs_r, as_s, as_r, ws, wr, cs2_s, cs2_r, os, orr, out_sem):
    blk = lax.axis_index("blk")
    x = lax.axis_index("vec")
    z = blk // NR
    rho = lax.rem(blk, NR)
    c = lax.rem(blk, NC)
    col = lax.rem(blk, NR)

    def zdev(dz, core):
        zz = lax.rem(z + dz + NZ, NZ)
        return zz * NR + (rho - c) + core

    small = [pltpu.make_async_copy(h, d, in_sem.at[n]) for n, (h, d) in enumerate(
        ((rows_h, rows), (jac_h, jac), (nbr_h, nbr), (flip_h, flip), (met_h, met)))]
    big = [pltpu.make_async_copy(vec_h.at[n // 2, n % 2], vec.at[n // 2, n % 2], vec_sem.at[n]) for n in range(4)]
    for cp in small[:1] + big + small[1:]:
        cp.start()

    bar = pltpu.get_barrier_semaphore()
    def xdev(d):
        return lax.rem(x + d + NX, NX)

    def zc(d):
        m = lax.rem(z * NC + c + d, NZ * NC)
        return (m // NC) * NR + (rho - c) + lax.rem(m, NC), x

    def yx(d):
        m = lax.rem((rho // NC) * NX + x + d, (NR // NC) * NX)
        return z * NR + (m // NX) * NC + c, lax.rem(m, NX)

    def yc(d):
        return z * NR + lax.rem(rho + d, NR), x

    partners = [(zdev(dz, core), x) for dz in (1, -1) for core in range(2)] + [yc(d) for d in range(1, NR)]
    partners += [(blk, xdev(d)) for d in range(1, NX)]
    for b_, x_ in partners:
        pl.semaphore_signal(bar, inc=1, device_id={"blk": b_, "vec": x_}, device_id_type=MESH)
    n_part = len(partners)

    def rcopy(src, dst, ssem, rsem, b_, x_):
        return pltpu.make_async_remote_copy(src_ref=src, dst_ref=dst, send_sem=ssem, recv_sem=rsem,
                                            device_id={"blk": b_, "vec": x_}, device_id_type=MESH)

    iota64 = lax.broadcasted_iota(jnp.int32, (64, 128), 0)
    iota8 = lax.broadcasted_iota(jnp.int32, (8, 128), 0)
    lane8 = lax.broadcasted_iota(jnp.int32, (8, 128), 1)
    zero8 = jnp.zeros((8, 128), F32)

    for cp in small + big:
        cp.wait()

    sig = jnp.where((iota8 >> 1) & 1 == 0, -1.0, 1.0)
    sk = jnp.where(iota8 < 4, 1.0, -1.0)
    odd = iota8 & 1

    def jmul(d, g_, f):
        acc = jac[f, d, 0] * g_[0]
        for g in range(1, NF):
            acc = acc + jac[f, d, g] * g_[g]
        return acc

    def faces(i, _):
        b, side, v = i // 4, lax.rem(i // 2, 2), lax.rem(i, 2)
        last = jnp.maximum(rows[b] - 1, 1)
        r = jnp.where(side == 0, 0, last)
        adj = jnp.where(side == 0, 1, last - 1)
        slot = b * 2 + side
        lane_row = b * 8 + side * 2 + v
        for f in range(NF):
            for k in range(2):
                a = vec[v, b, f, k, pl.ds(r, 1), :]
                pay[v, slot, f * 2 + k:f * 2 + k + 1, :] = a
                own[f, pl.ds(lane_row + 4 * k, 1), :] = a
                gst[f, pl.ds(lane_row + 4 * k, 1), :] = vec[v, b, f, k, pl.ds(adj, 1), :]
        for k in range(2):
            m = met[b, k, pl.ds(r, 1), :]
            pay[v, slot, 20 + k:21 + k, :] = m
            pay[v, slot, 22 + k:23 + k, :] = m
            own[10, pl.ds(lane_row + 4 * k, 1), :] = m
            own[11, pl.ds(lane_row + 4 * k, 1), :] = met[b, k, pl.ds(adj, 1), :]
        return 0

    lax.fori_loop(0, 8, faces, 0)

    def face_step(b, _):
        base = pl.ds(pl.multiple_of(b * 8, 8), 8)
        q = [own[f, base, :] for f in range(NF)]
        inside = [gst[f, base, :] for f in range(NF)]
        m0 = own[10, base, :]
        e = [pltpu.roll(a, 127, 1) for a in q]
        w = [pltpu.roll(a, 1, 1) for a in q]
        ok = [pltpu.roll(a, 4, 0) for a in q]
        ew = [a - b_ for a, b_ in zip(e, w)]
        for f in range(NF):
            flux = jmul(0, ew, f) + sk * jmul(2, ok, f) - sig * jmul(1, inside, f)
            own[NF + f, base, :] = (1.0 - 6.0 * VISC) * q[f] + VISC * (e[f] + w[f] + ok[f] + inside[f]) - m0 * flux
        return 0

    lax.fori_loop(0, 2, face_step, 0)

    def pack(i, _):
        b, side, v = i // 4, lax.rem(i // 2, 2), lax.rem(i, 2)
        lane_row = b * 8 + side * 2 + v
        for f in range(NF):
            for k in range(2):
                pay[v, b * 2 + side, 10 + f * 2 + k:11 + f * 2 + k, :] = own[NF + f, pl.ds(lane_row + 4 * k, 1), :]
        return 0

    lax.fori_loop(0, 8, pack, 0)
    req = jnp.where(lane8 == 0, nbr[0, 0], jnp.where(lane8 == 1, nbr[0, 1], jnp.where(lane8 == 2, nbr[1, 0], nbr[1, 1])))
    rq[rho] = req

    pl.semaphore_wait(bar, n_part)

    mine = pltpu.make_async_copy(pay.at[c], zb.at[z, c], loc_sem.at[0])
    mine.start()
    z_copies = []
    for j in range(2):
        core = lax.rem(c + j, NC)
        for h in range(2):
            for side, dz in ((0, 1), (1, -1)):
                n = j * 4 + h * 2 + side
                half = pl.ds(2 * h, 2)
                cp = rcopy(pay.at[core, half], zb.at[z, c, half], zs.at[n], zr.at[n], zdev(dz, core), x)
                cp.start()
                z_copies.append(cp)
    other = rcopy(pay.at[1 - c], zb.at[z, c], zs.at[8], zr.at[8], zdev(0, 1 - c), x)
    other.start()
    q_copies = []
    for d in range(1, NR):
        cp = rcopy(rq.at[rho], rq.at[rho], qs.at[d - 1], qr.at[d - 1], z * NR + lax.rem(rho + d, NR), x)
        cp.start()
        q_copies.append(cp)

    def fill(i, _):
        vb = i // 10
        v, b = vb // 2, lax.rem(vb, 2)
        fk = lax.rem(i, 10)
        f, k = fk // 2, lax.rem(fk, 2)
        q = vec[v, b, f, k]
        st[v, b, f, k, 8:72, :] = jnp.where(iota64 < rows[b], q, 0.0)
        st[v, b, f, k, 0:8, :] = zero8
        st[v, b, f, k, 72:80, :] = zero8
        fi[v, b, f, k, 0:8, :] = zero8
        fi[v, b, f, k, 72:80, :] = zero8
        return 0

    lax.fori_loop(0, 20, fill, 0)

    def advance_tile(src, v, b, t, scale, store):
        r0 = pl.multiple_of(t * 8, 8)
        alive = (iota8 + r0) < rows[b]
        qs_, d0, d1, base = [], [], [], []
        for k in range(2):
            qk = [src[v, b, f, k, pl.ds(r0 + 8, 8), :] for f in range(NF)]
            qs_.append(qk)
        for k in range(2):
            a0, a1, ab = [], [], []
            for f in range(NF):
                q = qs_[k][f]
                e = pltpu.roll(q, 127, 1)
                w = pltpu.roll(q, 1, 1)
                n = src[v, b, f, k, pl.ds(r0 + 9, 8), :]
                s = src[v, b, f, k, pl.ds(r0 + 7, 8), :]
                a0.append(e - w)
                a1.append(n - s)
                ab.append((scale * (1.0 - 6.0 * VISC)) * q + (scale * VISC) * ((e + w) + (n + s) + qs_[1 - k][f]))
            d0.append(a0)
            d1.append(a1)
            base.append(ab)
        mk = [met[b, k, pl.ds(r0, 8), :] * scale for k in range(2)]
        for f in range(NF):
            c0 = [jac[f, 0, g] for g in range(NF)]
            c1 = [jac[f, 1, g] for g in range(NF)]
            c2 = [jac[f, 2, g] for g in range(NF)]
            for k in range(2):
                acc = c0[0] * d0[k][0] + c1[0] * d1[k][0]
                oth = c2[0] * qs_[1 - k][0]
                for g in range(1, NF):
                    acc = acc + c0[g] * d0[k][g] + c1[g] * d1[k][g]
                    oth = oth + c2[g] * qs_[1 - k][g]
                flux = acc + oth if k == 0 else acc - oth
                store(f, k, jnp.where(alive, base[k][f] - mk[k] * flux, 0.0))

    def first_pass(i, sums):
        vb, t = i // 8, lax.rem(i, 8)
        v, b = vb // 2, lax.rem(vb, 2)
        r0 = t * 8
        row = iota8 + r0
        inner = jnp.logical_and(row > 0, row != rows[b] - 1)
        box = [jnp.zeros((8, 128), F32)]

        def store(f, k, val):
            fi[v, b, f, k, pl.ds(pl.multiple_of(r0 + 8, 8), 8), :] = val
            box[0] = box[0] + val * val

        advance_tile(st, v, b, t, 1.0, store)
        sq = jnp.where(inner, box[0], 0.0)
        s0, s1 = sums
        return s0 + jnp.where(v == 0, sq, 0.0), s1 + jnp.where(v == 1, sq, 0.0)

    ssq = lax.fori_loop(0, 16, first_pass, (zero8, zero8))

    def second_pass(v):
        def body(i, _):
            b, t = i // 8, lax.rem(i, 8)

            def store(f, k, val):
                gath[x, b * 2 + k, v, f, pl.ds(pl.multiple_of(t * 8, 8), 8), :] = val

            advance_tile(fi, v, b, t, SCALE, store)
            return 0

        lax.fori_loop(0, 16, body, 0)

    sends = []

    def send_second(v):
        for d in (2, 1, 3):
            here = gath.at[x, xdev(d), v]
            cp = rcopy(here, here, xs.at[v, d - 1], xr.at[v, d - 1], blk, xdev(d))
            cp.start()
            sends.append(cp)

    def move(n, v):
        src, q, to = MOVES[n]
        part = gath.at[src, q, v]
        return rcopy(part, part, ws.at[n, v], wr.at[n, v], blk, jnp.int32(to))

    def fix_move(n):
        src, q, to = MOVES[n]
        part = cb.at[src, q]
        return rcopy(part, part, cs2_s.at[n], cs2_r.at[n], blk, jnp.int32(to))

    def moves(which, vs):
        for n in range(len(MOVES)):
            if MOVES[n] in which:
                @pl.when(x == MOVES[n][0])
                def _():
                    for v in vs:
                        move(n, v).start()

    def fix_moves():
        for n in range(len(MOVES)):
            @pl.when(x == MOVES[n][0])
            def _():
                fix_move(n).start()

    drain = z_copies + [other]

    def ring_step(s, before):
        cps = []
        for j in range(2):
            core = lax.rem(c + j, NC)
            for h in range(2):
                for side, dz in ((0, 1), (1, -1)):
                    m = j * 4 + h * 2 + side
                    before[m].wait_recv()
                    if s == 3 and side != j:
                        continue
                    n = 9 + (s - 1) * 8 + m
                    part = zb.at[lax.rem(z - dz * s + NZ, NZ), core, pl.ds(2 * h, 2)]
                    cp = rcopy(part, part, zs.at[n], zr.at[n], zdev(dz, c), x)
                    cp.start()
                    cps.append(cp)
        drain.extend(cps)
        return cps

    second_pass(0)
    send_second(0)
    ring1 = ring_step(1, z_copies)
    lax.fori_loop(20, 40, fill, 0)
    ssq = lax.fori_loop(16, 32, first_pass, ssq)

    second_pass(1)
    send_second(1)
    moves(FAR, (0,))
    ring2 = ring_step(2, ring1)
    for cp in q_copies:
        cp.wait_recv()
    tosmem = pltpu.make_async_copy(rq, rqs, loc_sem.at[1])
    tosmem.start()
    ring3 = ring_step(3, ring2)
    mine.wait()
    other.wait_recv()
    tosmem.wait()
    for cp in ring3:
        cp.wait_recv()

    def pick(i, _):
        to, r = i // 4, lax.rem(i, 4)
        bid = rqs[to, 0, r]
        side = lax.rem(r, 2)
        o2[to, r] = zb[bid >> 4, (bid >> 1) & 1, (bid & 1) * 2 + (1 - side)]
        return 0

    y_copies = []
    for d in (4, 5, 3, 2, 6, 1, 7):
        to = lax.rem(rho + d, NR)
        lax.fori_loop(4 * to, 4 * to + 4, pick, 0)
        cp = rcopy(o2.at[to], rb.at[rho], ys.at[d - 1], yr.at[d - 1], z * NR + to, x)
        cp.start()
        y_copies.append(cp)
    lax.fori_loop(4 * rho, 4 * rho + 4, pick, 0)
    rb[rho] = o2[rho]
    for cp in y_copies:
        cp.wait_recv()
    drain += y_copies + q_copies

    rev = 127 - lane8

    def unpack(i, _):
        b, side, v = i // 4, lax.rem(i // 2, 2), lax.rem(i, 2)
        r = b * 2 + side
        bid = nbr[b, side]
        f_ = flip[b, side]
        lane_row = b * 8 + side * 2 + v
        src = ((bid >> 2) & 3) * 2 + v
        for h in range(3):
            q = rb[src, r, 8 * h:8 * h + 8, :]
            turned = jnp.take_along_axis(q, rev, axis=1)
            rowh = iota8 + 8 * h
            neg = jnp.logical_or(jnp.logical_or(rowh == 2, rowh == 3), jnp.logical_or(rowh == 12, rowh == 13))
            turned = jnp.where(neg, -turned, turned)
            q = jnp.where(f_ > 0, turned, q)
            for j in range(8):
                w = 8 * h + j
                if w >= 22:
                    continue
                item, k = (w // 2, w % 2)
                gst[item, pl.ds(lane_row + 4 * k, 1), :] = q[j:j + 1, :]
        sign = jnp.where(f_ > 0, -1.0, 1.0) + jnp.zeros((1, 128), F32)
        for k in range(2):
            gst[11, pl.ds(lane_row + 4 * k, 1), :] = sign
        return 0

    lax.fori_loop(0, 8, unpack, 0)

    def fix(b, sums):
        base = pl.ds(pl.multiple_of(b * 8, 8), 8)
        g0 = [gst[f, base, :] for f in range(NF)]
        gf = [gst[NF + f, base, :] for f in range(NF)]
        gm = gst[10, base, :]
        turn = gst[11, base, :]
        o = [own[f, base, :] for f in range(NF)]
        of = [own[NF + f, base, :] for f in range(NF)]
        m0 = own[10, base, :]
        m1 = own[11, base, :]
        od = [o[f] * turn if f == 1 else o[f] for f in range(NF)]
        g1, c1 = [], []
        total = zero8
        for f in range(NF):
            tf = jmul(1, od, f)
            if f == 1:
                tf = tf * turn
            g1.append(gf[f] + VISC * o[f] + sig * gm * tf)
            cf = VISC * g0[f] - sig * m0 * jmul(1, g0, f)
            c1.append(cf)
            ff = of[f] + cf
            total = total + ff * ff
        e = [pltpu.roll(cf, 127, 1) for cf in c1]
        w = [pltpu.roll(cf, 1, 1) for cf in c1]
        ok = [pltpu.roll(cf, 4, 0) for cf in c1]
        ew = [a - b_ for a, b_ in zip(e, w)]
        for f in range(NF):
            flux = jmul(0, ew, f) + sk * jmul(2, ok, f) + sig * jmul(1, g1, f)
            face = (1.0 - 6.0 * VISC) * c1[f] + VISC * (e[f] + w[f] + ok[f] + g1[f]) - m0 * flux
            near = VISC * c1[f] - sig * m1 * jmul(1, c1, f)
            face = face * SCALE
            near = near * SCALE
            cb[x, b * 2, f, 0:4, :] = face[0:4]
            cb[x, b * 2, f, 4:8, :] = near[0:4]
            cb[x, b * 2 + 1, f, 0:4, :] = face[4:8]
            cb[x, b * 2 + 1, f, 4:8, :] = near[4:8]
        s0, s1 = sums
        return s0 + jnp.where(odd == 0, total, 0.0), s1 + jnp.where(odd == 1, total, 0.0)

    ssq = lax.fori_loop(0, 2, fix, ssq)
    c_copies = []
    for d in (2, 1, 3):
        here = cb.at[x, xdev(d)]
        cp = rcopy(here, here, cs_s.at[d - 1], cs_r.at[d - 1], blk, xdev(d))
        cp.start()
        c_copies.append(cp)
    fix_moves()
    moves(EARLY, (0, 1))
    for cp in sends:
        cp.wait_recv()

    bq = x // 2
    my_last = jnp.where(bq == 0, rows[0], rows[1]) - 1
    safe_last = jnp.maximum(my_last, 1)

    def products(acc, left, right):
        res = list(acc)
        for v in range(8):
            for w in range(v + 1):
                res[pair(v, w)] = res[pair(v, w)] + left[v] * right[w]
        return tuple(res)

    def gram_tile(i, acc):
        f, t = i // 8, lax.rem(i, 8)
        row = iota8 + t * 8
        inner = jnp.logical_and(row > 1, jnp.logical_or(row < my_last - 1, row > my_last))
        vals = [gath[v // 2, x, v % 2, f, pl.ds(pl.multiple_of(t * 8, 8), 8), :] for v in range(8)]
        for v in range(8):
            near[v, f, pl.ds(pl.multiple_of(t * 8, 8), 8), :] = vals[v]
        return products(acc, [jnp.where(inner, q, 0.0) for q in vals], vals)

    grams = lax.fori_loop(0, 40, gram_tile, tuple(zero8 for _ in range(36)))

    def edges(i, _):
        f, v = i // 8, lax.rem(i, 8)
        for j, r in enumerate((0, safe_last, 1, safe_last - 1)):
            edge[v // 2, f, pl.ds(2 * j + lax.rem(v, 2), 1), :] = near[v, f, pl.ds(r, 1), :]
        return 0

    lax.fori_loop(0, 40, edges, 0)
    for cp in c_copies:
        cp.wait_recv()
    drain += sends + c_copies
    odd_row = (iota8 & 1) == 1

    def gram_edge(f, acc):
        vals = []
        for src in range(NX):
            both = edge[src, f] + cb[src, x, f]
            vals.append(jnp.where(odd_row, 0.0, both))
            vals.append(jnp.where(odd_row, 0.0, pltpu.roll(both, 7, 0)))
        return products(acc, vals, vals)

    grams = lax.fori_loop(0, NF, gram_edge, grams)
    gacc[...] = jnp.zeros((128, 128), F32)
    for n in range(36):
        gacc[n:n + 1, :] = jnp.sum(grams[n], axis=0, keepdims=True)
    for v in range(2):
        gacc[pl.ds(36 + 2 * x + v, 1), :] = jnp.sum(ssq[v], axis=0, keepdims=True)
    ones8 = jnp.ones((8, 128), F32)
    ar[...] = lax.dot_general(ones8, gacc[...], (((1,), (1,)), ((), ())), precision=HI, preferred_element_type=F32)[0:1, :]

    def exchange(src, buf, me, first, dev, then):
        buf[me] = src[...]
        cps = []
        for d in (8, 10, 9, 7, 6, 11, 5, 2, 14, 12, 4, 13, 3, 1, 15):
            b_, x_ = dev(d)
            cp = rcopy(src, buf.at[me], as_s.at[first + d - 1], as_r.at[first + d - 1], b_, x_)
            cp.start()
            cps.append(cp)
        then()
        for cp in cps:
            cp.wait_recv()
        drain.extend(cps)
        tot = [buf[j] for j in range(16)]
        while len(tot) > 1:
            tot = [a + b_ for a, b_ in zip(tot[::2], tot[1::2])]
        return tot[0]

    ar2[...] = exchange(ar, arx, z * NC + c, 0, zc, lambda: None)
    ar3 = exchange(ar2, ary, (rho // NC) * NX + x, 15, yx, lambda: moves(FAR, (1,)))

    r48 = lax.broadcasted_iota(jnp.int32, (48, 128), 0)
    l48 = lax.broadcasted_iota(jnp.int32, (48, 128), 1)
    spread = jnp.where(r48 == l48, jnp.broadcast_to(ar3[0:1, :], (48, 128)), 0.0)
    spl[...] = jnp.dot(spread, jnp.ones((128, 128), F32), precision=HI, preferred_element_type=F32)

    def entry(n):
        return spl[n:n + 1, :]

    s = [1.0 / (SCALE * jnp.sqrt(entry(36 + v) + EPS)) for v in range(8)]
    low = {}
    inv = []
    for j in range(8):
        a = entry(pair(j, j)) * s[j] * s[j]
        for k in range(j):
            a = a - low[j, k] * low[j, k]
        inv.append(lax.rsqrt(a))
        low[j, j] = a * inv[j]
        for i in range(j + 1, 8):
            a = entry(pair(i, j)) * s[i] * s[j]
            for k in range(j):
                a = a - low[i, k] * low[j, k]
            low[i, j] = a * inv[j]
    xx = {}
    for j in range(8):
        xx[j, j] = inv[j]
        for i in range(j + 1, 8):
            a = low[i, j] * xx[j, j]
            for k in range(j + 1, i):
                a = a + low[i, k] * xx[k, j]
            xx[i, j] = -a * inv[i]
    upper = zero8
    for i in range(8):
        for j in range(i + 1):
            mix[pair(i, j)] = jnp.broadcast_to(xx[i, j] * s[j], (8, 128))
            upper = jnp.where(jnp.logical_and(iota8 == j, lane8 == i), jnp.broadcast_to(low[i, j], (8, 128)), upper)
    fac[...] = upper[:, 0:8]

    def combine(q, outs, put):
        top = max(outs) // 2 + 1

        def body(f, _):
            last = rows[q // 2] - 1
            fixes = []
            for o in outs:
                tot = zero8
                for src in range(o // 2 + 1):
                    lo = mix[pair(o, 2 * src)]
                    hi = mix[pair(o, 2 * src + 1)] if 2 * src + 1 <= o else 0.0
                    tot = tot + jnp.where(odd_row, hi, lo) * cb[src, q, f]
                tot = tot + pltpu.roll(tot, 7, 0)
                fixes.append([jnp.broadcast_to(tot[r:r + 1], (8, 128)) for r in (0, 2, 4, 6)])
            for t in range(8):
                vals = [gath[w // 2, q, w % 2, f, 8 * t:8 * t + 8, :] for w in range(2 * top)]
                row = iota8 + 8 * t
                for n, o in enumerate(outs):
                    a = mix[pair(o, 0)] * vals[0]
                    for w in range(1, o + 1):
                        a = a + mix[pair(o, w)] * vals[w]
                    if t == 0:
                        a = a + jnp.where(row == 0, fixes[n][0], 0.0) + jnp.where(row == 1, fixes[n][2], 0.0)
                    if t >= 3:
                        a = a + jnp.where(row == last, fixes[n][1], 0.0) + jnp.where(row == last - 1, fixes[n][3], 0.0)
                    put(n, f, t, a)
            return 0

        lax.fori_loop(0, NF, body, 0)

    def home(i, v, q, to):
        return rcopy(res.at[i, v], out.at[v, q // 2, :, q % 2], os.at[i, v], orr.at[i, v], blk, jnp.int32(to))

    def own_copy(v, q):
        there = out.at[v, q // 2, :, q % 2]
        return pltpu.make_async_copy(bas.at[v, q // 2, :, q % 2], there, out_sem.at[v, q])

    def finish(g):
        beside = [(i, (g + d) % NX) for i, d in ((0, 1), (1, -1)) if (g + d) % NX > 0]
        for i, to in beside:
            def put(n, f, t, a, i=i):
                res[i, n, f, 8 * t:8 * t + 8, :] = a

            combine(g, [2 * to, 2 * to + 1], put)
            for v in range(2):
                home(i, v, g, to).start()
        mine_q = [g, (g + 2) % NX] if g > 0 else [0, 1, 2, 3]
        for q in mine_q:
            if q != g:
                for n in range(len(MOVES)):
                    if MOVES[n][1:] == (q, g):
                        move(n, 0).wait_recv()
                        move(n, 1).wait_recv()
                        fix_move(n).wait_recv()

            def put_own(n, f, t, a, q=q):
                bas[n, q // 2, f, q % 2, 8 * t:8 * t + 8, :] = a

            combine(q, [2 * g, 2 * g + 1], put_own)
            for v in range(2):
                own_copy(v, q).start()
        for n in range(len(MOVES)):
            if MOVES[n][0] == g:
                move(n, 0).wait_send()
                move(n, 1).wait_send()
                fix_move(n).wait_send()
        for q in mine_q:
            for v in range(2):
                own_copy(v, q).wait()
        for i, to in beside:
            for v in range(2):
                home(i, v, g, to).wait_send()
        if g > 0:
            for i, frm in ((0, (g - 1) % NX), (1, (g + 1) % NX)):
                for v in range(2):
                    home(i, v, frm, g).wait_recv()

    for cp in drain:
        cp.wait_send()
    for g in range(NX):
        @pl.when(x == g)
        def _():
            finish(g)


def per_device(vectors, metric, jacobians, block_rows, neighbours, flipped):
    vm = pl.BlockSpec(memory_space=pltpu.VMEM)
    hbm = pl.BlockSpec(memory_space=pltpu.HBM)
    dma = pltpu.SemaphoreType.DMA
    return pl.pallas_call(
        kernel,
        out_shape=(pltpu.VMEM(vectors.shape, F32), jax.ShapeDtypeStruct((8, 8), F32)),
        in_specs=[hbm] * 6,
        out_specs=(pl.BlockSpec(memory_space=pl.ANY), vm),
        scratch_shapes=[
            pltpu.VMEM(vectors.shape, F32),
            pltpu.VMEM(metric.shape, F32),
            pltpu.SMEM((NF, 3, NF), F32),
            pltpu.SMEM((2,), jnp.int32),
            pltpu.SMEM((2, 2), jnp.int32),
            pltpu.SMEM((2, 2), jnp.int32),
            pltpu.VMEM((2, 2, NF, 2, 80, 128), F32),
            pltpu.VMEM((2, 2, NF, 2, 80, 128), F32),
            pltpu.VMEM((4, 4, 2, NF, 64, 128), F32),
            pltpu.VMEM(vectors.shape, F32),
            pltpu.VMEM((2, 2, NF, 64, 128), F32),
            pltpu.VMEM((2, 4, 24, 128), F32),
            pltpu.VMEM((NZ, NC, 4, 24, 128), F32),
            pltpu.VMEM((NR, 8, 128), jnp.int32),
            pltpu.SMEM((NR, 8, 128), jnp.int32),
            pltpu.VMEM((NR, 4, 24, 128), F32),
            pltpu.VMEM((NR, 4, 24, 128), F32),
            pltpu.VMEM((12, 16, 128), F32),
            pltpu.VMEM((12, 16, 128), F32),
            pltpu.VMEM((4, 4, NF, 8, 128), F32),
            pltpu.VMEM((4, NF, 8, 128), F32),
            pltpu.VMEM((8, NF, 64, 128), F32),
            pltpu.VMEM((128, 128), F32),
            pltpu.VMEM((1, 128), F32),
            pltpu.VMEM((1, 128), F32),
            pltpu.VMEM((16, 1, 128), F32),
            pltpu.VMEM((16, 1, 128), F32),
            pltpu.VMEM((48, 128), F32),
            pltpu.VMEM((36, 8, 128), F32),
            dma((2,)), dma((5,)), dma((4,)),
            dma((2, 3)), dma((2, 3)),
            dma((33,)), dma((33,)),
            dma((7,)), dma((7,)),
            dma((7,)), dma((7,)),
            dma((3,)), dma((3,)),
            dma((30,)), dma((30,)),
            dma((len(MOVES), 2)), dma((len(MOVES), 2)),
            dma((6,)), dma((6,)),
            dma((2, 2)), dma((2, 2)),
            dma((2, 4)),
        ],
        compiler_params=pltpu.CompilerParams(collective_id=0, has_side_effects=True, vmem_limit_bytes=60 * 1024 * 1024),
        cost_estimate=pl.CostEstimate(flops=60_000_000, bytes_accessed=4_000_000, transcendentals=0),
    )(vectors, metric, jnp.transpose(jacobians, (1, 0, 2)), block_rows, neighbours, flipped)


def solution(mesh):
    wide = P("vec", "blk", None, None, None, None)
    in_specs = (wide, P("blk", None, None, None), P(), P("blk"), P("blk", None), P("blk", None))
    return jax.shard_map(per_device, mesh=mesh, in_specs=in_specs, out_specs=(wide, P()), check_vma=False)
```
